256 devices in a mesh: section: 2 (over x_lo), seq: 64 (over z, y, x_hi), head: 2 (over core).
Axes of the slice: x: 4 (x_hi: 2, x_lo: 2; x = x_hi * 2 + x_lo), y: 4, z: 8, core: 2. Of those that a mesh axis runs over, the one named last changes fastest.
Arguments:
- query_nope: bfloat16 [2, 8192, 64, 128], P('section', 'seq', 'head'), may hold values from -6 to 6
- query_rope: bfloat16 [2, 8192, 4096], P('section', 'seq', 'head'), may hold values from -8 to 8
- latent: bfloat16 [2, 8192, 576], P('section', ('seq', 'head')), may hold values from -8 to 8
- up_key: bfloat16 [64, 512, 128], P('head'), may hold values from -0.25 to 0.25
- value_up_weight: bfloat16 [64, 512, 128], P('head'), may hold values from -1.5 to 1.5
- lengths: int32 [32], replicated, may hold values from 1 to 4224, 8192 in all
- owner_request_table: int32 [256], replicated, may hold values from 0 to 255, each once
Outputs:
- attended: bfloat16 [2, 8192, 64, 128], P('section', 'seq', 'head')
The draws below stay inside these ranges and needn't reach their ends.
Inputs may be any that keep to these rules, and one draw needn't show every extreme that they name: The 32 lengths sum to 8192; one is exactly 4224. `owner_request_table`: every request 0 to 255 appears once.
All inputs are finite; a program needn't handle non-finite values.
Results may differ from the reference program's by a relative error of at most 0.0075.
Values may be sent and summed in bfloat16 or wider, within the bound.
A program may use at most 128 MiB of HBM per device.

```python
import math
import jax
import jax.numpy as jnp
import numpy as np
from jax import lax

HEADS = 64
KV_RANK = 512
ROPE_DIM = 64
NOPE_DIM = 128
V_DIM = 128
SAMPLES = 8
STEPS = 4
BLOCK = 64
TOK_DEV = 128
TOKENS = 8192
PROMPTS = 32
REQUESTS = 256
GROUPS = 8
LEN_MOST = 4224
N_SEQ = 64


def draw_latent(key, part):
    key = jax.random.fold_in(key, 3)
    starting_sample = jnp.clip(jax.random.normal(key, (2, TOKENS, KV_RANK + ROPE_DIM), jnp.float32), -6.0, 6.0)
    return starting_sample.astype(jnp.bfloat16)


def draw_query_rope(key, part):
    key = jax.random.fold_in(key, 5)
    starting_sample = jnp.clip(jax.random.normal(key, (2, TOKENS, HEADS, ROPE_DIM), jnp.float32), -6.0, 6.0)
    return starting_sample.reshape(2, TOKENS, HEADS * ROPE_DIM).astype(jnp.bfloat16)


def block_levels(stream_key, extent, pieces, smallest, top_value):
    def one(axis_at, shards_of):
        heights = jax.random.uniform(jax.random.fold_in(jax.random.fold_in(stream_key, 6), axis_at), (shards_of,), jnp.float32, smallest / len(pieces), top_value / len(pieces))
        return jnp.repeat(jnp.exp(heights), extent[axis_at] // shards_of).reshape((-1,) + (1,) * (len(extent) - axis_at - 1))

    level = one(*pieces[0])
    for cut in pieces[1:]:
        level = level * one(*cut)
    return level


def length_profile(number_of, total, most, slope):
    portions = [(1 << 20) // math.isqrt(rank ** slope) + 1 for rank in range(2, number_of + 1)]
    spare, holding = total - most - (number_of - 1), [1] * (number_of - 1)
    while spare > 0:
        free = [i for i in range(number_of - 1) if holding[i] < most]
        mass, left = sum([portions[i] for i in free]), spare
        for i in free:
            extra = min(most - holding[i], max(1, left * portions[i] // mass), spare)
            holding[i] = holding[i] + extra
            spare = spare - extra
    return np.array([most] + holding)


def ragged(stream_key, amount, total, most, slope):
    if amount == 2:
        one = jax.random.randint(stream_key, (), max(1, total - most), min(most, total - 1) + 1)
        return jnp.stack([one, total - one])
    sizes = jnp.asarray(length_profile(amount, total, most, slope), jnp.int32)
    pairs = (amount - 1) // 2
    giver, sink = sizes[1:1 + 2 * pairs:2], sizes[2:2 + 2 * pairs:2]
    room = jnp.minimum(giver - 1, most - sink)
    shifted = jax.random.randint(jax.random.fold_in(stream_key, 1), (pairs,), 0, 1 << 20) % (room + 1)
    sizes = sizes.at[1:1 + 2 * pairs:2].set(giver - shifted).at[2:2 + 2 * pairs:2].set(sink + shifted)
    return sizes[jax.random.permutation(jax.random.fold_in(stream_key, 2), amount)]


def centred(own_key, extent, width, bound, split=(), kind=jnp.bfloat16):
    result = jax.random.normal(own_key, extent, jnp.float32) * width
    if len(split) > 0:
        result = block_levels(own_key, extent, split, -0.22, 0.18) * result
    return jnp.clip(result, min=-bound, max=bound).astype(kind)


def setup_inputs(seed: int = 0) -> dict:
    seeds = jax.random.split(jax.random.key(seed), 8)
    return {
        "query_nope": centred(seeds[0], (2, TOKENS, HEADS, NOPE_DIM), 1.0, 6.0, ((0, 2), (1, 64), (2, 2))),
        "query_rope": draw_query_rope(jax.random.fold_in(seeds[7], 71), 0),
        "latent": draw_latent(jax.random.fold_in(seeds[7], 71), 0),
        "up_key": centred(seeds[3], (HEADS, KV_RANK, NOPE_DIM), KV_RANK ** -0.5, 0.25, ((0, 2),)),
        "value_up_weight": centred(seeds[4], (HEADS, KV_RANK, V_DIM), 0.25, 1.5, ((0, 2),)),
        "lengths": ragged(seeds[5], PROMPTS, TOKENS, LEN_MOST, 2).astype(jnp.int32),
        "owner_request_table": jax.random.permutation(seeds[6], REQUESTS).astype(jnp.int32),
    }


scale_top = 448.0
tiny_eps = 1e-06
masked_low = -1e+30

def absorb(part_nope, part_rope, up_key):
    row_count = part_rope.shape[0]
    lifted = jnp.einsum('thn,hkn->thk', part_nope.astype(jnp.float32), up_key.astype(jnp.float32))
    rope_part = part_rope.reshape(row_count, HEADS, ROPE_DIM).astype(jnp.float32)
    joined = jnp.concatenate([lifted, rope_part], axis=2).astype(jnp.bfloat16)
    return joined.reshape(row_count * HEADS, KV_RANK + ROPE_DIM)

def quantize(row_data):
    blocks = row_data.astype(jnp.float32).reshape(-1, BLOCK, row_data.shape[1])
    largest = lax.optimization_barrier(jnp.max(jnp.abs(blocks), axis=(1, 2)))
    block_scale = ((largest + tiny_eps) / scale_top).astype(jnp.bfloat16)
    stored = (blocks / block_scale.astype(jnp.float32)[:, None, None]).astype(jnp.bfloat16)
    return (stored.reshape(row_data.shape), jnp.repeat(block_scale, BLOCK))

def token_start(positions, starts):
    return lax.optimization_barrier(jnp.max(jnp.where(starts[None, :] <= positions[:, None], starts[None, :], 0), axis=1)).astype(jnp.int32)

def attend(queries, key_rows, scales, visible):
    soft_scale = 1.0 / math.sqrt(NOPE_DIM + ROPE_DIM)
    factor = scales.astype(jnp.float32)
    scores = jnp.dot(queries, key_rows.T, preferred_element_type=jnp.float32)
    scores = scores * (factor * soft_scale)[None, :]
    masked = jnp.where(visible, scores, masked_low)
    row_top = lax.optimization_barrier(jnp.max(masked, axis=1))
    expo_terms = jnp.where(visible, jnp.exp(masked - row_top[:, None]), 0.0)
    weights = (expo_terms * factor[None, :]).astype(jnp.bfloat16)
    summed = jnp.dot(weights, key_rows[:, :KV_RANK], preferred_element_type=jnp.float32)
    return (summed / lax.optimization_barrier(jnp.sum(expo_terms, axis=1))[:, None]).astype(jnp.bfloat16)

def project(latent_result, value_up_weight, row_count):
    reshaped_rows = latent_result.reshape(row_count, HEADS, KV_RANK).astype(jnp.float32)
    return jnp.einsum('ryb,ybw->ryw', reshaped_rows, value_up_weight.astype(jnp.float32)).astype(jnp.bfloat16)

def reference(query_nope, query_rope, latent, up_key, value_up_weight, lengths, owner_request_table):
    prompt_ends = jnp.cumsum(lengths).astype(jnp.int32)
    starts = (prompt_ends - lengths).astype(jnp.int32)
    stored, key_scale = quantize(latent[0])
    band_rows = STEPS * SAMPLES
    short_window = 4 * TOK_DEV

    def prefill_block(block_index):
        first_row = block_index * TOK_DEV
        positions = first_row + jnp.arange(TOK_DEV, dtype=jnp.int32)
        queries = absorb(lax.dynamic_slice_in_dim(query_nope[0], first_row, TOK_DEV, 0), lax.dynamic_slice_in_dim(query_rope[0], first_row, TOK_DEV, 0), up_key)
        prompt_low = token_start(positions, starts)
        reach = first_row + TOK_DEV - prompt_low[0]

        def windowed(window):

            def run_window(unused):
                window_start = jnp.clip(prompt_low[0], 0, TOKENS - window).astype(jnp.int32)
                key_rows = lax.dynamic_slice_in_dim(stored, window_start, window, 0)
                scales = lax.dynamic_slice_in_dim(key_scale, window_start, window, 0)
                key_spots = window_start + jnp.arange(window, dtype=jnp.int32)
                visible = (key_spots[None, :] >= prompt_low[:, None]) & (key_spots[None, :] <= positions[:, None])
                return attend(queries, key_rows, scales, jnp.repeat(visible, HEADS, axis=0))
            return run_window
        latent_result = lax.cond(reach <= short_window, windowed(short_window), windowed(LEN_MOST + TOK_DEV), 0)
        return project(latent_result, value_up_weight, TOK_DEV)

    def decode_request(request_index):
        first_row = request_index * band_rows
        queries = absorb(lax.dynamic_slice_in_dim(query_nope[1], first_row, band_rows, 0), lax.dynamic_slice_in_dim(query_rope[1], first_row, band_rows, 0), up_key)
        prompt = owner_request_table[request_index] // GROUPS
        prompt_low = starts[prompt]
        prompt_high = prompt_ends[prompt]
        fresh_rows = lax.dynamic_slice_in_dim(latent[1], first_row, band_rows, 0)
        step_row = jnp.arange(band_rows, dtype=jnp.int32) // SAMPLES
        sample_row = jnp.arange(band_rows, dtype=jnp.int32) % SAMPLES
        new_visible = (step_row[None, :] <= step_row[:, None]) & (sample_row[None, :] == sample_row[:, None])

        def windowed(window):

            def run_window(unused):
                window_start = jnp.clip(prompt_low, 0, TOKENS - window).astype(jnp.int32)
                cache_keys = lax.dynamic_slice_in_dim(stored, window_start, window, 0)
                cache_scales = lax.dynamic_slice_in_dim(key_scale, window_start, window, 0)
                key_spots = window_start + jnp.arange(window, dtype=jnp.int32)
                old_visible = (key_spots >= prompt_low) & (key_spots < prompt_high)
                key_rows = jnp.concatenate([cache_keys, fresh_rows], axis=0)
                scales = jnp.concatenate([cache_scales, jnp.ones((band_rows,), jnp.bfloat16)], axis=0)
                visible = jnp.concatenate([jnp.broadcast_to(old_visible[None, :], (band_rows, window)), new_visible], axis=1)
                return attend(queries, key_rows, scales, jnp.repeat(visible, HEADS, axis=0))
            return run_window
        latent_result = lax.cond(prompt_high - prompt_low <= short_window, windowed(short_window), windowed(LEN_MOST), 0)
        return project(latent_result, value_up_weight, band_rows)
    prefill_out = lax.map(prefill_block, jnp.arange(N_SEQ, dtype=jnp.int32)).reshape(TOKENS, HEADS, V_DIM)
    decode_out = lax.map(decode_request, jnp.arange(REQUESTS, dtype=jnp.int32)).reshape(TOKENS, HEADS, V_DIM)
    return jnp.stack([prefill_out, decode_out])
```

```python
import functools
import math

import jax
import jax.numpy as jnp
from jax import lax
from jax.experimental import pallas as pl
from jax.experimental.pallas import tpu as pltpu
from jax.sharding import PartitionSpec as P

SAMPLES = 8
STEPS = 4
BLOCK = 64

scale_top = 448.0
tiny_eps = 1e-06
masked_low = -1e30

KEY_BLOCK = 512
EDGE_BLOCK = 256
ROW_TILE = 512
LANES = 128


def dequantized(rows):
    blocks = rows.astype(jnp.float32).reshape(-1, BLOCK, rows.shape[1])
    largest = jnp.max(jnp.abs(blocks), axis=(1, 2))
    block_scale = ((largest + tiny_eps) / scale_top).astype(jnp.bfloat16)
    factor = block_scale.astype(jnp.float32)[:, None, None]
    stored = (blocks / factor).astype(jnp.bfloat16)
    keys = (stored.astype(jnp.float32) * factor).astype(jnp.bfloat16)
    return keys.reshape(rows.shape)


def token_start(positions, starts):
    return jnp.max(jnp.where(starts[None, :] <= positions[:, None], starts[None, :], 0), axis=1)


def over_lanes(value, width):
    return jnp.concatenate([value] * (width // LANES), axis=1)


def flash_kernel(
    kv_rank,
    exponent_scale,
    plan,
    q_ref,
    keys,
    own_keys,
    low_ref,
    bias_ref,
    out_ref,
    acc,
    top,
    total,
):
    band = pl.program_id(0)
    heads, tokens, width = q_ref.shape
    rows = heads * tokens
    first, full_from, full_to, last = (plan[i, band] for i in range(4))
    q = q_ref[...].reshape(rows, width)
    own = own_keys[...]
    nt = (((1,), (1,)), ((), ()))

    scores = lax.dot_general(q, own, nt, preferred_element_type=jnp.float32)
    bias = jnp.broadcast_to(bias_ref[...][None], (heads, tokens, tokens)).reshape(rows, tokens)
    scores = scores + bias
    own_top = jnp.max(scores, axis=1, keepdims=True)
    expo = jnp.exp2((scores - own_top) * exponent_scale)
    lane = lax.broadcasted_iota(jnp.int32, (rows, LANES), 1)
    total[...] = jnp.where(lane == 0, jnp.sum(expo, axis=1, keepdims=True), 0.0)
    top[...] = jnp.broadcast_to(own_top, (rows, LANES))
    acc[...] = jnp.dot(
        expo.astype(jnp.bfloat16), own[:, :kv_rank], preferred_element_type=jnp.float32
    )

    def fold(at, count, masked):
        at = pl.multiple_of(at, 16)
        key_block = keys[pl.ds(at, count), :]
        for r in range(0, rows, ROW_TILE):
            part = pl.ds(r, ROW_TILE)
            s = lax.dot_general(
                q[r : r + ROW_TILE], key_block, nt, preferred_element_type=jnp.float32
            )
            if masked:
                low = jnp.broadcast_to(
                    low_ref[...][None], (ROW_TILE // tokens, tokens, 1)
                ).reshape(ROW_TILE, 1)
                spot = at + lax.broadcasted_iota(jnp.int32, (1, count), 1)
                s = jnp.where((spot >= low) & (spot < last), s, masked_low)
            before = top[part, :]
            now = jnp.maximum(before, jnp.max(s, axis=1, keepdims=True))
            shrink = jnp.exp2((before - now) * exponent_scale)
            expo = jnp.exp2((s - over_lanes(now, count)) * exponent_scale)
            top[part, :] = now
            summed = total[part, :] * shrink
            for c in range(0, count, LANES):
                summed = summed + expo[:, c : c + LANES]
            total[part, :] = summed
            acc[part, :] = acc[part, :] * over_lanes(shrink, kv_rank) + jnp.dot(
                expo.astype(jnp.bfloat16),
                key_block[:, :kv_rank],
                preferred_element_type=jnp.float32,
            )

    big = (full_to - full_from) // KEY_BLOCK

    @pl.loop(0, (full_from - first + EDGE_BLOCK - 1) // EDGE_BLOCK)
    def _(i):
        fold(first + i * EDGE_BLOCK, EDGE_BLOCK, True)

    @pl.loop(0, big)
    def _(i):
        fold(full_from + i * KEY_BLOCK, KEY_BLOCK, False)

    rest = full_from + big * KEY_BLOCK

    @pl.loop(0, (last - rest + EDGE_BLOCK - 1) // EDGE_BLOCK)
    def _(i):
        fold(rest + i * EDGE_BLOCK, EDGE_BLOCK, True)

    norm = 1.0 / jnp.sum(total[...], axis=1, keepdims=True)
    out_ref[...] = (acc[...] * norm).astype(jnp.bfloat16).reshape(heads, tokens, kv_rank)


def shards(query_nope, query_rope, latent, up_key, value_up_weight, lengths, owner_request_table):
    section_index = lax.axis_index("section")
    owner_index = lax.axis_index("seq")
    is_prefill = section_index == 0
    seq_count = lax.axis_size("seq")
    tok_dev, head_dev, nope_dim = query_nope.shape[1:]
    rope_dim = query_rope.shape[2] // head_dev
    kv_rank = up_key.shape[1]
    width = kv_rank + rope_dim
    tokens_all = tok_dev * seq_count
    req_dev = owner_request_table.shape[0] // seq_count
    groups = owner_request_table.shape[0] // lengths.shape[0]
    band_tokens = tok_dev // req_dev
    exponent_scale = math.log2(math.e) / math.sqrt(nope_dim + rope_dim)

    own_part = dequantized(latent[0])
    came = lax.ppermute(own_part, "section", [(0, 1)])
    part = jnp.where(is_prefill, own_part, came)
    keys = lax.all_gather(part, ("seq", "head"), axis=0, tiled=True)
    keys = jnp.pad(keys, ((0, EDGE_BLOCK), (0, 0)))
    own_keys = lax.all_gather(
        jnp.where(is_prefill, own_part, latent[0]), "head", axis=0, tiled=True
    )

    lifted = jnp.einsum("thn,hkn->htk", query_nope[0], up_key, preferred_element_type=jnp.float32)
    rope_part = query_rope[0].reshape(tok_dev, head_dev, rope_dim).swapaxes(0, 1)
    queries = jnp.concatenate([lifted.astype(jnp.bfloat16), rope_part], axis=2)

    prompt_ends = jnp.cumsum(lengths)
    starts = prompt_ends - lengths
    positions = owner_index * tok_dev + jnp.arange(tok_dev, dtype=jnp.int32)
    prefill_low = token_start(positions, starts)
    band_at = owner_index * tok_dev + band_tokens * jnp.arange(req_dev, dtype=jnp.int32)
    own_requests = (
        lax.dynamic_slice_in_dim(owner_request_table, owner_index * req_dev, req_dev, 0) // groups
    )
    chosen = own_requests[:, None] == jnp.arange(lengths.shape[0], dtype=jnp.int32)[None, :]
    slot_low = jnp.sum(jnp.where(chosen, starts[None, :], 0), axis=1)
    slot_high = jnp.sum(jnp.where(chosen, prompt_ends[None, :], 0), axis=1)
    row_low = jnp.where(is_prefill, prefill_low, jnp.repeat(slot_low, band_tokens))
    by_band = row_low.reshape(req_dev, band_tokens)
    last = jnp.where(is_prefill, jnp.maximum(band_at, by_band[:, 0]), slot_high)
    first = jnp.minimum(by_band[:, 0], last) // 16 * 16
    highest_low = jnp.minimum(by_band[:, -1], last)
    full_from = jnp.minimum((highest_low + 15) // 16 * 16, last // 16 * 16)
    full_from = jnp.maximum(full_from, first)
    full_from = jnp.where(first == highest_low, first, full_from)
    full_from = first + (full_from - first + EDGE_BLOCK - 1) // EDGE_BLOCK * EDGE_BLOCK
    full_from = jnp.minimum(full_from, tokens_all)
    full_to = jnp.maximum(last, full_from)
    last_seen = last
    plan = jnp.stack([first, full_from, full_to, last_seen]).astype(jnp.int32)

    here = jnp.arange(band_tokens, dtype=jnp.int32)
    same_sample = here[None, :] % SAMPLES == here[:, None] % SAMPLES
    earlier_step = here[None, :] // SAMPLES <= here[:, None] // SAMPLES
    decode_seen = jnp.broadcast_to(
        (same_sample & earlier_step)[None], (req_dev, band_tokens, band_tokens)
    )
    prefill_seen = (here[None, None, :] <= here[None, :, None]) & (
        band_at[:, None, None] + here[None, None, :] >= by_band[:, :, None]
    )
    seen = jnp.where(is_prefill, prefill_seen, decode_seen)
    bias = jnp.where(seen, 0.0, masked_low).astype(jnp.float32).reshape(tok_dev, band_tokens)

    rows = head_dev * band_tokens
    latent_out = pl.pallas_call(
        functools.partial(flash_kernel, kv_rank, exponent_scale),
        out_shape=jax.ShapeDtypeStruct((head_dev, tok_dev, kv_rank), jnp.bfloat16),
        grid_spec=pltpu.PrefetchScalarGridSpec(
            num_scalar_prefetch=1,
            grid=(req_dev,),
            in_specs=[
                pl.BlockSpec((head_dev, band_tokens, width), lambda i, s: (0, i, 0)),
                pl.BlockSpec(memory_space=pltpu.VMEM),
                pl.BlockSpec((band_tokens, width), lambda i, s: (i, 0)),
                pl.BlockSpec((band_tokens, 1), lambda i, s: (i, 0)),
                pl.BlockSpec((band_tokens, band_tokens), lambda i, s: (i, 0)),
            ],
            out_specs=pl.BlockSpec((head_dev, band_tokens, kv_rank), lambda i, s: (0, i, 0)),
            scratch_shapes=[
                pltpu.VMEM((rows, kv_rank), jnp.float32),
                pltpu.VMEM((rows, LANES), jnp.float32),
                pltpu.VMEM((rows, LANES), jnp.float32),
            ],
        ),
        compiler_params=pltpu.CompilerParams(vmem_limit_bytes=48 << 20),
    )(plan, queries, keys, own_keys, row_low[:, None], bias)

    attended = jnp.einsum(
        "htk,hkv->thv", latent_out, value_up_weight, preferred_element_type=jnp.float32
    )
    return attended.astype(jnp.bfloat16)[None]


def solution(mesh):
    in_specs = (
        P("section", "seq", "head", None),
        P("section", "seq", "head"),
        P("section", ("seq", "head"), None),
        P("head", None, None),
        P("head", None, None),
        P(),
        P(),
    )
    out_specs = P("section", "seq", "head", None)
    return jax.shard_map(shards, mesh=mesh, in_specs=in_specs, out_specs=out_specs, check_vma=False)
```

```python
import functools
import math

import jax
import jax.numpy as jnp
from jax import lax
from jax.experimental import pallas as pl
from jax.experimental.pallas import tpu as pltpu
from jax.sharding import PartitionSpec as P

SAMPLES = 8
STEPS = 4
BLOCK = 64

scale_top = 448.0
tiny_eps = 1e-06
masked_low = -1e30

KEY_BLOCK = 1024
EDGE_BLOCK = 512
LANES = 128


def gather_kernel(
    z_count, y_count, own_in, keys, own_out, block, mine_sem, x_send, x_recv, own_sems,
    z_send, z_recv, y_send, y_recv, sib_send, sib_recv,
):
    section = lax.axis_index("section")
    seq = lax.axis_index("seq")
    core = lax.axis_index("head")
    z = seq // (2 * y_count)
    y = seq // 2 % y_count
    hi = seq % 2

    def place(dz, dy):
        return lax.rem(z + dz + z_count, z_count), lax.rem(y + dy + y_count, y_count)

    def device(dz=0, dy=0, to_hi=None, to_section=None, to_core=None):
        tz, ty = place(dz, dy)
        th = hi if to_hi is None else to_hi
        return (
            section if to_section is None else to_section,
            (tz * y_count + ty) * 2 + th,
            core if to_core is None else to_core,
        )

    barrier = pltpu.get_barrier_semaphore()
    peers = [
        device(to_core=1 - core),
        device(to_section=1 - section),
        device(to_hi=1 - hi),
        device(to_section=1 - section, to_hi=1 - hi),
        device(dz=1),
        device(dz=-1),
        device(dy=1),
        device(dy=-1),
    ]
    for peer in peers:
        pl.semaphore_signal(barrier, inc=1, device_id=peer, device_id_type=pl.DeviceIdType.MESH)

    @pl.when(section == 0)
    def _():
        rows = own_in[...].astype(jnp.float32)
        largest = jnp.max(jnp.abs(rows))
        spread = jnp.full((8, LANES), largest, jnp.float32)
        scale = ((spread + tiny_eps) / scale_top).astype(jnp.bfloat16).astype(jnp.float32)
        factor = scale[:1, :1]
        stored = (rows / factor).astype(jnp.bfloat16)
        block[...] = (stored.astype(jnp.float32) * factor).astype(jnp.bfloat16)

    @pl.when(section == 1)
    def _():
        block[...] = own_in[...]

    pl.semaphore_wait(barrier, len(peers))

    def send(src, dst, to, send_sem, recv_sem):
        copy = pltpu.make_async_remote_copy(
            src_ref=src,
            dst_ref=dst,
            send_sem=send_sem,
            recv_sem=recv_sem,
            device_id=to,
            device_id_type=pl.DeviceIdType.MESH,
        )
        copy.start()
        return copy

    def arrive(dst, recv_sem):
        pltpu.make_async_remote_copy(
            src_ref=dst,
            dst_ref=dst,
            send_sem=recv_sem,
            recv_sem=recv_sem,
            device_id=device(to_core=1 - core),
            device_id_type=pl.DeviceIdType.MESH,
        ).wait_recv()

    own_local = pltpu.make_async_copy(block, own_out.at[core], own_sems.at[0])
    own_local.start()
    own_away = send(
        block, own_out.at[core], device(to_core=1 - core), own_sems.at[1], own_sems.at[2]
    )

    @pl.when(section == 0)
    def _():
        spot = keys.at[z, y, hi, core]
        local = pltpu.make_async_copy(block, spot, mine_sem)
        local.start()
        went = [
            send(block, spot, device(to_section=1), x_send.at[0], x_recv.at[0]),
            send(block, spot, device(to_section=1, to_hi=1 - hi), x_send.at[1], x_recv.at[1]),
            send(block, spot, device(to_hi=1 - hi), x_send.at[2], x_recv.at[1]),
        ]
        local.wait()
        arrive(keys.at[z, y, 1 - hi, core], x_recv.at[1])
        for copy in went:
            copy.wait_send()

    @pl.when(section == 1)
    def _():
        arrive(keys.at[z, y, hi, core], x_recv.at[0])
        arrive(keys.at[z, y, 1 - hi, core], x_recv.at[1])

    half = z_count // 2

    @pl.when(core == 0)
    def _():
        c = 0
        went = [
            send(keys.at[z, y, :, c], keys.at[z, y, :, c], device(dy=1), y_send.at[0, 0], y_recv.at[0, 0]),
            send(keys.at[z, y, :, c], keys.at[z, y, :, c], device(dy=-1), y_send.at[0, 1], y_recv.at[0, 1]),
        ]
        _, low = place(0, -1)
        _, high = place(0, 1)
        _, far = place(0, 2)
        arrive(keys.at[z, low, :, c], y_recv.at[0, 0])
        went.append(
            send(keys.at[z, low, 0, c], keys.at[z, low, 0, c], device(dy=1), y_send.at[0, 2], y_recv.at[0, 2])
        )
        arrive(keys.at[z, high, :, c], y_recv.at[0, 1])
        went.append(
            send(keys.at[z, high, 1, c], keys.at[z, high, 1, c], device(dy=-1), y_send.at[0, 3], y_recv.at[0, 3])
        )
        arrive(keys.at[z, far, 0, c], y_recv.at[0, 2])
        arrive(keys.at[z, far, 1, c], y_recv.at[0, 3])

        def plane(at):
            return keys.at[at, :, :, c]

        def ahead(at, step, up):
            d = 1 if up else -1
            if step < half - 1:
                part = plane(at)
            else:
                part = keys.at[at, pl.ds(0 if up else y_count // 2, y_count // 2), :, c]
            j = 0 if up else 1
            went.append(send(part, part, device(dz=d), z_send.at[j, step], z_recv.at[j, step]))

        def to_sibling(at, n):
            went.append(
                send(plane(at), plane(at), device(to_core=1), sib_send.at[n], sib_recv.at[n])
            )

        ahead(z, 0, True)
        ahead(z, 0, False)
        to_sibling(z, 0)
        for s in range(1, half):
            below, _ = place(-s, 0)
            above, _ = place(s, 0)
            arrive(plane(below), z_recv.at[0, s - 1])
            ahead(below, s, True)
            arrive(plane(above), z_recv.at[1, s - 1])
            ahead(above, s, False)
            to_sibling(below, 2 * s - 1)
            to_sibling(above, 2 * s)
        across, _ = place(half, 0)
        arrive(keys.at[across, pl.ds(0, y_count // 2), :, c], z_recv.at[0, half - 1])
        arrive(keys.at[across, pl.ds(y_count // 2, y_count // 2), :, c], z_recv.at[1, half - 1])
        to_sibling(across, z_count - 1)
        for copy in went:
            copy.wait_send()

    @pl.when(core == 1)
    def _():
        c = 1
        went = []
        planes = [place(0, 0)[0]]
        for s in range(1, half):
            planes += [place(-s, 0)[0], place(s, 0)[0]]
        planes.append(place(half, 0)[0])
        _, low = place(0, -1)
        _, high = place(0, 1)
        _, far = place(0, 2)

        def ahead(at, step, up):
            d = 1 if up else -1
            j = 0 if up else 1
            if step < half - 1:
                part = keys.at[at, y, :, c]
            else:
                part = keys.at[at, y, 0 if up else 1, c]
            went.append(send(part, part, device(dz=d), z_send.at[j, step], z_recv.at[j, step]))

        def spread(n):
            part = keys.at[planes[n], y, :, c]
            went.append(send(part, part, device(dy=1), y_send.at[n, 0], y_recv.at[n, 0]))
            went.append(send(part, part, device(dy=-1), y_send.at[n, 1], y_recv.at[n, 1]))

        def spread_on(n):
            at = planes[n]
            arrive(keys.at[at, low, :, c], y_recv.at[n, 0])
            part = keys.at[at, low, 0, c]
            went.append(send(part, part, device(dy=1), y_send.at[n, 2], y_recv.at[n, 2]))
            arrive(keys.at[at, high, :, c], y_recv.at[n, 1])
            part = keys.at[at, high, 1, c]
            went.append(send(part, part, device(dy=-1), y_send.at[n, 3], y_recv.at[n, 3]))

        def finish(n):
            at = planes[n]
            arrive(keys.at[at, far, 0, c], y_recv.at[n, 2])
            arrive(keys.at[at, far, 1, c], y_recv.at[n, 3])
            part = keys.at[at, :, :, c]
            went.append(send(part, part, device(to_core=0), sib_send.at[n], sib_recv.at[n]))

        ahead(planes[0], 0, True)
        ahead(planes[0], 0, False)
        spread(0)
        for s in range(1, half):
            arrive(keys.at[planes[2 * s - 1], y, :, c], z_recv.at[0, s - 1])
            ahead(planes[2 * s - 1], s, True)
            arrive(keys.at[planes[2 * s], y, :, c], z_recv.at[1, s - 1])
            ahead(planes[2 * s], s, False)
            spread(2 * s - 1)
            spread(2 * s)
        arrive(keys.at[planes[-1], y, 0, c], z_recv.at[0, half - 1])
        arrive(keys.at[planes[-1], y, 1, c], z_recv.at[1, half - 1])
        spread(z_count - 1)
        for n in range(z_count):
            spread_on(n)
            if n >= 1:
                finish(n - 1)
        finish(z_count - 1)
        for copy in went:
            copy.wait_send()

    other = 1 - core
    order = [place(0, 0)[0]]
    for s in range(1, half):
        order += [place(-s, 0)[0], place(s, 0)[0]]
    order.append(place(half, 0)[0])
    for n, at in enumerate(order):
        arrive(keys.at[at, :, :, other], sib_recv.at[n])
    arrive(own_out.at[other], own_sems.at[2])
    own_away.wait_send()
    own_local.wait()


def gathered(own, seq_count):
    rows, width = own.shape
    y_count = 4
    z_count = seq_count // (2 * y_count)
    dma = pltpu.SemaphoreType.DMA
    keys, pair = pl.pallas_call(
        functools.partial(gather_kernel, z_count, y_count),
        out_shape=[
            jax.ShapeDtypeStruct((z_count, y_count, 2, 2, rows, width), own.dtype),
            jax.ShapeDtypeStruct((2, rows, width), own.dtype),
        ],
        in_specs=[pl.BlockSpec(memory_space=pltpu.VMEM)],
        out_specs=[pl.BlockSpec(memory_space=pl.ANY), pl.BlockSpec(memory_space=pl.ANY)],
        scratch_shapes=[
            pltpu.VMEM((rows, width), own.dtype),
            dma(()),
            dma((3,)),
            dma((2,)),
            dma((3,)),
            dma((2, z_count // 2)),
            dma((2, z_count // 2)),
            dma((z_count, 4)),
            dma((z_count, 4)),
            dma((z_count,)),
            dma((z_count,)),
        ],
        compiler_params=pltpu.CompilerParams(collective_id=0, has_side_effects=True),
    )(own)
    return keys.reshape(-1, width), pair.reshape(-1, width)


def token_start(positions, starts):
    return jnp.max(jnp.where(starts[None, :] <= positions[:, None], starts[None, :], 0), axis=1)


def over_lanes(value, width):
    return jnp.concatenate([value] * (width // LANES), axis=1)


def flash_kernel(
    kv_rank,
    exponent_scale,
    plan,
    q_ref,
    keys,
    own_keys,
    low_ref,
    bias_ref,
    out_ref,
    acc,
    top,
    total,
    held,
    sems,
):
    band = pl.program_id(0)
    heads, tokens, width = q_ref.shape
    rows = heads * tokens
    all_keys = keys.shape[0]
    first, full_from, last = (plan[i, band] for i in range(3))
    chunks = (last - first + KEY_BLOCK - 1) // KEY_BLOCK

    def chunk_at(i):
        return pl.multiple_of(jnp.minimum(first + i * KEY_BLOCK, all_keys - KEY_BLOCK), 16)

    def fetch(i):
        slot = lax.rem(i, 2)
        return pltpu.make_async_copy(
            keys.at[pl.ds(chunk_at(i), KEY_BLOCK), :], held.at[slot], sems.at[slot]
        )

    @pl.when(chunks > 0)
    def _():
        fetch(0).start()

    q = q_ref[...].reshape(rows, width)
    own = own_keys[...]
    nt = (((1,), (1,)), ((), ()))

    scores = lax.dot_general(q, own, nt, preferred_element_type=jnp.float32)
    bias = jnp.broadcast_to(bias_ref[...][None], (heads, tokens, tokens)).reshape(rows, tokens)
    scores = scores + bias
    own_top = jnp.max(scores, axis=1, keepdims=True)
    expo = jnp.exp2((scores - own_top) * exponent_scale)
    lane = lax.broadcasted_iota(jnp.int32, (rows, LANES), 1)
    total[...] = jnp.where(lane == 0, jnp.sum(expo, axis=1, keepdims=True), 0.0)
    top[...] = jnp.broadcast_to(own_top, (rows, LANES))
    acc[...] = jnp.dot(
        expo.astype(jnp.bfloat16), own[:, :kv_rank], preferred_element_type=jnp.float32
    )

    def fold(key_block, low_spot, at):
        count = key_block.shape[0]
        s = lax.dot_general(q, key_block, nt, preferred_element_type=jnp.float32)
        if low_spot is not None:
            low = jnp.broadcast_to(low_ref[...][None], (heads, tokens, 1)).reshape(rows, 1)
            spot = at + lax.broadcasted_iota(jnp.int32, (1, count), 1)
            s = jnp.where((spot >= jnp.maximum(low, low_spot)) & (spot < last), s, masked_low)
        before = top[...]
        now = jnp.maximum(before, jnp.max(s, axis=1, keepdims=True))
        shrink = jnp.exp2((before - now) * exponent_scale)
        expo = jnp.exp2((s - over_lanes(now, count)) * exponent_scale)
        top[...] = now
        summed = total[...] * shrink
        for c in range(0, count, LANES):
            summed = summed + expo[:, c : c + LANES]
        total[...] = summed
        acc[...] = acc[...] * over_lanes(shrink, kv_rank) + jnp.dot(
            expo.astype(jnp.bfloat16), key_block[:, :kv_rank], preferred_element_type=jnp.float32
        )

    @pl.loop(0, chunks)
    def _(i):
        slot = lax.rem(i, 2)
        fetch(i).wait()

        @pl.when(i + 1 < chunks)
        def _():
            fetch(i + 1).start()

        nominal = first + i * KEY_BLOCK
        at = chunk_at(i)
        whole = (nominal >= full_from) & (nominal + KEY_BLOCK <= last)

        @pl.when(whole)
        def _():
            fold(held[slot], None, None)

        @pl.when(jnp.logical_not(whole))
        def _():
            skip = (nominal - at) // EDGE_BLOCK

            @pl.loop(skip, (jnp.minimum(last - at, KEY_BLOCK) + EDGE_BLOCK - 1) // EDGE_BLOCK)
            def _(j):
                here = pl.multiple_of(j * EDGE_BLOCK, EDGE_BLOCK)
                fold(held[slot, pl.ds(here, EDGE_BLOCK), :], nominal, at + here)

    norm = 1.0 / jnp.sum(total[...], axis=1, keepdims=True)
    out_ref[...] = (acc[...] * norm).astype(jnp.bfloat16).reshape(heads, tokens, kv_rank)


def shards(query_nope, query_rope, latent, up_key, value_up_weight, lengths, owner_request_table):
    section_index = lax.axis_index("section")
    owner_index = lax.axis_index("seq")
    is_prefill = section_index == 0
    seq_count = lax.axis_size("seq")
    tok_dev, head_dev, nope_dim = query_nope.shape[1:]
    rope_dim = query_rope.shape[2] // head_dev
    kv_rank = up_key.shape[1]
    width = kv_rank + rope_dim
    req_dev = owner_request_table.shape[0] // seq_count
    groups = owner_request_table.shape[0] // lengths.shape[0]
    band_tokens = tok_dev // req_dev
    exponent_scale = math.log2(math.e) / math.sqrt(nope_dim + rope_dim)

    keys, own_keys = gathered(latent[0], seq_count)

    lifted = jnp.einsum("thn,hkn->htk", query_nope[0], up_key, preferred_element_type=jnp.float32)
    rope_part = query_rope[0].reshape(tok_dev, head_dev, rope_dim).swapaxes(0, 1)
    queries = jnp.concatenate([lifted.astype(jnp.bfloat16), rope_part], axis=2)

    prompt_ends = jnp.cumsum(lengths)
    starts = prompt_ends - lengths
    positions = owner_index * tok_dev + jnp.arange(tok_dev, dtype=jnp.int32)
    prefill_low = token_start(positions, starts)
    band_at = owner_index * tok_dev + band_tokens * jnp.arange(req_dev, dtype=jnp.int32)
    own_requests = (
        lax.dynamic_slice_in_dim(owner_request_table, owner_index * req_dev, req_dev, 0) // groups
    )
    chosen = own_requests[:, None] == jnp.arange(lengths.shape[0], dtype=jnp.int32)[None, :]
    slot_low = jnp.sum(jnp.where(chosen, starts[None, :], 0), axis=1)
    slot_high = jnp.sum(jnp.where(chosen, prompt_ends[None, :], 0), axis=1)
    row_low = jnp.where(is_prefill, prefill_low, jnp.repeat(slot_low, band_tokens))
    by_band = row_low.reshape(req_dev, band_tokens)
    last = jnp.where(is_prefill, jnp.maximum(band_at, by_band[:, 0]), slot_high)
    first = jnp.minimum(by_band[:, 0], last) // 16 * 16
    highest_low = jnp.minimum(by_band[:, -1], last)
    plan = jnp.stack([first, highest_low, last]).astype(jnp.int32)

    here = jnp.arange(band_tokens, dtype=jnp.int32)
    same_sample = here[None, :] % SAMPLES == here[:, None] % SAMPLES
    earlier_step = here[None, :] // SAMPLES <= here[:, None] // SAMPLES
    decode_seen = jnp.broadcast_to(
        (same_sample & earlier_step)[None], (req_dev, band_tokens, band_tokens)
    )
    prefill_seen = (here[None, None, :] <= here[None, :, None]) & (
        band_at[:, None, None] + here[None, None, :] >= by_band[:, :, None]
    )
    seen = jnp.where(is_prefill, prefill_seen, decode_seen)
    bias = jnp.where(seen, 0.0, masked_low).astype(jnp.float32).reshape(tok_dev, band_tokens)

    rows = head_dev * band_tokens
    latent_out = pl.pallas_call(
        functools.partial(flash_kernel, kv_rank, exponent_scale),
        out_shape=jax.ShapeDtypeStruct((head_dev, tok_dev, kv_rank), jnp.bfloat16),
        grid_spec=pltpu.PrefetchScalarGridSpec(
            num_scalar_prefetch=1,
            grid=(req_dev,),
            in_specs=[
                pl.BlockSpec((head_dev, band_tokens, width), lambda i, s: (0, i, 0)),
                pl.BlockSpec(memory_space=pl.ANY),
                pl.BlockSpec((band_tokens, width), lambda i, s: (i, 0)),
                pl.BlockSpec((band_tokens, 1), lambda i, s: (i, 0)),
                pl.BlockSpec((band_tokens, band_tokens), lambda i, s: (i, 0)),
            ],
            out_specs=pl.BlockSpec((head_dev, band_tokens, kv_rank), lambda i, s: (0, i, 0)),
            scratch_shapes=[
                pltpu.VMEM((rows, kv_rank), jnp.float32),
                pltpu.VMEM((rows, LANES), jnp.float32),
                pltpu.VMEM((rows, LANES), jnp.float32),
                pltpu.VMEM((2, KEY_BLOCK, width), jnp.bfloat16),
                pltpu.SemaphoreType.DMA((2,)),
            ],
        ),
        compiler_params=pltpu.CompilerParams(vmem_limit_bytes=48 << 20),
    )(plan, queries, keys, own_keys, row_low[:, None], bias)

    attended = jnp.einsum(
        "htk,hkv->thv", latent_out, value_up_weight, preferred_element_type=jnp.float32
    )
    return attended.astype(jnp.bfloat16)[None]


def solution(mesh):
    in_specs = (
        P("section", "seq", "head", None),
        P("section", "seq", "head"),
        P("section", ("seq", "head"), None),
        P("head", None, None),
        P("head", None, None),
        P(),
        P(),
    )
    out_specs = P("section", "seq", "head", None)
    return jax.shard_map(shards, mesh=mesh, in_specs=in_specs, out_specs=out_specs, check_vma=False)
```

```python
import functools
import math

import jax
import jax.numpy as jnp
from jax import lax
from jax.experimental import pallas as pl
from jax.experimental.pallas import tpu as pltpu
from jax.sharding import PartitionSpec as P

SAMPLES = 8
STEPS = 4
BLOCK = 64

scale_top = 448.0
tiny_eps = 1e-06
masked_low = -1e30

KEY_BLOCK = 1024
EDGE_BLOCK = 512
LANES = 128


def prefill_kernel(
    z_count, y_count, kv_rank, exponent_scale, own_in, q_nope, q_rope, up_key, lengths,
    keys, own_out, q_out, latent_out, block, nope, up, q, acc, top, total, held, bias,
    in_sems, out_sems, held_sems, x_send, x_recv, own_sems,
    z_send, z_recv, y_send, y_recv, sib_send, sib_recv,
):
    section = lax.axis_index("section")
    seq = lax.axis_index("seq")
    core = lax.axis_index("head")
    z = seq // (2 * y_count)
    y = seq // 2 % y_count
    hi = seq % 2
    half = z_count // 2
    heads, tokens, width = q.shape
    plane_blocks = 2 * y_count
    at_block = seq % plane_blocks
    plane_keys = plane_blocks * tokens
    nt = (((1,), (1,)), ((), ()))

    def plane_at(dz):
        return lax.rem(z + dz + z_count, z_count)

    def row_at(dy):
        return lax.rem(y + dy + y_count, y_count)

    def device(dz=0, dy=0, to_hi=None, to_section=None, to_core=None):
        th = hi if to_hi is None else to_hi
        return (
            section if to_section is None else to_section,
            (plane_at(dz) * y_count + row_at(dy)) * 2 + th,
            core if to_core is None else to_core,
        )

    loads = [
        pltpu.make_async_copy(q_nope, nope, in_sems.at[0]),
        pltpu.make_async_copy(up_key, up, in_sems.at[1]),
    ]
    for load in loads:
        load.start()

    barrier = pltpu.get_barrier_semaphore()
    peers = [
        device(to_core=1 - core),
        device(to_section=1 - section),
        device(to_hi=1 - hi),
        device(to_section=1 - section, to_hi=1 - hi),
        device(dz=1),
        device(dz=-1),
        device(dy=1),
        device(dy=-1),
    ]
    for peer in peers:
        pl.semaphore_signal(barrier, inc=1, device_id=peer, device_id_type=pl.DeviceIdType.MESH)

    @pl.when(section == 0)
    def _():
        rows = own_in[...].astype(jnp.float32)
        largest = jnp.max(jnp.abs(rows))
        spread = jnp.full((8, LANES), largest, jnp.float32)
        scale = ((spread + tiny_eps) / scale_top).astype(jnp.bfloat16).astype(jnp.float32)
        factor = scale[:1, :1]
        stored = (rows / factor).astype(jnp.bfloat16)
        block[...] = (stored.astype(jnp.float32) * factor).astype(jnp.bfloat16)

    @pl.when(section == 1)
    def _():
        block[...] = own_in[...]

    pl.semaphore_wait(barrier, len(peers))

    def remote(src, dst, to, send_sem, recv_sem):
        return pltpu.make_async_remote_copy(
            src_ref=src,
            dst_ref=dst,
            send_sem=send_sem,
            recv_sem=recv_sem,
            device_id=to,
            device_id_type=pl.DeviceIdType.MESH,
        )

    def arrive(dst, recv_sem):
        remote(dst, dst, device(to_core=1 - core), recv_sem, recv_sem).wait_recv()

    def own_local():
        return pltpu.make_async_copy(block, own_out.at[core], own_sems.at[0])

    def own_away():
        to = device(to_core=1 - core)
        return remote(block, own_out.at[core], to, own_sems.at[1], own_sems.at[2])

    def x_copies():
        spot = keys.at[z, y, hi, core]
        return [
            remote(block, spot, device(to_section=1), x_send.at[0], x_recv.at[0]),
            remote(block, spot, device(to_hi=1 - hi), x_send.at[2], x_recv.at[1]),
            remote(block, spot, device(to_section=1, to_hi=1 - hi), x_send.at[1], x_recv.at[1]),
        ]

    def x_local():
        return pltpu.make_async_copy(block, keys.at[z, y, hi, core], x_send.at[3])

    @pl.when(section == 0)
    def _():
        x_local().start()
        for copy in x_copies():
            copy.start()

    own_local().start()
    own_away().start()

    for load in loads:
        load.wait()

    @pl.loop(0, heads // 2)
    def _(pair):
        rope = q_rope[:, pl.ds(pl.multiple_of(pair * LANES, LANES), LANES)]
        for side in range(2):
            head = pair * 2 + side
            lifted = lax.dot_general(nope[head], up[head], nt, preferred_element_type=jnp.float32)
            q[head, :, :kv_rank] = lifted.astype(jnp.bfloat16)
            q[head, :, kv_rank:] = rope[:, side * (LANES // 2) : (side + 1) * (LANES // 2)]

    @pl.when(section == 1)
    def _():
        pltpu.make_async_copy(q, q_out, out_sems.at[0]).start()

    @pl.when(section == 0)
    def _():
        x_local().wait()
        arrive(keys.at[z, y, 1 - hi, core], x_recv.at[1])

    @pl.when(section == 1)
    def _():
        arrive(keys.at[z, y, hi, core], x_recv.at[0])
        arrive(keys.at[z, y, 1 - hi, core], x_recv.at[1])

    low, high, far = row_at(-1), row_at(1), row_at(2)
    planes = [z]
    for s in range(1, half):
        planes += [plane_at(-s), plane_at(s)]
    planes.append(plane_at(half))
    steps = [[0]] + [[2 * s - 1, 2 * s] for s in range(1, half)] + [[z_count - 1]]

    a_went = []

    def a_send(src, to, send_sem, recv_sem):
        copy = lambda: remote(src(), src(), to(), send_sem(), recv_sem())
        a_went.append(copy)
        copy().start()

    def a_plane(n):
        return lambda: keys.at[planes[n], :, :, 0]

    def a_ahead(n, step, up_way):
        d, j = (1, 0) if up_way else (-1, 1)
        part = a_plane(n)
        if step == half - 1:
            part = lambda: keys.at[planes[n], pl.ds(j * (y_count // 2), y_count // 2), :, 0]
        a_send(
            part, lambda: device(dz=d), lambda: z_send.at[j, step], lambda: z_recv.at[j, step]
        )

    def a_sibling(n):
        a_send(
            a_plane(n), lambda: device(to_core=1), lambda: sib_send.at[n], lambda: sib_recv.at[n]
        )

    def a_y(src, d, k):
        a_send(src, lambda: device(dy=d), lambda: y_send.at[0, k], lambda: y_recv.at[0, k])

    def a_start():
        mine = lambda: keys.at[z, y, :, 0]
        a_y(mine, 1, 0)
        a_y(mine, -1, 1)
        arrive(keys.at[z, low, :, 0], y_recv.at[0, 0])
        a_y(lambda: keys.at[z, low, 0, 0], 1, 2)
        arrive(keys.at[z, high, :, 0], y_recv.at[0, 1])
        a_y(lambda: keys.at[z, high, 1, 0], -1, 3)
        arrive(keys.at[z, far, 0, 0], y_recv.at[0, 2])
        arrive(keys.at[z, far, 1, 0], y_recv.at[0, 3])
        a_ahead(0, 0, True)
        a_ahead(0, 0, False)
        a_sibling(0)

    def a_point(s):
        if s < half:
            below, above = steps[s]
            arrive(a_plane(below)(), z_recv.at[0, s - 1])
            a_ahead(below, s, True)
            arrive(a_plane(above)(), z_recv.at[1, s - 1])
            a_ahead(above, s, False)
            a_sibling(below)
            a_sibling(above)
        else:
            for j in range(2):
                part = keys.at[planes[-1], pl.ds(j * (y_count // 2), y_count // 2), :, 0]
                arrive(part, z_recv.at[j, half - 1])
            a_sibling(z_count - 1)

    b_went = []

    def b_send(src, to, send_sem, recv_sem):
        copy = lambda: remote(src(), src(), to(), send_sem(), recv_sem())
        b_went.append(copy)
        copy().start()

    def b_ahead(n, step, up_way):
        d, j = (1, 0) if up_way else (-1, 1)
        if step < half - 1:
            part = lambda: keys.at[planes[n], y, :, 1]
        else:
            part = lambda: keys.at[planes[n], y, j, 1]
        b_send(
            part, lambda: device(dz=d), lambda: z_send.at[j, step], lambda: z_recv.at[j, step]
        )

    def b_y(src, d, n, k):
        b_send(src, lambda: device(dy=d), lambda: y_send.at[n, k], lambda: y_recv.at[n, k])

    def b_spread(n):
        b_y(lambda: keys.at[planes[n], y, :, 1], 1, n, 0)
        b_y(lambda: keys.at[planes[n], y, :, 1], -1, n, 1)

    def b_spread_on(n):
        arrive(keys.at[planes[n], low, :, 1], y_recv.at[n, 0])
        b_y(lambda: keys.at[planes[n], low, 0, 1], 1, n, 2)
        arrive(keys.at[planes[n], high, :, 1], y_recv.at[n, 1])
        b_y(lambda: keys.at[planes[n], high, 1, 1], -1, n, 3)

    def b_finish(n):
        arrive(keys.at[planes[n], far, 0, 1], y_recv.at[n, 2])
        arrive(keys.at[planes[n], far, 1, 1], y_recv.at[n, 3])
        b_send(
            lambda: keys.at[planes[n], :, :, 1],
            lambda: device(to_core=0),
            lambda: sib_send.at[n],
            lambda: sib_recv.at[n],
        )

    def b_chain(s):
        if s < half:
            below, above = steps[s]
            arrive(keys.at[planes[below], y, :, 1], z_recv.at[0, s - 1])
            b_ahead(below, s, True)
            arrive(keys.at[planes[above], y, :, 1], z_recv.at[1, s - 1])
            b_ahead(above, s, False)
        else:
            arrive(keys.at[planes[-1], y, 0, 1], z_recv.at[0, half - 1])
            arrive(keys.at[planes[-1], y, 1, 1], z_recv.at[1, half - 1])
        for n in steps[s]:
            b_spread(n)

    def b_start():
        b_ahead(0, 0, True)
        b_ahead(0, 0, False)
        b_spread(0)
        b_spread_on(0)
        b_chain(1)
        b_finish(0)

    def b_point(s):
        for n in steps[s]:
            b_spread_on(n)
        if s < half:
            b_chain(s + 1)
        for n in steps[s]:
            b_finish(n)

    def point(s):
        @pl.when(core == 0)
        def _():
            a_start() if s == 0 else a_point(s)

        @pl.when(core == 1)
        def _():
            b_start() if s == 0 else b_point(s)

    def from_sibling(s):
        for n in steps[s]:
            arrive(keys.at[planes[n], :, :, 1 - core], sib_recv.at[n])

    @pl.when(section == 0)
    def _():
        top[...] = jnp.full(top.shape, masked_low, jnp.float32)
        total[...] = jnp.zeros(total.shape, jnp.float32)
        acc[...] = jnp.zeros(acc.shape, jnp.float32)

    token = lax.broadcasted_iota(jnp.int32, (tokens, 1), 0)
    position = seq * tokens + token
    count = lengths.shape[0]
    before_it = lax.broadcasted_iota(jnp.int32, (count, count), 0) < lax.broadcasted_iota(
        jnp.int32, (count, count), 1
    )
    starts = jnp.sum(
        jnp.where(before_it, lengths[...].astype(jnp.float32), 0.0), axis=0, keepdims=True
    )
    row_low = jnp.max(
        jnp.where(starts <= position.astype(jnp.float32), starts, 0.0), axis=1, keepdims=True
    ).astype(jnp.int32)

    chunk = plane_keys // 2
    tile_heads = 8
    rows = tile_heads * tokens

    def fold(first_spot, side):
        spot = first_spot + lax.broadcasted_iota(jnp.int32, (1, chunk), 1)
        seen = (spot >= row_low) & (spot <= position)
        bias[...] = jnp.where(seen, 0.0, masked_low)

        @pl.loop(0, heads // tile_heads)
        def _(tile):
            part = pl.ds(pl.multiple_of(tile * rows, rows), rows)
            asked = q[pl.ds(tile * tile_heads, tile_heads)].reshape(rows, width)
            s = lax.dot_general(asked, held[side].reshape(chunk, width), nt, preferred_element_type=jnp.float32)
            s = (s.reshape(tile_heads, tokens, chunk) + bias[...][None]).reshape(rows, chunk)
            before = top[part, :]
            now = jnp.maximum(before, jnp.max(s, axis=1, keepdims=True))
            shrink = jnp.exp2((before - now) * exponent_scale)
            expo = jnp.exp2((s - over_lanes(now, chunk)) * exponent_scale)
            top[part, :] = now
            summed = total[part, :] * shrink
            for c in range(0, chunk, LANES):
                summed = summed + expo[:, c : c + LANES]
            total[part, :] = summed
            acc[part, :] = acc[part, :] * over_lanes(shrink, kv_rank) + jnp.dot(
                expo.astype(jnp.bfloat16),
                held[side].reshape(chunk, width)[:, :kv_rank],
                preferred_element_type=jnp.float32,
            )

    @pl.loop(0, 2 * half + 3)
    def _(i):
        for s in range(half + 1):

            @pl.when(i == max(2 * s - 1, 0))
            def _():
                point(s)

            @pl.when(i == 2 * s)
            def _():
                from_sibling(s)

        back = i // 2
        last_step = i == 2 * half + 2
        side = jnp.where(last_step, 1, i % 2)
        plane = lax.rem(z - back + z_count, z_count)
        reached = (section == 0) & (z >= back)
        reached = reached & (jnp.logical_not(last_step) | (at_block == 0))

        def load(part):
            here = keys.at[plane, pl.ds(part * (y_count // 2), y_count // 2)]
            return pltpu.make_async_copy(here, held.at[part], held_sems.at[part])

        @pl.when(reached & (i % 2 == 0) & jnp.logical_not(last_step))
        def _():
            load(0).start()
            load(1).start()

        @pl.when(reached & last_step)
        def _():
            load(1).start()

        @pl.when(reached)
        def _():
            load(side).wait()

        needed = reached & ((i != 1) | (at_block >= plane_blocks // 2))
        needed = needed & ((i != 2 * half) | (at_block <= plane_blocks // 2))

        @pl.when(needed)
        def _():
            fold((z - back) * plane_keys + side * chunk, side)

    @pl.when(section == 0)
    def _():
        @pl.loop(0, heads)
        def _(head):
            part = pl.ds(pl.multiple_of(head * tokens, tokens), tokens)
            norm = 1.0 / jnp.sum(total[part, :], axis=1, keepdims=True)
            q[head, :, :kv_rank] = (acc[part, :] * norm).astype(jnp.bfloat16)

        done = pltpu.make_async_copy(q.at[:, :, pl.ds(0, kv_rank)], latent_out, out_sems.at[1])
        done.start()
        done.wait()
        for copy in x_copies():
            copy.wait_send()

    @pl.when(section == 1)
    def _():
        pltpu.make_async_copy(q, q_out, out_sems.at[0]).wait()

    @pl.when(core == 0)
    def _():
        for copy in a_went:
            copy().wait_send()

    @pl.when(core == 1)
    def _():
        for copy in b_went:
            copy().wait_send()

    arrive(own_out.at[1 - core], own_sems.at[2])
    own_away().wait_send()
    own_local().wait()


def prefill_part(own, q_nope, q_rope, up_key, lengths, seq_count, exponent_scale):
    rows, width = own.shape
    heads, tokens, _ = q_nope.shape
    kv_rank = up_key.shape[1]
    y_count = 4
    z_count = seq_count // (2 * y_count)
    dma = pltpu.SemaphoreType.DMA
    bf16 = own.dtype
    chunk = y_count * tokens
    vmem = pl.BlockSpec(memory_space=pltpu.VMEM)
    hbm = pl.BlockSpec(memory_space=pl.ANY)
    return pl.pallas_call(
        functools.partial(prefill_kernel, z_count, y_count, kv_rank, exponent_scale),
        out_shape=[
            jax.ShapeDtypeStruct((z_count, y_count, 2, 2, rows, width), bf16),
            jax.ShapeDtypeStruct((2, rows, width), bf16),
            jax.ShapeDtypeStruct((heads, tokens, width), bf16),
            jax.ShapeDtypeStruct((heads, tokens, kv_rank), bf16),
        ],
        in_specs=[vmem, hbm, vmem, hbm, vmem],
        out_specs=[hbm] * 4,
        scratch_shapes=[
            pltpu.VMEM((rows, width), bf16),
            pltpu.VMEM(q_nope.shape, bf16),
            pltpu.VMEM(up_key.shape, bf16),
            pltpu.VMEM((heads, tokens, width), bf16),
            pltpu.VMEM((heads * tokens, kv_rank), jnp.float32),
            pltpu.VMEM((heads * tokens, LANES), jnp.float32),
            pltpu.VMEM((heads * tokens, LANES), jnp.float32),
            pltpu.VMEM((2, y_count // 2, 2, 2, rows, width), bf16),
            pltpu.VMEM((tokens, chunk), jnp.float32),
            dma((2,)),
            dma((2,)),
            dma((2,)),
            dma((4,)),
            dma((2,)),
            dma((3,)),
            dma((2, z_count // 2)),
            dma((2, z_count // 2)),
            dma((z_count, 4)),
            dma((z_count, 4)),
            dma((z_count,)),
            dma((z_count,)),
        ],
        compiler_params=pltpu.CompilerParams(
            collective_id=0, has_side_effects=True, vmem_limit_bytes=56 << 20
        ),
    )(own, q_nope, q_rope, up_key, lengths)


def over_lanes(value, width):
    return jnp.concatenate([value] * (width // LANES), axis=1)


def decode_kernel(
    kv_rank,
    groups,
    exponent_scale,
    lengths,
    table,
    q_ref,
    keys,
    own_keys,
    _,
    out_ref,
    acc,
    top,
    total,
    held,
    ready,
    sems,
    out_sem,
):
    band = pl.program_id(0)
    heads, tokens, width = q_ref.shape
    rows = heads * tokens
    all_keys = keys.shape[0]
    nt = (((1,), (1,)), ((), ()))

    @pl.when(lax.axis_index("section") == 1)
    def _():
        prompt = table[lax.axis_index("seq") * pl.num_programs(0) + band] // groups
        low = lax.fori_loop(0, prompt, lambda k, at: at + lengths[k], jnp.int32(0))
        last = low + lengths[prompt]
        first = low // 16 * 16
        chunks = (last - first + KEY_BLOCK - 1) // KEY_BLOCK

        def chunk_at(i):
            return pl.multiple_of(jnp.minimum(first + i * KEY_BLOCK, all_keys - KEY_BLOCK), 16)

        def fetch(i):
            slot = lax.rem(i, 2)
            return pltpu.make_async_copy(
                keys.at[pl.ds(chunk_at(i), KEY_BLOCK), :], held.at[slot], sems.at[slot]
            )

        fetch(0).start()

        q = q_ref[...].reshape(rows, width)
        own = own_keys[...]
        scores = lax.dot_general(q, own, nt, preferred_element_type=jnp.float32)
        asked = lax.broadcasted_iota(jnp.int32, (tokens, tokens), 0)
        key = lax.broadcasted_iota(jnp.int32, (tokens, tokens), 1)
        seen = (asked % SAMPLES == key % SAMPLES) & (key // SAMPLES <= asked // SAMPLES)
        bias = jnp.where(seen, 0.0, masked_low)
        bias = jnp.broadcast_to(bias[None], (heads, tokens, tokens)).reshape(rows, tokens)
        scores = scores + bias
        own_top = jnp.max(scores, axis=1, keepdims=True)
        expo = jnp.exp2((scores - own_top) * exponent_scale)
        lane = lax.broadcasted_iota(jnp.int32, (rows, LANES), 1)
        total[...] = jnp.where(lane == 0, jnp.sum(expo, axis=1, keepdims=True), 0.0)
        top[...] = jnp.broadcast_to(own_top, (rows, LANES))
        acc[...] = jnp.dot(
            expo.astype(jnp.bfloat16), own[:, :kv_rank], preferred_element_type=jnp.float32
        )

        def fold(key_block, low_spot, at):
            count = key_block.shape[0]
            s = lax.dot_general(q, key_block, nt, preferred_element_type=jnp.float32)
            if low_spot is not None:
                spot = at + lax.broadcasted_iota(jnp.int32, (1, count), 1)
                here = (spot >= jnp.maximum(low, low_spot)) & (spot < last)
                s = s + jnp.where(here, 0.0, masked_low)
            before = top[...]
            now = jnp.maximum(before, jnp.max(s, axis=1, keepdims=True))
            shrink = jnp.exp2((before - now) * exponent_scale)
            expo = jnp.exp2((s - over_lanes(now, count)) * exponent_scale)
            top[...] = now
            summed = total[...] * shrink
            for c in range(0, count, LANES):
                summed = summed + expo[:, c : c + LANES]
            total[...] = summed
            acc[...] = acc[...] * over_lanes(shrink, kv_rank) + jnp.dot(
                expo.astype(jnp.bfloat16),
                key_block[:, :kv_rank],
                preferred_element_type=jnp.float32,
            )

        @pl.loop(0, chunks)
        def _(i):
            slot = lax.rem(i, 2)
            fetch(i).wait()

            @pl.when(i + 1 < chunks)
            def _():
                fetch(i + 1).start()

            nominal = first + i * KEY_BLOCK
            at = chunk_at(i)
            whole = (nominal >= low) & (nominal + KEY_BLOCK <= last)

            @pl.when(whole)
            def _():
                fold(held[slot], None, None)

            @pl.when(jnp.logical_not(whole))
            def _():
                skip = (nominal - at) // EDGE_BLOCK

                @pl.loop(skip, (jnp.minimum(last - at, KEY_BLOCK) + EDGE_BLOCK - 1) // EDGE_BLOCK)
                def _(j):
                    here = pl.multiple_of(j * EDGE_BLOCK, EDGE_BLOCK)
                    fold(held[slot, pl.ds(here, EDGE_BLOCK), :], nominal, at + here)

        norm = 1.0 / jnp.sum(total[...], axis=1, keepdims=True)
        ready[...] = (acc[...] * norm).astype(jnp.bfloat16).reshape(heads, tokens, kv_rank)
        spot = pl.ds(pl.multiple_of(band * tokens, tokens), tokens)
        done = pltpu.make_async_copy(ready, out_ref.at[:, spot, :], out_sem)
        done.start()
        done.wait()


def shards(query_nope, query_rope, latent, up_key, value_up_weight, lengths, owner_request_table):
    seq_count = lax.axis_size("seq")
    tok_dev, head_dev, nope_dim = query_nope.shape[1:]
    rope_dim = query_rope.shape[2] // head_dev
    kv_rank = up_key.shape[1]
    width = kv_rank + rope_dim
    req_dev = owner_request_table.shape[0] // seq_count
    groups = owner_request_table.shape[0] // lengths.shape[0]
    band_tokens = tok_dev // req_dev
    exponent_scale = math.log2(math.e) / math.sqrt(nope_dim + rope_dim)

    keys, pair, queries, latent_out = prefill_part(
        latent[0],
        query_nope[0].swapaxes(0, 1),
        query_rope[0],
        up_key,
        lengths[:, None],
        seq_count,
        exponent_scale,
    )
    rows = head_dev * band_tokens
    latent_out = pl.pallas_call(
        functools.partial(decode_kernel, kv_rank, groups, exponent_scale),
        out_shape=jax.ShapeDtypeStruct((head_dev, tok_dev, kv_rank), jnp.bfloat16),
        grid_spec=pltpu.PrefetchScalarGridSpec(
            num_scalar_prefetch=2,
            grid=(req_dev,),
            in_specs=[
                pl.BlockSpec((head_dev, band_tokens, width), lambda i, *_: (0, i, 0)),
                pl.BlockSpec(memory_space=pl.ANY),
                pl.BlockSpec((band_tokens, width), lambda i, *_: (i, 0)),
                pl.BlockSpec(memory_space=pl.ANY),
            ],
            out_specs=pl.BlockSpec(memory_space=pl.ANY),
            scratch_shapes=[
                pltpu.VMEM((rows, kv_rank), jnp.float32),
                pltpu.VMEM((rows, LANES), jnp.float32),
                pltpu.VMEM((rows, LANES), jnp.float32),
                pltpu.VMEM((2, KEY_BLOCK, width), jnp.bfloat16),
                pltpu.VMEM((head_dev, band_tokens, kv_rank), jnp.bfloat16),
                pltpu.SemaphoreType.DMA((2,)),
                pltpu.SemaphoreType.DMA,
            ],
        ),
        input_output_aliases={5: 0},
        compiler_params=pltpu.CompilerParams(vmem_limit_bytes=48 << 20),
    )(
        lengths,
        owner_request_table,
        queries,
        keys.reshape(-1, width),
        pair.reshape(-1, width),
        latent_out,
    )

    attended = jnp.einsum(
        "htk,hkv->thv", latent_out, value_up_weight, preferred_element_type=jnp.float32
    )
    return attended.astype(jnp.bfloat16)[None]


def solution(mesh):
    in_specs = (
        P("section", "seq", "head", None),
        P("section", "seq", "head"),
        P("section", ("seq", "head"), None),
        P("head", None, None),
        P("head", None, None),
        P(),
        P(),
    )
    out_specs = P("section", "seq", "head", None)
    return jax.shard_map(shards, mesh=mesh, in_specs=in_specs, out_specs=out_specs, check_vma=False)
```

```python
import functools
import math

import jax
import jax.numpy as jnp
from jax import lax
from jax.experimental import pallas as pl
from jax.experimental.pallas import tpu as pltpu
from jax.sharding import PartitionSpec as P

SAMPLES = 8
STEPS = 4
BLOCK = 64

scale_top = 448.0
tiny_eps = 1e-06
masked_low = -1e30

KEY_BLOCK = 1024
EDGE_BLOCK = 512
LANES = 128


def prefill_kernel(
    z_count, y_count, kv_rank, exponent_scale, own_in, q_nope, q_rope, up_key, lengths,
    keys, own_out, q_out, latent_out, block, nope, up, q, acc, top, total, held, bias,
    in_sems, out_sems, held_sems, x_send, x_recv, own_sems,
    z_send, z_recv, y_send, y_recv, sib_send, sib_recv,
):
    section = lax.axis_index("section")
    seq = lax.axis_index("seq")
    core = lax.axis_index("head")
    z = seq // (2 * y_count)
    y = seq // 2 % y_count
    hi = seq % 2
    half = z_count // 2
    heads, tokens, width = q.shape
    plane_blocks = 2 * y_count
    at_block = seq % plane_blocks
    plane_keys = plane_blocks * tokens
    nt = (((1,), (1,)), ((), ()))

    def plane_at(dz):
        return lax.rem(z + dz + z_count, z_count)

    def row_at(dy):
        return lax.rem(y + dy + y_count, y_count)

    def device(dz=0, dy=0, to_hi=None, to_section=None, to_core=None):
        th = hi if to_hi is None else to_hi
        return (
            section if to_section is None else to_section,
            (plane_at(dz) * y_count + row_at(dy)) * 2 + th,
            core if to_core is None else to_core,
        )

    loads = [
        pltpu.make_async_copy(q_nope, nope, in_sems.at[0]),
        pltpu.make_async_copy(up_key, up, in_sems.at[1]),
    ]
    for load in loads:
        load.start()

    barrier = pltpu.get_barrier_semaphore()
    peers = [
        device(to_core=1 - core),
        device(to_section=1 - section),
        device(to_hi=1 - hi),
        device(to_section=1 - section, to_hi=1 - hi),
        device(dz=1),
        device(dz=-1),
        device(dy=1),
        device(dy=-1),
    ]
    for peer in peers:
        pl.semaphore_signal(barrier, inc=1, device_id=peer, device_id_type=pl.DeviceIdType.MESH)

    @pl.when(section == 0)
    def _():
        rows = own_in[...].astype(jnp.float32)
        largest = jnp.max(jnp.abs(rows))
        spread = jnp.full((8, LANES), largest, jnp.float32)
        scale = ((spread + tiny_eps) / scale_top).astype(jnp.bfloat16).astype(jnp.float32)
        factor = scale[:1, :1]
        stored = (rows / factor).astype(jnp.bfloat16)
        block[...] = (stored.astype(jnp.float32) * factor).astype(jnp.bfloat16)

    @pl.when(section == 1)
    def _():
        block[...] = own_in[...]

    pl.semaphore_wait(barrier, len(peers))

    def remote(src, dst, to, send_sem, recv_sem):
        return pltpu.make_async_remote_copy(
            src_ref=src,
            dst_ref=dst,
            send_sem=send_sem,
            recv_sem=recv_sem,
            device_id=to,
            device_id_type=pl.DeviceIdType.MESH,
        )

    def arrive(dst, recv_sem):
        remote(dst, dst, device(to_core=1 - core), recv_sem, recv_sem).wait_recv()

    def own_local():
        return pltpu.make_async_copy(block, own_out.at[core], own_sems.at[0])

    def own_away():
        to = device(to_core=1 - core)
        return remote(block, own_out.at[core], to, own_sems.at[1], own_sems.at[2])

    def x_copies():
        spot = keys.at[z, y, hi, core]
        return [
            remote(block, spot, device(to_section=1), x_send.at[0], x_recv.at[0]),
            remote(block, spot, device(to_hi=1 - hi), x_send.at[2], x_recv.at[1]),
            remote(block, spot, device(to_section=1, to_hi=1 - hi), x_send.at[1], x_recv.at[1]),
        ]

    def x_local():
        return pltpu.make_async_copy(block, keys.at[z, y, hi, core], x_send.at[3])

    @pl.when(section == 0)
    def _():
        x_local().start()
        for copy in x_copies():
            copy.start()

    own_local().start()
    own_away().start()

    for load in loads:
        load.wait()

    @pl.loop(0, heads // 2)
    def _(pair):
        rope = q_rope[:, pl.ds(pl.multiple_of(pair * LANES, LANES), LANES)]
        for side in range(2):
            head = pair * 2 + side
            lifted = lax.dot_general(nope[head], up[head], nt, preferred_element_type=jnp.float32)
            q[head, :, :kv_rank] = lifted.astype(jnp.bfloat16)
            q[head, :, kv_rank:] = rope[:, side * (LANES // 2) : (side + 1) * (LANES // 2)]

    @pl.when(section == 1)
    def _():
        pltpu.make_async_copy(q, q_out, out_sems.at[0]).start()

    @pl.when(section == 0)
    def _():
        x_local().wait()
        arrive(keys.at[z, y, 1 - hi, core], x_recv.at[1])

    @pl.when(section == 1)
    def _():
        arrive(keys.at[z, y, hi, core], x_recv.at[0])
        arrive(keys.at[z, y, 1 - hi, core], x_recv.at[1])

    low, high, far = row_at(-1), row_at(1), row_at(2)
    columns = [y, low, high, far]
    planes = [z]
    for s in range(1, half):
        planes += [plane_at(-s), plane_at(s)]
    planes.append(plane_at(half))
    steps = [[0]] + [[2 * s - 1, 2 * s] for s in range(1, half)] + [[z_count - 1]]

    def sender(went):
        def send(src, to, send_sem, recv_sem):
            copy = lambda: remote(src(), src(), to(), send_sem(), recv_sem())
            went.append(copy)
            copy().start()

        return send

    went = {(section_of, core_of): [] for section_of in range(2) for core_of in range(2)}

    def along_y(send, n, c, src, d, k):
        send(src, lambda: device(dy=d), lambda: y_send.at[n, k], lambda: y_recv.at[n, k])

    def spread(send, n, c):
        mine = lambda: keys.at[planes[n], y, :, c]
        along_y(send, n, c, mine, 1, 0)
        along_y(send, n, c, mine, -1, 1)

    def spread_on(send, n, c):
        arrive(keys.at[planes[n], low, :, c], y_recv.at[n, 0])
        along_y(send, n, c, lambda: keys.at[planes[n], low, 0, c], 1, 2)
        arrive(keys.at[planes[n], high, :, c], y_recv.at[n, 1])
        along_y(send, n, c, lambda: keys.at[planes[n], high, 1, c], -1, 3)

    def spread_end(n, c):
        arrive(keys.at[planes[n], far, 0, c], y_recv.at[n, 2])
        arrive(keys.at[planes[n], far, 1, c], y_recv.at[n, 3])

    def to_sibling(send, n, c):
        send(
            lambda: keys.at[planes[n], :, :, c],
            lambda: device(to_core=1 - c),
            lambda: sib_send.at[n],
            lambda: sib_recv.at[n],
        )

    def along_z(send, src, up_way, step, k):
        d, j = (1, 0) if up_way else (-1, 1)
        send(
            src,
            lambda: device(dz=d),
            lambda: z_send.at[j, step, k],
            lambda: z_recv.at[j, step, k],
        )

    def decode_a():
        send = sender(went[1, 0])
        ways = ((0, True), (1, False))

        def cell(n, k):
            return lambda: keys.at[planes[n], columns[k], :, 0]

        def column(k):
            for _, up_way in ways:
                along_z(send, cell(0, k), up_way, 0, k)

        spread(send, 0, 0)
        column(0)
        arrive(keys.at[z, low, :, 0], y_recv.at[0, 0])
        along_y(send, 0, 0, lambda: keys.at[z, low, 0, 0], 1, 2)
        column(1)
        arrive(keys.at[z, high, :, 0], y_recv.at[0, 1])
        along_y(send, 0, 0, lambda: keys.at[z, high, 1, 0], -1, 3)
        column(2)
        spread_end(0, 0)
        column(3)
        to_sibling(send, 0, 0)
        for s in range(1, half):
            for k in range(y_count):
                for n, (j, up_way) in zip(steps[s], ways):
                    arrive(cell(n, k)(), z_recv.at[j, s - 1, k])
                    if s < half - 1 or k // 2 == j:
                        along_z(send, cell(n, k), up_way, s, k)
            for n in steps[s]:
                to_sibling(send, n, 0)
        for k in range(y_count):
            arrive(cell(z_count - 1, k)(), z_recv.at[k // 2, half - 1, k])
        to_sibling(send, z_count - 1, 0)

    def decode_b():
        send = sender(went[1, 1])
        ways = ((0, True), (1, False))

        def ahead(n, s, j, up_way):
            if s < half - 1:
                part = lambda: keys.at[planes[n], y, :, 1]
            else:
                part = lambda: keys.at[planes[n], y, j, 1]
            along_z(send, part, up_way, s, 0)

        for j, up_way in ways:
            ahead(0, 0, j, up_way)
        spread(send, 0, 1)
        for s in range(1, half):
            for n, (j, up_way) in zip(steps[s], ways):
                arrive(keys.at[planes[n], y, :, 1], z_recv.at[j, s - 1, 0])
                ahead(n, s, j, up_way)
                spread(send, n, 1)
            if s == 1:
                spread_on(send, 0, 1)
        for j in range(2):
            arrive(keys.at[planes[-1], y, j, 1], z_recv.at[j, half - 1, 0])
        spread(send, z_count - 1, 1)
        for n in range(z_count):
            if n >= 1:
                spread_on(send, n, 1)
                spread_end(n - 1, 1)
                to_sibling(send, n - 1, 1)
        spread_end(z_count - 1, 1)
        to_sibling(send, z_count - 1, 1)

    behind = [0] + [2 * s - 1 for s in range(1, half)] + [z_count - 1]
    past = planes[2 * (half - 1)]

    def prefill_a_start():
        send = sender(went[0, 0])
        spread(send, 0, 0)
        spread_on(send, 0, 0)
        spread_end(0, 0)
        along_z(send, lambda: keys.at[z, :, :, 0], True, 0, 0)
        to_sibling(send, 0, 0)

    def prefill_a(s):
        send = sender(went[0, 0])
        n = behind[s]
        arrive(keys.at[planes[n], :, :, 0], z_recv.at[0, s - 1, 0])
        if s < half:
            along_z(send, lambda: keys.at[planes[n], :, :, 0], True, s, 0)
        else:
            along_z(send, lambda: keys.at[planes[n], y_count - 1, 1, 0], True, 0, 1)
        to_sibling(send, n, 0)

    def prefill_a_end():
        send = sender(went[0, 0])
        spot = lambda: keys.at[past, y_count - 1, 1, 0]
        arrive(spot(), z_recv.at[0, 0, 1])
        send(
            spot,
            lambda: device(to_core=1),
            lambda: sib_send.at[2 * (half - 1)],
            lambda: sib_recv.at[2 * (half - 1)],
        )

    def prefill_b_start():
        send = sender(went[0, 1])
        along_z(send, lambda: keys.at[z, y, :, 1], True, 0, 0)
        spread(send, 0, 1)
        spread_on(send, 0, 1)
        spread_end(0, 1)
        to_sibling(send, 0, 1)

    def prefill_b_chain(s):
        send = sender(went[0, 1])
        n = behind[s]
        arrive(keys.at[planes[n], y, :, 1], z_recv.at[0, s - 1, 0])
        if s < half:
            along_z(send, lambda: keys.at[planes[n], y, :, 1], True, s, 0)
        else:
            along_z(send, lambda: keys.at[planes[n], y, 1, 1], True, 0, 1)
        spread(send, n, 1)

    def prefill_b_on(s):
        spread_on(sender(went[0, 1]), behind[s], 1)

    def prefill_b_end(s):
        spread_end(behind[s], 1)
        to_sibling(sender(went[0, 1]), behind[s], 1)

    def prefill_b_past():
        arrive(keys.at[past, y, 1, 1], z_recv.at[0, 0, 1])
        n = 2 * (half - 1)
        along_y(sender(went[0, 1]), n, 1, lambda: keys.at[past, y, 1, 1], 1, 0)

    def prefill_b_past_end():
        n = 2 * (half - 1)
        spot = lambda: keys.at[past, low, 1, 1]
        arrive(spot(), y_recv.at[n, 0])
        sender(went[0, 1])(
            spot, lambda: device(to_core=0), lambda: sib_send.at[n], lambda: sib_recv.at[n]
        )

    def from_sibling(n):
        arrive(keys.at[planes[n], :, :, 1 - core], sib_recv.at[n])

    def past_from_sibling():
        n = 2 * (half - 1)

        @pl.when(core == 0)
        def _():
            arrive(keys.at[past, low, 1, 1], sib_recv.at[n])

        @pl.when(core == 1)
        def _():
            arrive(keys.at[past, y_count - 1, 1, 0], sib_recv.at[n])

    def on_core(at, c, *events):
        @pl.when((core == c) if at is True else (at & (core == c)))
        def _():
            for event in events:
                event()

    @pl.when(section == 1)
    def _():
        on_core(True, 0, decode_a)
        on_core(True, 1, decode_b)
        for n in range(z_count):
            from_sibling(n)

    @pl.when(section == 0)
    def _():
        top[...] = jnp.full(top.shape, masked_low, jnp.float32)
        total[...] = jnp.zeros(total.shape, jnp.float32)
        acc[...] = jnp.zeros(acc.shape, jnp.float32)

    token = lax.broadcasted_iota(jnp.int32, (tokens, 1), 0)
    position = seq * tokens + token
    count = lengths.shape[1]
    before_it = lax.broadcasted_iota(jnp.int32, (count, count), 0) < lax.broadcasted_iota(
        jnp.int32, (count, count), 1
    )
    earlier = jnp.where(before_it, 1.0, 0.0).astype(jnp.bfloat16)
    wide = jnp.broadcast_to(lengths[...], (8, count))
    digits = [(wide // 64).astype(jnp.bfloat16), (wide % 64).astype(jnp.bfloat16)]
    upper, lower = [jnp.dot(d, earlier, preferred_element_type=jnp.float32) for d in digits]
    starts = (upper * 64.0 + lower)[:1]
    row_low = jnp.max(
        jnp.where(starts <= position.astype(jnp.float32), starts, 0.0), axis=1, keepdims=True
    ).astype(jnp.int32)

    chunk = plane_keys // 2
    tile_heads = 8
    rows = tile_heads * tokens
    tiles = heads // tile_heads

    def fold(tile, key_block):
        count = key_block.shape[0]
        part = pl.ds(pl.multiple_of(tile * rows, rows), rows)
        asked = q[pl.ds(tile * tile_heads, tile_heads)].reshape(rows, width)
        s = lax.dot_general(asked, key_block, nt, preferred_element_type=jnp.float32)
        s = (s.reshape(tile_heads, tokens, count) + bias[:, :count][None]).reshape(rows, count)
        before = top[part, :]
        now = jnp.maximum(before, jnp.max(s, axis=1, keepdims=True))
        shrink = jnp.exp2((before - now) * exponent_scale)
        expo = jnp.exp2((s - over_lanes(now, count)) * exponent_scale)
        top[part, :] = now
        summed = total[part, :] * shrink
        for c in range(0, count, LANES):
            summed = summed + expo[:, c : c + LANES]
        total[part, :] = summed
        acc[part, :] = acc[part, :] * over_lanes(shrink, kv_rank) + jnp.dot(
            expo.astype(jnp.bfloat16),
            key_block[:, :kv_rank],
            preferred_element_type=jnp.float32,
        )

    def hide(first_spot, count):
        spot = first_spot + lax.broadcasted_iota(jnp.int32, (1, count), 1)
        seen = (spot >= row_low) & (spot <= position)
        bias[:, :count] = jnp.where(seen, 0.0, masked_low)

    last_step = 4 * (half + 1)

    @pl.when(section == 0)
    def _():
        @pl.loop(0, last_step + 1)
        def _(step):
            on_core(step == 0, 0, prefill_a_start)
            on_core(step == 0, 1, prefill_b_start)
            for s in range(1, half + 1):
                on_core(step == 4 * s - 1, 0, functools.partial(prefill_a, s))
                on_core(step == 4 * s - 3, 1, functools.partial(prefill_b_chain, s))
                on_core(step == 4 * s - 2, 1, functools.partial(prefill_b_on, s))
                on_core(step == 4 * s - 1, 1, functools.partial(prefill_b_end, s))
            on_core(step == last_step - 1, 0, prefill_a_end)
            on_core(step == last_step - 2, 1, prefill_b_past)
            on_core(step == last_step - 1, 1, prefill_b_past_end)
            for s in range(half + 1):

                @pl.when(step == 4 * s)
                def _():
                    from_sibling(behind[s])

            @pl.when(step == last_step)
            def _():
                past_from_sibling()

            back = step // 4
            side = step // 2 % 2
            turn = step % 2
            is_last = step == last_step
            plane = lax.rem(z - back + z_count, z_count)
            reached = (z >= back) & jnp.logical_not(is_last)

            def load(part):
                here = keys.at[plane, pl.ds(part * (y_count // 2), y_count // 2)]
                return pltpu.make_async_copy(here, held.at[part], held_sems.at[part])

            def load_past():
                return pltpu.make_async_copy(
                    keys.at[past, y_count - 1, 1], held.at[0, 0, 0], held_sems.at[0]
                )

            @pl.when(reached & (step % 4 == 0))
            def _():
                load(0).start()
                load(1).start()

            @pl.when(reached & (turn == 0))
            def _():
                load(side).wait()

            mid = plane_blocks // 2
            rim_own = (back == 0) & (side == 1)
            rim_far = (back == half) & (side == 0)
            few = (rim_own | rim_far) & (at_block == mid)
            none = (rim_own & (at_block < mid)) | (rim_far & (at_block > mid))
            first_spot = (z - back) * plane_keys + side * chunk
            few_spot = jnp.where(rim_far, first_spot + chunk - tokens, first_spot)

            @pl.when(reached & jnp.logical_not(few | none))
            def _():
                @pl.when(turn == 0)
                def _():
                    hide(first_spot, chunk)

                @pl.loop(0, tiles // 2)
                def _(tile):
                    fold(turn * (tiles // 2) + tile, held[side].reshape(chunk, width))

            edge = (z > half) & is_last & (at_block == 0)

            @pl.when(edge)
            def _():
                load_past().start()
                load_past().wait()

            @pl.when(edge | (reached & few & (turn == 0)))
            def _():
                hide(jnp.where(is_last, first_spot + plane_keys - tokens, few_spot), tokens)
                spot = jnp.where(rim_far, y_count - 1, 0)
                block_keys = held[
                    jnp.where(is_last, 0, side), spot // 2, spot % 2
                ].reshape(tokens, width)

                @pl.loop(0, tiles)
                def _(tile):
                    fold(tile, block_keys)

    @pl.when(section == 0)
    def _():
        @pl.loop(0, heads)
        def _(head):
            part = pl.ds(pl.multiple_of(head * tokens, tokens), tokens)
            norm = 1.0 / jnp.sum(total[part, :], axis=1, keepdims=True)
            q[head, :, :kv_rank] = (acc[part, :] * norm).astype(jnp.bfloat16)

        done = pltpu.make_async_copy(q.at[:, :, pl.ds(0, kv_rank)], latent_out, out_sems.at[1])
        done.start()
        done.wait()
        for copy in x_copies():
            copy.wait_send()

    @pl.when(section == 1)
    def _():
        pltpu.make_async_copy(q, q_out, out_sems.at[0]).wait()

    for (section_of, core_of), copies in went.items():

        @pl.when((section == section_of) & (core == core_of))
        def _():
            for copy in copies:
                copy().wait_send()

    arrive(own_out.at[1 - core], own_sems.at[2])
    own_away().wait_send()
    own_local().wait()


def prefill_part(own, q_nope, q_rope, up_key, lengths, seq_count, exponent_scale):
    rows, width = own.shape
    heads, tokens, _ = q_nope.shape
    kv_rank = up_key.shape[1]
    y_count = 4
    z_count = seq_count // (2 * y_count)
    dma = pltpu.SemaphoreType.DMA
    bf16 = own.dtype
    chunk = y_count * tokens
    vmem = pl.BlockSpec(memory_space=pltpu.VMEM)
    hbm = pl.BlockSpec(memory_space=pl.ANY)
    return pl.pallas_call(
        functools.partial(prefill_kernel, z_count, y_count, kv_rank, exponent_scale),
        out_shape=[
            jax.ShapeDtypeStruct((z_count, y_count, 2, 2, rows, width), bf16),
            jax.ShapeDtypeStruct((2, rows, width), bf16),
            jax.ShapeDtypeStruct((heads, tokens, width), bf16),
            jax.ShapeDtypeStruct((heads, tokens, kv_rank), bf16),
        ],
        in_specs=[vmem, hbm, vmem, hbm, vmem],
        out_specs=[hbm] * 4,
        scratch_shapes=[
            pltpu.VMEM((rows, width), bf16),
            pltpu.VMEM(q_nope.shape, bf16),
            pltpu.VMEM(up_key.shape, bf16),
            pltpu.VMEM((heads, tokens, width), bf16),
            pltpu.VMEM((heads * tokens, kv_rank), jnp.float32),
            pltpu.VMEM((heads * tokens, LANES), jnp.float32),
            pltpu.VMEM((heads * tokens, LANES), jnp.float32),
            pltpu.VMEM((2, y_count // 2, 2, 2, rows, width), bf16),
            pltpu.VMEM((tokens, chunk), jnp.float32),
            dma((2,)),
            dma((2,)),
            dma((2,)),
            dma((4,)),
            dma((2,)),
            dma((3,)),
            dma((2, z_count // 2, y_count)),
            dma((2, z_count // 2, y_count)),
            dma((z_count, 4)),
            dma((z_count, 4)),
            dma((z_count,)),
            dma((z_count,)),
        ],
        compiler_params=pltpu.CompilerParams(
            collective_id=0, has_side_effects=True, vmem_limit_bytes=56 << 20
        ),
    )(own, q_nope, q_rope, up_key, lengths)


def over_lanes(value, width):
    return jnp.concatenate([value] * (width // LANES), axis=1)


def decode_kernel(
    kv_rank,
    groups,
    exponent_scale,
    lengths,
    table,
    q_ref,
    keys,
    own_keys,
    _,
    out_ref,
    acc,
    top,
    total,
    held,
    ready,
    q_held,
    sems,
    q_sems,
    out_sems,
):
    band = pl.program_id(0)
    bands = pl.num_programs(0)
    _, heads, tokens, width = q_held.shape
    rows = heads * tokens
    all_keys = keys.shape[0]
    nt = (((1,), (1,)), ((), ()))

    @pl.when(lax.axis_index("section") == 1)
    def _():
        def prompt_range(which):
            prompt = table[lax.axis_index("seq") * bands + which] // groups
            low = lax.fori_loop(0, prompt, lambda k, at: at + lengths[k], jnp.int32(0))
            return low, low + lengths[prompt]

        def chunk_at(start, i):
            return pl.multiple_of(jnp.minimum(start + i * KEY_BLOCK, all_keys - KEY_BLOCK), 16)

        def fetch_from(start, i, slot):
            return pltpu.make_async_copy(
                keys.at[pl.ds(chunk_at(start, i), KEY_BLOCK), :], held.at[slot], sems.at[slot]
            )

        def band_rows(which):
            return pl.ds(pl.multiple_of(which * tokens, tokens), tokens)

        def fetch_q(which):
            slot = lax.rem(which, 2)
            return pltpu.make_async_copy(
                q_ref.at[:, band_rows(which), :], q_held.at[slot], q_sems.at[slot]
            )

        def leave(which):
            slot = lax.rem(which, 2)
            return pltpu.make_async_copy(
                ready.at[slot], out_ref.at[:, band_rows(which), :], out_sems.at[slot]
            )

        low, last = prompt_range(band)
        first = low // 16 * 16
        chunks = (last - first + KEY_BLOCK - 1) // KEY_BLOCK

        def fetch(i):
            slot = jnp.where(i == 0, lax.rem(band, 2), 2 + lax.rem(i, 2))
            return fetch_from(first, i, slot)

        @pl.when(band == 0)
        def _():
            fetch_q(0).start()
            fetch(0).start()

        @pl.when(band + 1 < bands)
        def _():
            fetch_q(band + 1).start()
            next_low, _ = prompt_range(band + 1)
            fetch_from(next_low // 16 * 16, 0, lax.rem(band + 1, 2)).start()

        fetch_q(band).wait()
        q = q_held[lax.rem(band, 2)].reshape(rows, width)
        own = own_keys[...]
        scores = lax.dot_general(q, own, nt, preferred_element_type=jnp.float32)
        asked = lax.broadcasted_iota(jnp.int32, (tokens, tokens), 0)
        key = lax.broadcasted_iota(jnp.int32, (tokens, tokens), 1)
        seen = (asked % SAMPLES == key % SAMPLES) & (key // SAMPLES <= asked // SAMPLES)
        bias = jnp.where(seen, 0.0, masked_low)
        bias = jnp.broadcast_to(bias[None], (heads, tokens, tokens)).reshape(rows, tokens)
        scores = scores + bias
        own_top = jnp.max(scores, axis=1, keepdims=True)
        expo = jnp.exp2((scores - own_top) * exponent_scale)
        lane = lax.broadcasted_iota(jnp.int32, (rows, LANES), 1)
        total[...] = jnp.where(lane == 0, jnp.sum(expo, axis=1, keepdims=True), 0.0)
        top[...] = jnp.broadcast_to(own_top, (rows, LANES))
        acc[...] = jnp.dot(
            expo.astype(jnp.bfloat16), own[:, :kv_rank], preferred_element_type=jnp.float32
        )

        def fold(key_block, low_spot, at):
            count = key_block.shape[0]
            s = lax.dot_general(q, key_block, nt, preferred_element_type=jnp.float32)
            if low_spot is not None:
                spot = at + lax.broadcasted_iota(jnp.int32, (1, count), 1)
                here = (spot >= jnp.maximum(low, low_spot)) & (spot < last)
                s = s + jnp.where(here, 0.0, masked_low)
            before = top[...]
            now = jnp.maximum(before, jnp.max(s, axis=1, keepdims=True))
            shrink = jnp.exp2((before - now) * exponent_scale)
            expo = jnp.exp2((s - over_lanes(now, count)) * exponent_scale)
            top[...] = now
            summed = total[...] * shrink
            for c in range(0, count, LANES):
                summed = summed + expo[:, c : c + LANES]
            total[...] = summed
            acc[...] = acc[...] * over_lanes(shrink, kv_rank) + jnp.dot(
                expo.astype(jnp.bfloat16),
                key_block[:, :kv_rank],
                preferred_element_type=jnp.float32,
            )

        @pl.loop(0, chunks)
        def _(i):
            slot = jnp.where(i == 0, lax.rem(band, 2), 2 + lax.rem(i, 2))
            fetch(i).wait()

            @pl.when(i + 1 < chunks)
            def _():
                fetch(i + 1).start()

            nominal = first + i * KEY_BLOCK
            at = chunk_at(first, i)
            whole = (nominal >= low) & (nominal + KEY_BLOCK <= last)

            @pl.when(whole)
            def _():
                fold(held[slot], None, None)

            @pl.when(jnp.logical_not(whole))
            def _():
                skip = (nominal - at) // EDGE_BLOCK

                @pl.loop(skip, (jnp.minimum(last - at, KEY_BLOCK) + EDGE_BLOCK - 1) // EDGE_BLOCK)
                def _(j):
                    here = pl.multiple_of(j * EDGE_BLOCK, EDGE_BLOCK)
                    fold(held[slot, pl.ds(here, EDGE_BLOCK), :], nominal, at + here)

        norm = 1.0 / jnp.sum(total[...], axis=1, keepdims=True)
        @pl.when(band >= 2)
        def _():
            leave(band - 2).wait()

        ready[lax.rem(band, 2)] = (
            (acc[...] * norm).astype(jnp.bfloat16).reshape(heads, tokens, kv_rank)
        )
        leave(band).start()

        @pl.when(band == bands - 1)
        def _():
            leave(band - 1).wait()
            leave(band).wait()


def shards(query_nope, query_rope, latent, up_key, value_up_weight, lengths, owner_request_table):
    seq_count = lax.axis_size("seq")
    tok_dev, head_dev, nope_dim = query_nope.shape[1:]
    rope_dim = query_rope.shape[2] // head_dev
    kv_rank = up_key.shape[1]
    width = kv_rank + rope_dim
    req_dev = owner_request_table.shape[0] // seq_count
    groups = owner_request_table.shape[0] // lengths.shape[0]
    band_tokens = tok_dev // req_dev
    exponent_scale = math.log2(math.e) / math.sqrt(nope_dim + rope_dim)

    keys, pair, queries, latent_out = prefill_part(
        latent[0],
        query_nope[0].swapaxes(0, 1),
        query_rope[0],
        up_key,
        lengths[None, :],
        seq_count,
        exponent_scale,
    )
    rows = head_dev * band_tokens
    latent_out = pl.pallas_call(
        functools.partial(decode_kernel, kv_rank, groups, exponent_scale),
        out_shape=jax.ShapeDtypeStruct((head_dev, tok_dev, kv_rank), jnp.bfloat16),
        grid_spec=pltpu.PrefetchScalarGridSpec(
            num_scalar_prefetch=2,
            grid=(req_dev,),
            in_specs=[
                pl.BlockSpec(memory_space=pl.ANY),
                pl.BlockSpec(memory_space=pl.ANY),
                pl.BlockSpec((band_tokens, width), lambda i, *_: (i, 0)),
                pl.BlockSpec(memory_space=pl.ANY),
            ],
            out_specs=pl.BlockSpec(memory_space=pl.ANY),
            scratch_shapes=[
                pltpu.VMEM((rows, kv_rank), jnp.float32),
                pltpu.VMEM((rows, LANES), jnp.float32),
                pltpu.VMEM((rows, LANES), jnp.float32),
                pltpu.VMEM((4, KEY_BLOCK, width), jnp.bfloat16),
                pltpu.VMEM((2, head_dev, band_tokens, kv_rank), jnp.bfloat16),
                pltpu.VMEM((2, head_dev, band_tokens, width), jnp.bfloat16),
                pltpu.SemaphoreType.DMA((4,)),
                pltpu.SemaphoreType.DMA((2,)),
                pltpu.SemaphoreType.DMA((2,)),
            ],
        ),
        input_output_aliases={5: 0},
        compiler_params=pltpu.CompilerParams(vmem_limit_bytes=58 << 20),
    )(
        lengths,
        owner_request_table,
        queries,
        keys.reshape(-1, width),
        pair.reshape(-1, width),
        latent_out,
    )

    attended = jnp.einsum(
        "htk,hkv->thv", latent_out, value_up_weight, preferred_element_type=jnp.float32
    )
    return attended.astype(jnp.bfloat16)[None]


def solution(mesh):
    in_specs = (
        P("section", "seq", "head", None),
        P("section", "seq", "head"),
        P("section", ("seq", "head"), None),
        P("head", None, None),
        P("head", None, None),
        P(),
        P(),
    )
    out_specs = P("section", "seq", "head", None)
    return jax.shard_map(shards, mesh=mesh, in_specs=in_specs, out_specs=out_specs, check_vma=False)
```

```python
import functools
import math

import jax
import jax.numpy as jnp
from jax import lax
from jax.experimental import pallas as pl
from jax.experimental.pallas import tpu as pltpu
from jax.sharding import PartitionSpec as P

SAMPLES = 8
STEPS = 4
BLOCK = 64

scale_top = 448.0
tiny_eps = 1e-06
masked_low = -1e30

KEY_BLOCK = 1024
EDGE_BLOCK = 512
LANES = 128


def prefill_kernel(
    z_count, y_count, kv_rank, exponent_scale, own_in, q_nope, q_rope, up_key, lengths,
    keys, own_out, q_out, latent_out, block, nope, up, q, acc, top, total, held, bias,
    in_sems, out_sems, held_sems, x_send, x_recv, own_sems,
    z_send, z_recv, y_send, y_recv, sib_send, sib_recv,
):
    section = lax.axis_index("section")
    seq = lax.axis_index("seq")
    core = lax.axis_index("head")
    z = seq // (2 * y_count)
    y = seq // 2 % y_count
    hi = seq % 2
    half = z_count // 2
    heads, tokens, width = q.shape
    plane_blocks = 2 * y_count
    at_block = seq % plane_blocks
    plane_keys = plane_blocks * tokens
    nt = (((1,), (1,)), ((), ()))

    def plane_at(dz):
        return lax.rem(z + dz + z_count, z_count)

    def row_at(dy):
        return lax.rem(y + dy + y_count, y_count)

    def device(dz=0, dy=0, to_hi=None, to_section=None, to_core=None):
        th = hi if to_hi is None else to_hi
        return (
            section if to_section is None else to_section,
            (plane_at(dz) * y_count + row_at(dy)) * 2 + th,
            core if to_core is None else to_core,
        )

    loads = [
        pltpu.make_async_copy(q_nope, nope, in_sems.at[0]),
        pltpu.make_async_copy(up_key, up, in_sems.at[1]),
    ]
    for load in loads:
        load.start()

    barrier = pltpu.get_barrier_semaphore()
    peers = [
        device(to_core=1 - core),
        device(to_section=1 - section),
        device(to_hi=1 - hi),
        device(to_section=1 - section, to_hi=1 - hi),
        device(dz=1),
        device(dz=-1),
        device(dy=1),
        device(dy=-1),
    ]
    for peer in peers:
        pl.semaphore_signal(barrier, inc=1, device_id=peer, device_id_type=pl.DeviceIdType.MESH)

    @pl.when(section == 0)
    def _():
        rows = own_in[...].astype(jnp.float32)
        largest = jnp.max(jnp.abs(rows))
        spread = jnp.full((8, LANES), largest, jnp.float32)
        scale = ((spread + tiny_eps) / scale_top).astype(jnp.bfloat16).astype(jnp.float32)
        factor = scale[:1, :1]
        stored = (rows / factor).astype(jnp.bfloat16)
        block[...] = (stored.astype(jnp.float32) * factor).astype(jnp.bfloat16)

    @pl.when(section == 1)
    def _():
        block[...] = own_in[...]

    pl.semaphore_wait(barrier, len(peers))

    def remote(src, dst, to, send_sem, recv_sem):
        return pltpu.make_async_remote_copy(
            src_ref=src,
            dst_ref=dst,
            send_sem=send_sem,
            recv_sem=recv_sem,
            device_id=to,
            device_id_type=pl.DeviceIdType.MESH,
        )

    def arrive(dst, recv_sem):
        remote(dst, dst, device(to_core=1 - core), recv_sem, recv_sem).wait_recv()

    def own_local():
        return pltpu.make_async_copy(block, own_out.at[core], own_sems.at[0])

    def own_away():
        to = device(to_core=1 - core)
        return remote(block, own_out.at[core], to, own_sems.at[1], own_sems.at[2])

    def x_copies():
        spot = keys.at[z, y, hi, core]
        return [
            remote(block, spot, device(to_section=1), x_send.at[0], x_recv.at[0]),
            remote(block, spot, device(to_hi=1 - hi), x_send.at[2], x_recv.at[1]),
            remote(block, spot, device(to_section=1, to_hi=1 - hi), x_send.at[1], x_recv.at[1]),
        ]

    def x_local():
        return pltpu.make_async_copy(block, keys.at[z, y, hi, core], x_send.at[3])

    @pl.when(section == 0)
    def _():
        x_local().start()
        for copy in x_copies():
            copy.start()

    own_local().start()
    own_away().start()

    for load in loads:
        load.wait()

    @pl.loop(0, heads // 2)
    def _(pair):
        rope = q_rope[:, pl.ds(pl.multiple_of(pair * LANES, LANES), LANES)]
        for side in range(2):
            head = pair * 2 + side
            lifted = lax.dot_general(nope[head], up[head], nt, preferred_element_type=jnp.float32)
            q[head, :, :kv_rank] = lifted.astype(jnp.bfloat16)
            q[head, :, kv_rank:] = rope[:, side * (LANES // 2) : (side + 1) * (LANES // 2)]

    @pl.when(section == 1)
    def _():
        pltpu.make_async_copy(q, q_out, out_sems.at[0]).start()

    @pl.when(section == 0)
    def _():
        x_local().wait()
        arrive(keys.at[z, y, 1 - hi, core], x_recv.at[1])

    @pl.when(section == 1)
    def _():
        arrive(keys.at[z, y, hi, core], x_recv.at[0])
        arrive(keys.at[z, y, 1 - hi, core], x_recv.at[1])

    low, high, far = row_at(-1), row_at(1), row_at(2)
    columns = [y, low, high, far]
    planes = [z]
    for s in range(1, half):
        planes += [plane_at(-s), plane_at(s)]
    planes.append(plane_at(half))
    steps = [[0]] + [[2 * s - 1, 2 * s] for s in range(1, half)] + [[z_count - 1]]

    def sender(went):
        def send(src, to, send_sem, recv_sem):
            copy = lambda: remote(src(), src(), to(), send_sem(), recv_sem())
            went.append(copy)
            copy().start()

        return send

    went = [[], [], []]

    def along_y(send, n, c, src, d, k):
        send(src, lambda: device(dy=d), lambda: y_send.at[n, k], lambda: y_recv.at[n, k])

    def spread(send, n, c):
        mine = lambda: keys.at[planes[n], y, :, c]
        along_y(send, n, c, mine, 1, 0)
        along_y(send, n, c, mine, -1, 1)

    def spread_on(send, n, c):
        arrive(keys.at[planes[n], low, :, c], y_recv.at[n, 0])
        along_y(send, n, c, lambda: keys.at[planes[n], low, 0, c], 1, 2)
        arrive(keys.at[planes[n], high, :, c], y_recv.at[n, 1])
        along_y(send, n, c, lambda: keys.at[planes[n], high, 1, c], -1, 3)

    def spread_end(n, c):
        arrive(keys.at[planes[n], far, 0, c], y_recv.at[n, 2])
        arrive(keys.at[planes[n], far, 1, c], y_recv.at[n, 3])

    def to_sibling(send, n, c):
        send(
            lambda: keys.at[planes[n], :, :, c],
            lambda: device(to_core=1 - c),
            lambda: sib_send.at[n],
            lambda: sib_recv.at[n],
        )

    def along_z(send, src, up_way, step, k):
        d, j = (1, 0) if up_way else (-1, 1)
        send(
            src,
            lambda: device(dz=d),
            lambda: z_send.at[j, step, k],
            lambda: z_recv.at[j, step, k],
        )

    def decode_a():
        send = sender(went[1])
        ways = ((0, True), (1, False))

        def cell(n, k):
            return lambda: keys.at[planes[n], columns[k], :, 0]

        def column(k):
            for _, up_way in ways:
                along_z(send, cell(0, k), up_way, 0, k)

        spread(send, 0, 0)
        column(0)
        arrive(keys.at[z, low, :, 0], y_recv.at[0, 0])
        along_y(send, 0, 0, lambda: keys.at[z, low, 0, 0], 1, 2)
        column(1)
        arrive(keys.at[z, high, :, 0], y_recv.at[0, 1])
        along_y(send, 0, 0, lambda: keys.at[z, high, 1, 0], -1, 3)
        column(2)
        spread_end(0, 0)
        column(3)
        to_sibling(send, 0, 0)
        for s in range(1, half):
            for k in range(y_count):
                for n, (j, up_way) in zip(steps[s], ways):
                    arrive(cell(n, k)(), z_recv.at[j, s - 1, k])
                    if s < half - 1 or k // 2 == j:
                        along_z(send, cell(n, k), up_way, s, k)
            for n in steps[s]:
                to_sibling(send, n, 0)
        for k in range(y_count):
            arrive(cell(z_count - 1, k)(), z_recv.at[k // 2, half - 1, k])
        to_sibling(send, z_count - 1, 0)

    def decode_b():
        send = sender(went[2])
        ways = ((0, True), (1, False))

        def ahead(n, s, j, up_way):
            if s < half - 1:
                part = lambda: keys.at[planes[n], y, :, 1]
            else:
                part = lambda: keys.at[planes[n], y, j, 1]
            along_z(send, part, up_way, s, 0)

        for j, up_way in ways:
            ahead(0, 0, j, up_way)
        spread(send, 0, 1)
        for s in range(1, half):
            for n, (j, up_way) in zip(steps[s], ways):
                arrive(keys.at[planes[n], y, :, 1], z_recv.at[j, s - 1, 0])
                ahead(n, s, j, up_way)
                spread(send, n, 1)
            if s == 1:
                spread_on(send, 0, 1)
        for j in range(2):
            arrive(keys.at[planes[-1], y, j, 1], z_recv.at[j, half - 1, 0])
        spread(send, z_count - 1, 1)
        for n in range(z_count):
            if n >= 1:
                spread_on(send, n, 1)
                spread_end(n - 1, 1)
                to_sibling(send, n - 1, 1)
        spread_end(z_count - 1, 1)
        to_sibling(send, z_count - 1, 1)

    behind = [0] + [2 * s - 1 for s in range(1, half)] + [z_count - 1]
    past = planes[2 * (half - 1)]
    forward = sender(went[0])

    def ahead(n, s):
        along_z(forward, lambda: keys.at[planes[n], y, :, core], True, s, 0)

    def prefill_start():
        ahead(0, 0)
        spread(forward, 0, core)
        prefill_chain(1)
        spread_on(forward, 0, core)
        spread_end(0, core)
        to_sibling(forward, 0, core)
        prefill_on(1)
        from_sibling(0)

    def prefill_chain(s):
        n = behind[s]
        arrive(keys.at[planes[n], y, :, core], z_recv.at[0, s - 1, 0])
        if s < half:
            ahead(n, s)
        else:
            along_z(forward, lambda: keys.at[planes[n], y, 1, core], True, 0, 1)
        spread(forward, n, core)

    def prefill_on(s):
        spread_on(forward, behind[s], core)

    def prefill_end(s):
        spread_end(behind[s], core)
        to_sibling(forward, behind[s], core)

    def prefill_past():
        arrive(keys.at[past, y, 1, core], z_recv.at[0, 0, 1])
        n = 2 * (half - 1)
        along_y(forward, n, core, lambda: keys.at[past, y, 1, core], 1, 0)

    def prefill_past_end():
        n = 2 * (half - 1)
        spot = lambda: keys.at[past, low, 1, core]
        arrive(spot(), y_recv.at[n, 0])
        forward(
            spot,
            lambda: device(to_core=1 - core),
            lambda: sib_send.at[n],
            lambda: sib_recv.at[n],
        )

    def from_sibling(n):
        arrive(keys.at[planes[n], :, :, 1 - core], sib_recv.at[n])

    def on(at, event):
        @pl.when(at)
        def _():
            event()

    @pl.when(section == 1)
    def _():
        on(core == 0, decode_a)
        on(core == 1, decode_b)
        for n in range(z_count):
            from_sibling(n)

    @pl.when(section == 0)
    def _():
        top[...] = jnp.full(top.shape, masked_low, jnp.float32)
        total[...] = jnp.zeros(total.shape, jnp.float32)
        acc[...] = jnp.zeros(acc.shape, jnp.float32)

    token = lax.broadcasted_iota(jnp.int32, (tokens, 1), 0)
    position = seq * tokens + token
    count = lengths.shape[1]
    before_it = lax.broadcasted_iota(jnp.int32, (count, count), 0) < lax.broadcasted_iota(
        jnp.int32, (count, count), 1
    )
    earlier = jnp.where(before_it, 1.0, 0.0).astype(jnp.bfloat16)
    wide = jnp.broadcast_to(lengths[...], (8, count))
    digits = [(wide // 64).astype(jnp.bfloat16), (wide % 64).astype(jnp.bfloat16)]
    upper, lower = [jnp.dot(d, earlier, preferred_element_type=jnp.float32) for d in digits]
    starts = (upper * 64.0 + lower)[:1]
    row_low = jnp.max(
        jnp.where(starts <= position.astype(jnp.float32), starts, 0.0), axis=1, keepdims=True
    ).astype(jnp.int32)

    chunk = plane_keys // 2
    tile_heads = 8
    rows = tile_heads * tokens
    tiles = heads // tile_heads

    def fold(tile, key_block):
        count = key_block.shape[0]
        part = pl.ds(pl.multiple_of(tile * rows, rows), rows)
        asked = q[pl.ds(tile * tile_heads, tile_heads)].reshape(rows, width)
        s = lax.dot_general(asked, key_block, nt, preferred_element_type=jnp.float32)
        s = (s.reshape(tile_heads, tokens, count) + bias[:, :count][None]).reshape(rows, count)
        before = top[part, :]
        now = jnp.maximum(before, jnp.max(s, axis=1, keepdims=True))
        shrink = jnp.exp2((before - now) * exponent_scale)
        expo = jnp.exp2((s - over_lanes(now, count)) * exponent_scale)
        top[part, :] = now
        summed = total[part, :] * shrink
        for c in range(0, count, LANES):
            summed = summed + expo[:, c : c + LANES]
        total[part, :] = summed
        acc[part, :] = acc[part, :] * over_lanes(shrink, kv_rank) + jnp.dot(
            expo.astype(jnp.bfloat16),
            key_block[:, :kv_rank],
            preferred_element_type=jnp.float32,
        )

    def hide(first_spot, count):
        spot = first_spot + lax.broadcasted_iota(jnp.int32, (1, count), 1)
        seen = (spot >= row_low) & (spot <= position)
        bias[:, :count] = jnp.where(seen, 0.0, masked_low)

    def past_from_sibling():
        arrive(keys.at[past, low, 1, 1 - core], sib_recv.at[2 * (half - 1)])

    last_step = 4 * (half + 1)
    events = {
        0: [prefill_start],
        1: [functools.partial(prefill_end, 1), functools.partial(prefill_chain, 2)],
        last_step - 8: [prefill_past],
        last_step - 6: [prefill_past_end],
        last_step - 2: [past_from_sibling],
    }
    for s in range(1, half + 1):
        if s > 1:
            events.setdefault(4 * s - 5 - (s > 3), []).append(functools.partial(prefill_on, s))
            events.setdefault(4 * s - 4 - (s > 3), []).append(functools.partial(prefill_end, s))
        if s > 2:
            events.setdefault(3 * s - 5, []).append(functools.partial(prefill_chain, s))
        events.setdefault(4 * s - (2 if s == 1 else 3), []).append(
            functools.partial(from_sibling, behind[s])
        )

    @pl.when(section == 0)
    def _():
        @pl.loop(0, last_step + 1)
        def _(step):
            for at_step in sorted(events):
                for event in events[at_step]:
                    on(step == at_step, event)

            run = step // 2
            turn = step % 2
            is_last = step == last_step
            own_rest = run == 2 * half + 1
            back = jnp.where(own_rest, 0, jnp.where(is_last, half + 1, (run + 1) // 2))
            side = jnp.where(run == 0, 0, (run + 1) % 2)
            side = jnp.where(run == 2 * half - 1, 1, jnp.where(run == 2 * half, 0, side))
            side = jnp.where(own_rest, 1, side)
            slot = jnp.where(own_rest, 1, back % 2)
            reached = (z >= back) & jnp.logical_not(is_last)
            edge = (z > half) & (at_block == 0)

            def load(back, part, slot):
                plane = lax.rem(z - back + z_count, z_count)
                here = keys.at[plane, pl.ds(part * (y_count // 2), y_count // 2)]
                return pltpu.make_async_copy(here, held.at[slot, part], held_sems.at[slot, part])

            def load_past():
                return pltpu.make_async_copy(
                    keys.at[past, y_count - 1, 1], held.at[1, 0, 0, 0], held_sems.at[1, 0]
                )

            @pl.when(step == 0)
            def _():
                load(0, 0, 0).start()

            for s in range(1, half + 1):

                @pl.when((step == 4 * s - (2 if s == 1 else 3)) & (z >= s))
                def _():
                    load(s, 0, s % 2).start()
                    load(s, 1, s % 2).start()

            @pl.when(step == last_step - 4)
            def _():
                load(0, 1, 1).start()

            @pl.when(edge & (step == last_step - 2))
            def _():
                load_past().start()

            @pl.when(reached & (turn == 0))
            def _():
                load(back, side, slot).wait()

            @pl.when(edge & is_last)
            def _():
                load_past().wait()

            mid = plane_blocks // 2
            rim_own = (back == 0) & (side == 1)
            rim_far = (back == half) & (side == 0)
            few = (rim_own | rim_far) & (at_block == mid)
            none = (rim_own & (at_block < mid)) | (rim_far & (at_block > mid))
            first_spot = (z - back) * plane_keys + side * chunk
            few_spot = jnp.where(rim_far, first_spot + chunk - tokens, first_spot)

            @pl.when(reached & jnp.logical_not(few | none))
            def _():
                @pl.when(turn == 0)
                def _():
                    hide(first_spot, chunk)

                for tile in range(tiles // 2):
                    fold(turn * (tiles // 2) + tile, held[slot, side].reshape(chunk, width))

            @pl.when((edge & is_last) | (reached & few & (turn == 0)))
            def _():
                past_spot = (z - half - 1) * plane_keys + plane_keys - tokens
                hide(jnp.where(is_last, past_spot, few_spot), tokens)
                spot = jnp.where(rim_far, y_count - 1, 0)
                block_keys = held[
                    slot, jnp.where(is_last, 0, side), spot // 2, spot % 2
                ].reshape(tokens, width)

                @pl.loop(0, tiles)
                def _(tile):
                    fold(tile, block_keys)

    @pl.when(section == 0)
    def _():
        @pl.loop(0, heads)
        def _(head):
            part = pl.ds(pl.multiple_of(head * tokens, tokens), tokens)
            norm = 1.0 / jnp.sum(total[part, :], axis=1, keepdims=True)
            q[head, :, :kv_rank] = (acc[part, :] * norm).astype(jnp.bfloat16)
            pltpu.make_async_copy(
                q.at[head, :, pl.ds(0, kv_rank)], latent_out.at[head], out_sems.at[1]
            ).start()

        pltpu.make_async_copy(
            q.at[:, :, pl.ds(0, kv_rank)], latent_out, out_sems.at[1]
        ).wait()
        for copy in x_copies():
            copy.wait_send()

    @pl.when(section == 1)
    def _():
        pltpu.make_async_copy(q, q_out, out_sems.at[0]).wait()

    groups = [section == 0, (section == 1) & (core == 0), (section == 1) & (core == 1)]
    for group, copies in zip(groups, went):

        @pl.when(group)
        def _():
            for copy in copies:
                copy().wait_send()

    arrive(own_out.at[1 - core], own_sems.at[2])
    own_away().wait_send()
    own_local().wait()


def prefill_part(own, q_nope, q_rope, up_key, lengths, seq_count, exponent_scale):
    rows, width = own.shape
    heads, tokens, _ = q_nope.shape
    kv_rank = up_key.shape[1]
    y_count = 4
    z_count = seq_count // (2 * y_count)
    dma = pltpu.SemaphoreType.DMA
    bf16 = own.dtype
    chunk = y_count * tokens
    vmem = pl.BlockSpec(memory_space=pltpu.VMEM)
    hbm = pl.BlockSpec(memory_space=pl.ANY)
    return pl.pallas_call(
        functools.partial(prefill_kernel, z_count, y_count, kv_rank, exponent_scale),
        out_shape=[
            jax.ShapeDtypeStruct((z_count, y_count, 2, 2, rows, width), bf16),
            jax.ShapeDtypeStruct((2, rows, width), bf16),
            jax.ShapeDtypeStruct((heads, tokens, width), bf16),
            jax.ShapeDtypeStruct((heads, tokens, kv_rank), bf16),
        ],
        in_specs=[vmem, hbm, vmem, hbm, vmem],
        out_specs=[hbm] * 4,
        scratch_shapes=[
            pltpu.VMEM((rows, width), bf16),
            pltpu.VMEM(q_nope.shape, bf16),
            pltpu.VMEM(up_key.shape, bf16),
            pltpu.VMEM((heads, tokens, width), bf16),
            pltpu.VMEM((heads * tokens, kv_rank), jnp.float32),
            pltpu.VMEM((heads * tokens, LANES), jnp.float32),
            pltpu.VMEM((heads * tokens, LANES), jnp.float32),
            pltpu.VMEM((2, 2, y_count // 2, 2, 2, rows, width), bf16),
            pltpu.VMEM((tokens, chunk), jnp.float32),
            dma((2,)),
            dma((2,)),
            dma((2, 2)),
            dma((4,)),
            dma((2,)),
            dma((3,)),
            dma((2, z_count // 2, y_count)),
            dma((2, z_count // 2, y_count)),
            dma((z_count, 4)),
            dma((z_count, 4)),
            dma((z_count,)),
            dma((z_count,)),
        ],
        compiler_params=pltpu.CompilerParams(
            collective_id=0, has_side_effects=True, vmem_limit_bytes=56 << 20
        ),
    )(own, q_nope, q_rope, up_key, lengths)


def over_lanes(value, width):
    return jnp.concatenate([value] * (width // LANES), axis=1)


def decode_kernel(
    kv_rank,
    groups,
    exponent_scale,
    lengths,
    table,
    q_ref,
    keys,
    own_keys,
    _,
    out_ref,
    acc,
    top,
    total,
    held,
    ready,
    q_held,
    sems,
    q_sems,
    out_sems,
):
    band = pl.program_id(0)
    bands = pl.num_programs(0)
    _, heads, tokens, width = q_held.shape
    rows = heads * tokens
    all_keys = keys.shape[0]
    nt = (((1,), (1,)), ((), ()))

    @pl.when(lax.axis_index("section") == 1)
    def _():
        def prompt_range(which):
            prompt = table[lax.axis_index("seq") * bands + which] // groups
            low = lax.fori_loop(0, prompt, lambda k, at: at + lengths[k], jnp.int32(0))
            return low, low + lengths[prompt]

        def chunk_at(start, i):
            return pl.multiple_of(jnp.minimum(start + i * KEY_BLOCK, all_keys - KEY_BLOCK), 16)

        def fetch_from(start, i, slot):
            return pltpu.make_async_copy(
                keys.at[pl.ds(chunk_at(start, i), KEY_BLOCK), :], held.at[slot], sems.at[slot]
            )

        def band_rows(which):
            return pl.ds(pl.multiple_of(which * tokens, tokens), tokens)

        def fetch_q(which):
            slot = lax.rem(which, 2)
            return pltpu.make_async_copy(
                q_ref.at[:, band_rows(which), :], q_held.at[slot], q_sems.at[slot]
            )

        def leave(which):
            slot = lax.rem(which, 2)
            return pltpu.make_async_copy(
                ready.at[slot], out_ref.at[:, band_rows(which), :], out_sems.at[slot]
            )

        low, last = prompt_range(band)
        first = low // 16 * 16
        chunks = (last - first + KEY_BLOCK - 1) // KEY_BLOCK

        def fetch(i):
            slot = jnp.where(i == 0, lax.rem(band, 2), 2 + lax.rem(i, 2))
            return fetch_from(first, i, slot)

        @pl.when(band == 0)
        def _():
            fetch_q(0).start()
            fetch(0).start()

        @pl.when(band + 1 < bands)
        def _():
            fetch_q(band + 1).start()
            next_low, _ = prompt_range(band + 1)
            fetch_from(next_low // 16 * 16, 0, lax.rem(band + 1, 2)).start()

        fetch_q(band).wait()
        q = q_held[lax.rem(band, 2)].reshape(rows, width)
        own = own_keys[...]
        scores = lax.dot_general(q, own, nt, preferred_element_type=jnp.float32)
        asked = lax.broadcasted_iota(jnp.int32, (tokens, tokens), 0)
        key = lax.broadcasted_iota(jnp.int32, (tokens, tokens), 1)
        seen = (asked % SAMPLES == key % SAMPLES) & (key // SAMPLES <= asked // SAMPLES)
        bias = jnp.where(seen, 0.0, masked_low)
        bias = jnp.broadcast_to(bias[None], (heads, tokens, tokens)).reshape(rows, tokens)
        scores = scores + bias
        own_top = jnp.max(scores, axis=1, keepdims=True)
        expo = jnp.exp2((scores - own_top) * exponent_scale)
        lane = lax.broadcasted_iota(jnp.int32, (rows, LANES), 1)
        total[...] = jnp.where(lane == 0, jnp.sum(expo, axis=1, keepdims=True), 0.0)
        top[...] = jnp.broadcast_to(own_top, (rows, LANES))
        acc[...] = jnp.dot(
            expo.astype(jnp.bfloat16), own[:, :kv_rank], preferred_element_type=jnp.float32
        )

        def fold(key_block, low_spot, at):
            count = key_block.shape[0]
            s = lax.dot_general(q, key_block, nt, preferred_element_type=jnp.float32)
            if low_spot is not None:
                spot = at + lax.broadcasted_iota(jnp.int32, (1, count), 1)
                here = (spot >= jnp.maximum(low, low_spot)) & (spot < last)
                s = s + jnp.where(here, 0.0, masked_low)
            before = top[...]
            now = jnp.maximum(before, jnp.max(s, axis=1, keepdims=True))
            shrink = jnp.exp2((before - now) * exponent_scale)
            expo = jnp.exp2((s - over_lanes(now, count)) * exponent_scale)
            top[...] = now
            summed = total[...] * shrink
            for c in range(0, count, LANES):
                summed = summed + expo[:, c : c + LANES]
            total[...] = summed
            acc[...] = acc[...] * over_lanes(shrink, kv_rank) + jnp.dot(
                expo.astype(jnp.bfloat16),
                key_block[:, :kv_rank],
                preferred_element_type=jnp.float32,
            )

        @pl.loop(0, chunks)
        def _(i):
            slot = jnp.where(i == 0, lax.rem(band, 2), 2 + lax.rem(i, 2))
            fetch(i).wait()

            @pl.when(i + 1 < chunks)
            def _():
                fetch(i + 1).start()

            nominal = first + i * KEY_BLOCK
            at = chunk_at(first, i)
            whole = (nominal >= low) & (nominal + KEY_BLOCK <= last)

            @pl.when(whole)
            def _():
                fold(held[slot], None, None)

            @pl.when(jnp.logical_not(whole))
            def _():
                skip = (nominal - at) // EDGE_BLOCK

                @pl.loop(skip, (jnp.minimum(last - at, KEY_BLOCK) + EDGE_BLOCK - 1) // EDGE_BLOCK)
                def _(j):
                    here = pl.multiple_of(j * EDGE_BLOCK, EDGE_BLOCK)
                    fold(held[slot, pl.ds(here, EDGE_BLOCK), :], nominal, at + here)

        norm = 1.0 / jnp.sum(total[...], axis=1, keepdims=True)
        @pl.when(band >= 2)
        def _():
            leave(band - 2).wait()

        ready[lax.rem(band, 2)] = (
            (acc[...] * norm).astype(jnp.bfloat16).reshape(heads, tokens, kv_rank)
        )
        leave(band).start()

        @pl.when(band == bands - 1)
        def _():
            leave(band - 1).wait()
            leave(band).wait()


def shards(query_nope, query_rope, latent, up_key, value_up_weight, lengths, owner_request_table):
    seq_count = lax.axis_size("seq")
    tok_dev, head_dev, nope_dim = query_nope.shape[1:]
    rope_dim = query_rope.shape[2] // head_dev
    kv_rank = up_key.shape[1]
    width = kv_rank + rope_dim
    req_dev = owner_request_table.shape[0] // seq_count
    groups = owner_request_table.shape[0] // lengths.shape[0]
    band_tokens = tok_dev // req_dev
    exponent_scale = math.log2(math.e) / math.sqrt(nope_dim + rope_dim)

    keys, pair, queries, latent_out = prefill_part(
        latent[0],
        query_nope[0].swapaxes(0, 1),
        query_rope[0],
        up_key,
        lengths[None, :],
        seq_count,
        exponent_scale,
    )
    rows = head_dev * band_tokens
    latent_out = pl.pallas_call(
        functools.partial(decode_kernel, kv_rank, groups, exponent_scale),
        out_shape=jax.ShapeDtypeStruct((head_dev, tok_dev, kv_rank), jnp.bfloat16),
        grid_spec=pltpu.PrefetchScalarGridSpec(
            num_scalar_prefetch=2,
            grid=(req_dev,),
            in_specs=[
                pl.BlockSpec(memory_space=pl.ANY),
                pl.BlockSpec(memory_space=pl.ANY),
                pl.BlockSpec((band_tokens, width), lambda i, *_: (i, 0)),
                pl.BlockSpec(memory_space=pl.ANY),
            ],
            out_specs=pl.BlockSpec(memory_space=pl.ANY),
            scratch_shapes=[
                pltpu.VMEM((rows, kv_rank), jnp.float32),
                pltpu.VMEM((rows, LANES), jnp.float32),
                pltpu.VMEM((rows, LANES), jnp.float32),
                pltpu.VMEM((4, KEY_BLOCK, width), jnp.bfloat16),
                pltpu.VMEM((2, head_dev, band_tokens, kv_rank), jnp.bfloat16),
                pltpu.VMEM((2, head_dev, band_tokens, width), jnp.bfloat16),
                pltpu.SemaphoreType.DMA((4,)),
                pltpu.SemaphoreType.DMA((2,)),
                pltpu.SemaphoreType.DMA((2,)),
            ],
        ),
        input_output_aliases={5: 0},
        compiler_params=pltpu.CompilerParams(vmem_limit_bytes=58 << 20),
    )(
        lengths,
        owner_request_table,
        queries,
        keys.reshape(-1, width),
        pair.reshape(-1, width),
        latent_out,
    )

    attended = jnp.einsum(
        "htk,hkv->thv", latent_out, value_up_weight, preferred_element_type=jnp.float32
    )
    return attended.astype(jnp.bfloat16)[None]


def solution(mesh):
    in_specs = (
        P("section", "seq", "head", None),
        P("section", "seq", "head"),
        P("section", ("seq", "head"), None),
        P("head", None, None),
        P("head", None, None),
        P(),
        P(),
    )
    out_specs = P("section", "seq", "head", None)
    return jax.shard_map(shards, mesh=mesh, in_specs=in_specs, out_specs=out_specs, check_vma=False)
```

```python
import functools
import math

import jax
import jax.numpy as jnp
from jax import lax
from jax.experimental import pallas as pl
from jax.experimental.pallas import tpu as pltpu
from jax.sharding import PartitionSpec as P

SAMPLES = 8
STEPS = 4
BLOCK = 64

scale_top = 448.0
tiny_eps = 1e-06
masked_low = -1e30

KEY_BLOCK = 1024
EDGE_BLOCK = 512

CHAIN_STEPS = (0, 1, 3, 5)
ON_STEPS = (0, 2, 5, 8)
END_STEPS = (1, 3, 7, 10)
SIBLING_STEPS = (2, 5, 9, 13)
PAST_STEPS = (8, 10, 15)
LANES = 128


def prefill_kernel(
    z_count, y_count, kv_rank, exponent_scale, own_in, q_nope, q_rope, up_key, value_up, lengths,
    keys, own_out, q_out, out, block, nope, up, q, acc, top, total, held, bias, ready,
    in_sems, out_sems, held_sems, x_send, x_recv, own_sems,
    z_send, z_recv, y_send, y_recv, sib_send, sib_recv,
):
    section = lax.axis_index("section")
    seq = lax.axis_index("seq")
    core = lax.axis_index("head")
    z = seq // (2 * y_count)
    y = seq // 2 % y_count
    hi = seq % 2
    half = z_count // 2
    heads, tokens, width = q.shape
    plane_blocks = 2 * y_count
    at_block = seq % plane_blocks
    plane_keys = plane_blocks * tokens
    nt = (((1,), (1,)), ((), ()))

    def plane_at(dz):
        return lax.rem(z + dz + z_count, z_count)

    def row_at(dy):
        return lax.rem(y + dy + y_count, y_count)

    def device(dz=0, dy=0, to_hi=None, to_section=None, to_core=None):
        th = hi if to_hi is None else to_hi
        return (
            section if to_section is None else to_section,
            (plane_at(dz) * y_count + row_at(dy)) * 2 + th,
            core if to_core is None else to_core,
        )

    loads = [
        pltpu.make_async_copy(q_nope, nope, in_sems.at[0]),
        pltpu.make_async_copy(up_key, up, in_sems.at[1]),
    ]
    for load in loads:
        load.start()

    barrier = pltpu.get_barrier_semaphore()
    peers = [
        device(to_core=1 - core),
        device(to_section=1 - section),
        device(to_hi=1 - hi),
        device(to_section=1 - section, to_hi=1 - hi),
        device(dz=1),
        device(dz=-1),
        device(dy=1),
        device(dy=-1),
    ]
    for peer in peers:
        pl.semaphore_signal(barrier, inc=1, device_id=peer, device_id_type=pl.DeviceIdType.MESH)

    @pl.when(section == 0)
    def _():
        rows = own_in[...].astype(jnp.float32)
        largest = jnp.max(jnp.abs(rows))
        spread = jnp.full((8, LANES), largest, jnp.float32)
        scale = ((spread + tiny_eps) / scale_top).astype(jnp.bfloat16).astype(jnp.float32)
        factor = scale[:1, :1]
        stored = (rows / factor).astype(jnp.bfloat16)
        block[...] = (stored.astype(jnp.float32) * factor).astype(jnp.bfloat16)

    @pl.when(section == 1)
    def _():
        block[...] = own_in[...]

    pl.semaphore_wait(barrier, len(peers))

    def remote(src, dst, to, send_sem, recv_sem):
        return pltpu.make_async_remote_copy(
            src_ref=src,
            dst_ref=dst,
            send_sem=send_sem,
            recv_sem=recv_sem,
            device_id=to,
            device_id_type=pl.DeviceIdType.MESH,
        )

    def arrive(dst, recv_sem):
        remote(dst, dst, device(to_core=1 - core), recv_sem, recv_sem).wait_recv()

    def own_local():
        return pltpu.make_async_copy(block, own_out.at[core], own_sems.at[0])

    def own_away():
        to = device(to_core=1 - core)
        return remote(block, own_out.at[core], to, own_sems.at[1], own_sems.at[2])

    def x_copies():
        spot = keys.at[z, y, hi, core]
        return [
            remote(block, spot, device(to_hi=1 - hi), x_send.at[2], x_recv.at[1]),
            remote(block, spot, device(to_section=1), x_send.at[0], x_recv.at[0]),
            remote(block, spot, device(to_section=1, to_hi=1 - hi), x_send.at[1], x_recv.at[1]),
        ]

    def x_local():
        return pltpu.make_async_copy(block, keys.at[z, y, hi, core], x_send.at[3])

    @pl.when(section == 0)
    def _():
        x_local().start()
        for copy in x_copies():
            copy.start()

    own_local().start()
    own_away().start()

    for load in loads:
        load.wait()

    @pl.loop(0, heads // 2)
    def _(pair):
        rope = q_rope[:, pl.ds(pl.multiple_of(pair * LANES, LANES), LANES)]
        for side in range(2):
            head = pair * 2 + side
            lifted = lax.dot_general(nope[head], up[head], nt, preferred_element_type=jnp.float32)
            q[head, :, :kv_rank] = lifted.astype(jnp.bfloat16)
            q[head, :, kv_rank:] = rope[:, side * (LANES // 2) : (side + 1) * (LANES // 2)]

    def load_value_up():
        return pltpu.make_async_copy(value_up, up, in_sems.at[1])

    @pl.when(section == 0)
    def _():
        load_value_up().start()

    @pl.when(section == 1)
    def _():
        pltpu.make_async_copy(q, q_out, out_sems.at[0]).start()

    @pl.when(section == 0)
    def _():
        x_local().wait()
        arrive(keys.at[z, y, 1 - hi, core], x_recv.at[1])

    @pl.when(section == 1)
    def _():
        arrive(keys.at[z, y, hi, core], x_recv.at[0])
        arrive(keys.at[z, y, 1 - hi, core], x_recv.at[1])

    low, high, far = row_at(-1), row_at(1), row_at(2)
    columns = [y, low, high, far]
    planes = [z]
    for s in range(1, half):
        planes += [plane_at(-s), plane_at(s)]
    planes.append(plane_at(half))
    steps = [[0]] + [[2 * s - 1, 2 * s] for s in range(1, half)] + [[z_count - 1]]

    def sender(went):
        def send(src, to, send_sem, recv_sem):
            copy = lambda: remote(src(), src(), to(), send_sem(), recv_sem())
            went.append(copy)
            copy().start()

        return send

    went = [[], [], []]

    def along_y(send, n, c, src, d, k):
        send(src, lambda: device(dy=d), lambda: y_send.at[n, k], lambda: y_recv.at[n, k])

    def spread(send, n, c):
        mine = lambda: keys.at[planes[n], y, :, c]
        along_y(send, n, c, mine, 1, 0)
        along_y(send, n, c, mine, -1, 1)

    def spread_on(send, n, c):
        arrive(keys.at[planes[n], low, :, c], y_recv.at[n, 0])
        along_y(send, n, c, lambda: keys.at[planes[n], low, 0, c], 1, 2)
        arrive(keys.at[planes[n], high, :, c], y_recv.at[n, 1])
        along_y(send, n, c, lambda: keys.at[planes[n], high, 1, c], -1, 3)

    def spread_end(n, c):
        arrive(keys.at[planes[n], far, 0, c], y_recv.at[n, 2])
        arrive(keys.at[planes[n], far, 1, c], y_recv.at[n, 3])

    def to_sibling(send, n, c):
        send(
            lambda: keys.at[planes[n], :, :, c],
            lambda: device(to_core=1 - c),
            lambda: sib_send.at[n],
            lambda: sib_recv.at[n],
        )

    def along_z(send, src, up_way, step, k):
        d, j = (1, 0) if up_way else (-1, 1)
        send(
            src,
            lambda: device(dz=d),
            lambda: z_send.at[j, step, k],
            lambda: z_recv.at[j, step, k],
        )

    def decode_a():
        send = sender(went[1])
        ways = ((0, True), (1, False))

        def cell(n, k):
            return lambda: keys.at[planes[n], columns[k], :, 0]

        def column(k):
            for _, up_way in ways:
                along_z(send, cell(0, k), up_way, 0, k)

        spread(send, 0, 0)
        column(0)
        arrive(keys.at[z, low, :, 0], y_recv.at[0, 0])
        along_y(send, 0, 0, lambda: keys.at[z, low, 0, 0], 1, 2)
        column(1)
        arrive(keys.at[z, high, :, 0], y_recv.at[0, 1])
        along_y(send, 0, 0, lambda: keys.at[z, high, 1, 0], -1, 3)
        column(2)
        spread_end(0, 0)
        column(3)
        to_sibling(send, 0, 0)
        for s in range(1, half):
            for k in range(y_count):
                for n, (j, up_way) in zip(steps[s], ways):
                    arrive(cell(n, k)(), z_recv.at[j, s - 1, k])
                    if s < half - 1 or k // 2 == j:
                        along_z(send, cell(n, k), up_way, s, k)
            for n in steps[s]:
                to_sibling(send, n, 0)
        for k in range(y_count):
            arrive(cell(z_count - 1, k)(), z_recv.at[k // 2, half - 1, k])
        to_sibling(send, z_count - 1, 0)

    def decode_b():
        send = sender(went[2])
        ways = ((0, True), (1, False))

        def ahead(n, s, j, up_way):
            if s < half - 1:
                part = lambda: keys.at[planes[n], y, :, 1]
            else:
                part = lambda: keys.at[planes[n], y, j, 1]
            along_z(send, part, up_way, s, 0)

        for j, up_way in ways:
            ahead(0, 0, j, up_way)
        spread(send, 0, 1)
        for s in range(1, half):
            for n, (j, up_way) in zip(steps[s], ways):
                arrive(keys.at[planes[n], y, :, 1], z_recv.at[j, s - 1, 0])
                ahead(n, s, j, up_way)
                spread(send, n, 1)
            if s == 1:
                spread_on(send, 0, 1)
        for j in range(2):
            arrive(keys.at[planes[-1], y, j, 1], z_recv.at[j, half - 1, 0])
        spread(send, z_count - 1, 1)
        for n in range(z_count):
            if n >= 1:
                spread_on(send, n, 1)
                spread_end(n - 1, 1)
                to_sibling(send, n - 1, 1)
        spread_end(z_count - 1, 1)
        to_sibling(send, z_count - 1, 1)

    behind = [0] + [2 * s - 1 for s in range(1, half)] + [z_count - 1]
    past = planes[2 * (half - 1)]
    forward = sender(went[0])

    def ahead(n, s):
        along_z(forward, lambda: keys.at[planes[n], y, :, core], True, s, 0)

    def prefill_start():
        ahead(0, 0)
        spread(forward, 0, core)
        prefill_chain(1)
        spread_on(forward, 0, core)
        spread_end(0, core)
        to_sibling(forward, 0, core)
        prefill_on(1)
        from_sibling(0)

    def prefill_chain(s):
        n = behind[s]
        arrive(keys.at[planes[n], y, :, core], z_recv.at[0, s - 1, 0])
        if s < half:
            ahead(n, s)
        else:
            along_z(forward, lambda: keys.at[planes[n], y, 1, core], True, 0, 1)
        spread(forward, n, core)

    def prefill_on(s):
        spread_on(forward, behind[s], core)

    def prefill_end(s):
        spread_end(behind[s], core)
        to_sibling(forward, behind[s], core)

    def prefill_past():
        arrive(keys.at[past, y, 1, core], z_recv.at[0, 0, 1])
        n = 2 * (half - 1)
        along_y(forward, n, core, lambda: keys.at[past, y, 1, core], 1, 0)

    def prefill_past_end():
        n = 2 * (half - 1)
        spot = lambda: keys.at[past, low, 1, core]
        arrive(spot(), y_recv.at[n, 0])
        forward(
            spot,
            lambda: device(to_core=1 - core),
            lambda: sib_send.at[n],
            lambda: sib_recv.at[n],
        )

    def from_sibling(n):
        arrive(keys.at[planes[n], :, :, 1 - core], sib_recv.at[n])

    def on(at, event):
        @pl.when(at)
        def _():
            event()

    @pl.when(section == 1)
    def _():
        on(core == 0, decode_a)
        on(core == 1, decode_b)
        for n in range(z_count):
            from_sibling(n)

    @pl.when(section == 0)
    def _():
        top[...] = jnp.full(top.shape, masked_low, jnp.float32)
        total[...] = jnp.zeros(total.shape, jnp.float32)
        acc[...] = jnp.zeros(acc.shape, jnp.float32)

    token = lax.broadcasted_iota(jnp.int32, (tokens, 1), 0)
    position = seq * tokens + token
    count = lengths.shape[1]
    before_it = lax.broadcasted_iota(jnp.int32, (count, count), 0) < lax.broadcasted_iota(
        jnp.int32, (count, count), 1
    )
    earlier = jnp.where(before_it, 1.0, 0.0).astype(jnp.bfloat16)
    wide = jnp.broadcast_to(lengths[...], (8, count))
    digits = [(wide // 64).astype(jnp.bfloat16), (wide % 64).astype(jnp.bfloat16)]
    upper, lower = [jnp.dot(d, earlier, preferred_element_type=jnp.float32) for d in digits]
    starts = (upper * 64.0 + lower)[:1]
    row_low = jnp.max(
        jnp.where(starts <= position.astype(jnp.float32), starts, 0.0), axis=1, keepdims=True
    ).astype(jnp.int32)

    chunk = plane_keys // 2
    tile_heads = 8
    rows = tile_heads * tokens
    tiles = heads // tile_heads

    def fold(tile, key_block):
        count = key_block.shape[0]
        part = pl.ds(pl.multiple_of(tile * rows, rows), rows)
        asked = q[pl.ds(tile * tile_heads, tile_heads)].reshape(rows, width)
        s = lax.dot_general(asked, key_block, nt, preferred_element_type=jnp.float32)
        s = (s.reshape(tile_heads, tokens, count) + bias[:, :count][None]).reshape(rows, count)
        before = top[part, :]
        now = jnp.maximum(before, jnp.max(s, axis=1, keepdims=True))
        shrink = jnp.exp2((before - now) * exponent_scale)
        expo = jnp.exp2((s - over_lanes(now, count)) * exponent_scale)
        top[part, :] = now
        summed = total[part, :] * shrink
        for c in range(0, count, LANES):
            summed = summed + expo[:, c : c + LANES]
        total[part, :] = summed
        acc[part, :] = acc[part, :] * over_lanes(shrink, kv_rank) + jnp.dot(
            expo.astype(jnp.bfloat16),
            key_block[:, :kv_rank],
            preferred_element_type=jnp.float32,
        )

    def past_from_sibling():
        arrive(keys.at[past, low, 1, 1 - core], sib_recv.at[2 * (half - 1)])

    last_step = 4 * (half + 1)
    timetable = [
        (prefill_chain, CHAIN_STEPS),
        (prefill_on, ON_STEPS),
        (prefill_end, END_STEPS),
        (lambda s: from_sibling(behind[s]), SIBLING_STEPS),
    ]
    events = {0: [prefill_start]}
    for s in range(1, half + 1):
        for event, at_steps in timetable:
            if at_steps[s - 1] > 0:
                spot = events.setdefault(at_steps[s - 1], [])
                spot.append(functools.partial(event, s))
    for event, at_step in zip((prefill_past, prefill_past_end, past_from_sibling), PAST_STEPS):
        events.setdefault(at_step, []).append(event)

    @pl.when(section == 0)
    def _():
        mid = plane_blocks // 2
        at_first, at_mid = at_block == 0, at_block == mid
        reaches_past = at_first & (z > half)

        @pl.loop(0, last_step)
        def _(step):
            for at_step in sorted(events):
                for event in events[at_step]:
                    on(step == at_step, event)

            run = step // 2
            turn = step % 2
            rest = run == 2 * half + 1
            back = jnp.where(rest, 0, (run + 1) // 2)
            side = jnp.where(run == 0, 0, (run + 1) % 2)
            side = jnp.where(rest, 1, side)
            slot = jnp.where(rest, 1, back % 2)
            reached = z >= back

            def load(back, part, slot, into):
                plane = lax.rem(z - back + z_count, z_count)
                here = keys.at[plane, pl.ds(part * (y_count // 2), y_count // 2)]
                return pltpu.make_async_copy(here, held.at[slot, into], held_sems.at[slot, into])

            def load_first():
                return pltpu.make_async_copy(
                    keys.at[past, y_count - 1, 1], held.at[1, 0, 0, 0], held_sems.at[1, 0]
                )

            def load_mid():
                return pltpu.make_async_copy(
                    keys.at[planes[-1], y_count // 2 - 1, 1],
                    held.at[1, 1, y_count // 2 - 1, 1],
                    held_sems.at[1, 0],
                )

            @pl.when(step == 0)
            def _():
                load(0, 0, 0, 0).start()

            for s in range(1, half + 1):

                @pl.when((step == SIBLING_STEPS[s - 1]) & (z >= s))
                def _():
                    load(s, 0, s % 2, 0).start()
                    load(s, 1, s % 2, 1).start()

            @pl.when(step == last_step - 5)
            def _():
                @pl.when(reaches_past)
                def _():
                    load_first().start()

                @pl.when(at_block >= mid)
                def _():
                    rest_load = load(0, 1, 1, 1)
                    rest_load.start()
                    rest_load.wait()

                @pl.when(at_mid)
                def _():
                    load_mid().start()

            @pl.when(reached & (turn == 0) & jnp.logical_not(rest))
            def _():
                load(back, side, slot, side).wait()

            at_past = reaches_past & (run == 2 * half)

            @pl.when(at_past & (turn == 0))
            def _():
                load_first().wait()

            @pl.when((turn == 0) & rest & at_mid)
            def _():
                load_mid().wait()

            none = (rest & (at_block < mid)) | ((run == 2 * half - 1) & (at_block >= mid))
            first_spot = (z - back) * plane_keys + side * chunk

            @pl.when(reached & jnp.logical_not(none))
            def _():
                @pl.when(turn == 0)
                def _():
                    lane = lax.broadcasted_iota(jnp.int32, (1, chunk + tokens), 1)
                    spot = first_spot + lane
                    shift = (half * plane_keys) + chunk
                    spot = jnp.where(
                        rest & at_mid & (lane >= chunk - tokens), spot - shift, spot
                    )
                    spot = jnp.where(lane >= chunk, spot - plane_keys - tokens, spot)
                    seen = (spot >= row_low) & (spot <= position)
                    bias[...] = jnp.where(seen, 0.0, masked_low)

                here = held.at[slot, side]

                @pl.when(at_past)
                def _():
                    behind_it = held[1, 0, 0, 0].reshape(tokens, width)
                    key_block = jnp.concatenate([here[...].reshape(chunk, width), behind_it])

                    @pl.loop(0, tiles // 2)
                    def _(tile):
                        fold(turn * (tiles // 2) + tile, key_block)

                @pl.when(jnp.logical_not(at_past))
                def _():
                    for tile in range(tiles // 2):
                        fold(turn * (tiles // 2) + tile, here[...].reshape(chunk, width))

    @pl.when(section == 0)
    def _():
        load_value_up().wait()

        @pl.loop(0, heads)
        def _(head):
            part = pl.ds(pl.multiple_of(head * tokens, tokens), tokens)
            norm = 1.0 / jnp.sum(total[part, :], axis=1, keepdims=True)
            mixed = (acc[part, :] * norm).astype(jnp.bfloat16)
            ready[head] = jnp.dot(mixed, up[head], preferred_element_type=jnp.float32).astype(
                jnp.bfloat16
            )

        done = pltpu.make_async_copy(ready, out, out_sems.at[1])
        done.start()
        done.wait()
        for copy in x_copies():
            copy.wait_send()

    @pl.when(section == 1)
    def _():
        pltpu.make_async_copy(q, q_out, out_sems.at[0]).wait()

    groups = [section == 0, (section == 1) & (core == 0), (section == 1) & (core == 1)]
    for group, copies in zip(groups, went):

        @pl.when(group)
        def _():
            for copy in copies:
                copy().wait_send()

    arrive(own_out.at[1 - core], own_sems.at[2])
    own_away().wait_send()
    own_local().wait()


def prefill_part(own, q_nope, q_rope, up_key, value_up, lengths, seq_count, exponent_scale):
    rows, width = own.shape
    heads, tokens, _ = q_nope.shape
    kv_rank = up_key.shape[1]
    y_count = 4
    z_count = seq_count // (2 * y_count)
    dma = pltpu.SemaphoreType.DMA
    bf16 = own.dtype
    chunk = y_count * tokens
    vmem = pl.BlockSpec(memory_space=pltpu.VMEM)
    hbm = pl.BlockSpec(memory_space=pl.ANY)
    return pl.pallas_call(
        functools.partial(prefill_kernel, z_count, y_count, kv_rank, exponent_scale),
        out_shape=[
            jax.ShapeDtypeStruct((z_count, y_count, 2, 2, rows, width), bf16),
            jax.ShapeDtypeStruct((2, rows, width), bf16),
            jax.ShapeDtypeStruct((heads, tokens, width), bf16),
            jax.ShapeDtypeStruct((heads, tokens, value_up.shape[2]), bf16),
        ],
        in_specs=[vmem, hbm, vmem, hbm, hbm, vmem],
        out_specs=[hbm] * 4,
        scratch_shapes=[
            pltpu.VMEM((rows, width), bf16),
            pltpu.VMEM(q_nope.shape, bf16),
            pltpu.VMEM(up_key.shape, bf16),
            pltpu.VMEM((heads, tokens, width), bf16),
            pltpu.VMEM((heads * tokens, kv_rank), jnp.float32),
            pltpu.VMEM((heads * tokens, LANES), jnp.float32),
            pltpu.VMEM((heads * tokens, LANES), jnp.float32),
            pltpu.VMEM((2, 2, y_count // 2, 2, 2, rows, width), bf16),
            pltpu.VMEM((tokens, chunk + tokens), jnp.float32),
            pltpu.VMEM((heads, tokens, value_up.shape[2]), bf16),
            dma((2,)),
            dma((2,)),
            dma((2, 2)),
            dma((4,)),
            dma((2,)),
            dma((3,)),
            dma((2, z_count // 2, y_count)),
            dma((2, z_count // 2, y_count)),
            dma((z_count, 4)),
            dma((z_count, 4)),
            dma((z_count,)),
            dma((z_count,)),
        ],
        compiler_params=pltpu.CompilerParams(
            collective_id=0, has_side_effects=True, vmem_limit_bytes=56 << 20
        ),
    )(own, q_nope, q_rope, up_key, value_up, lengths)


def over_lanes(value, width):
    return jnp.concatenate([value] * (width // LANES), axis=1)


def decode_kernel(
    kv_rank,
    groups,
    exponent_scale,
    lengths,
    table,
    q_ref,
    keys,
    own_keys,
    value_up,
    _,
    out_ref,
    acc,
    top,
    total,
    held,
    lat,
    up,
    ready,
    q_held,
    sems,
    q_sems,
    up_sems,
):
    band = pl.program_id(0)
    bands = pl.num_programs(0)
    _, heads, tokens, width = q_held.shape
    rows = heads * tokens
    all_keys = keys.shape[0]
    nt = (((1,), (1,)), ((), ()))

    @pl.when(lax.axis_index("section") == 1)
    def _():
        def prompt_range(which):
            prompt = table[lax.axis_index("seq") * bands + which] // groups
            low = lax.fori_loop(0, prompt, lambda k, at: at + lengths[k], jnp.int32(0))
            return low, low + lengths[prompt]

        def chunk_at(start, i):
            return pl.multiple_of(jnp.minimum(start + i * KEY_BLOCK, all_keys - KEY_BLOCK), 16)

        def fetch_from(start, i, slot):
            return pltpu.make_async_copy(
                keys.at[pl.ds(chunk_at(start, i), KEY_BLOCK), :], held.at[slot], sems.at[slot]
            )

        def band_rows(which):
            return pl.ds(pl.multiple_of(which * tokens, tokens), tokens)

        def fetch_q(which):
            slot = lax.rem(which, 2)
            return pltpu.make_async_copy(
                q_ref.at[:, band_rows(which), :], q_held.at[slot], q_sems.at[slot]
            )

        def load_up():
            return pltpu.make_async_copy(value_up, up, up_sems.at[0])

        low, last = prompt_range(band)
        first = low // 16 * 16
        chunks = (last - first + KEY_BLOCK - 1) // KEY_BLOCK

        def fetch(i):
            slot = jnp.where(i == 0, lax.rem(band, 2), 2 + lax.rem(i, 2))
            return fetch_from(first, i, slot)

        @pl.when(band == 0)
        def _():
            fetch_q(0).start()
            fetch(0).start()
            load_up().start()

        @pl.when(band + 1 < bands)
        def _():
            fetch_q(band + 1).start()
            next_low, _ = prompt_range(band + 1)
            fetch_from(next_low // 16 * 16, 0, lax.rem(band + 1, 2)).start()

        fetch_q(band).wait()
        q = q_held[lax.rem(band, 2)].reshape(rows, width)
        def score(key_block):
            return lax.dot_general(q, key_block, nt, preferred_element_type=jnp.float32)

        def in_range(at, count, low_spot):
            spot = at + lax.broadcasted_iota(jnp.int32, (1, count), 1)
            return jnp.where((spot >= jnp.maximum(low, low_spot)) & (spot < last), 0.0, masked_low)

        def weigh(scores, now):
            return jnp.exp2((scores - now) * exponent_scale)

        def mix(weights, key_block):
            return jnp.dot(
                weights.astype(jnp.bfloat16),
                key_block[:, :kv_rank],
                preferred_element_type=jnp.float32,
            )

        def begin(key_block, at):
            own = own_keys[...]
            asked = lax.broadcasted_iota(jnp.int32, (tokens, tokens), 0)
            key = lax.broadcasted_iota(jnp.int32, (tokens, tokens), 1)
            seen = (asked % SAMPLES == key % SAMPLES) & (key // SAMPLES <= asked // SAMPLES)
            bias = jnp.where(seen, 0.0, masked_low)
            bias = jnp.broadcast_to(bias[None], (heads, tokens, tokens)).reshape(rows, tokens)
            new = score(own) + bias
            count = key_block.shape[0]
            old = score(key_block) + in_range(at, count, low)
            now = jnp.maximum(
                jnp.max(new, axis=1, keepdims=True), jnp.max(old, axis=1, keepdims=True)
            )
            new = weigh(new, now)
            old = weigh(old, now)
            top[...] = jnp.broadcast_to(now, (rows, LANES))
            lane = lax.broadcasted_iota(jnp.int32, (rows, LANES), 1)
            summed = jnp.where(lane == 0, jnp.sum(new, axis=1, keepdims=True), 0.0)
            for c in range(0, count, LANES):
                summed = summed + old[:, c : c + LANES]
            total[...] = summed
            acc[...] = mix(new, own) + mix(old, key_block)

        def fold(key_block, low_spot, at):
            count = key_block.shape[0]
            s = score(key_block)
            if low_spot is not None:
                s = s + in_range(at, count, low_spot)
            before = top[...]
            now = jnp.maximum(before, jnp.max(s, axis=1, keepdims=True))
            shrink = jnp.exp2((before - now) * exponent_scale)
            expo = weigh(s, over_lanes(now, count))
            top[...] = now
            summed = total[...] * shrink
            for c in range(0, count, LANES):
                summed = summed + expo[:, c : c + LANES]
            total[...] = summed
            acc[...] = acc[...] * over_lanes(shrink, kv_rank) + mix(expo, key_block)

        @pl.loop(0, chunks)
        def _(i):
            slot = jnp.where(i == 0, lax.rem(band, 2), 2 + lax.rem(i, 2))
            fetch(i).wait()

            @pl.when(i + 1 < chunks)
            def _():
                fetch(i + 1).start()

            nominal = first + i * KEY_BLOCK
            at = chunk_at(first, i)
            whole = (i > 0) & (nominal + KEY_BLOCK <= last)
            skip = (nominal - at) // EDGE_BLOCK

            @pl.when(i == 0)
            def _():
                here = pl.multiple_of(skip * EDGE_BLOCK, EDGE_BLOCK)
                begin(held[slot, pl.ds(here, EDGE_BLOCK), :], at + here)

            @pl.when(whole)
            def _():
                fold(held[slot], None, None)

            @pl.when(jnp.logical_not(whole))
            def _():
                begun = skip + jnp.where(i == 0, 1, 0)

                @pl.loop(begun, (jnp.minimum(last - at, KEY_BLOCK) + EDGE_BLOCK - 1) // EDGE_BLOCK)
                def _(j):
                    here = pl.multiple_of(j * EDGE_BLOCK, EDGE_BLOCK)
                    fold(held[slot, pl.ds(here, EDGE_BLOCK), :], nominal, at + here)

        norm = 1.0 / jnp.sum(total[...], axis=1, keepdims=True)
        lat[:, band_rows(band), :] = (
            (acc[...] * norm).astype(jnp.bfloat16).reshape(heads, tokens, kv_rank)
        )

        @pl.when(band == bands - 1)
        def _():
            load_up().wait()

            @pl.loop(0, heads)
            def _(head):
                ready[head] = jnp.dot(
                    lat[head], up[head], preferred_element_type=jnp.float32
                ).astype(jnp.bfloat16)

            done = pltpu.make_async_copy(ready, out_ref, up_sems.at[1])
            done.start()
            done.wait()


def shards(query_nope, query_rope, latent, up_key, value_up_weight, lengths, owner_request_table):
    seq_count = lax.axis_size("seq")
    tok_dev, head_dev, nope_dim = query_nope.shape[1:]
    rope_dim = query_rope.shape[2] // head_dev
    kv_rank = up_key.shape[1]
    width = kv_rank + rope_dim
    req_dev = owner_request_table.shape[0] // seq_count
    groups = owner_request_table.shape[0] // lengths.shape[0]
    band_tokens = tok_dev // req_dev
    exponent_scale = math.log2(math.e) / math.sqrt(nope_dim + rope_dim)

    keys, pair, queries, prefill_out = prefill_part(
        latent[0],
        query_nope[0].swapaxes(0, 1),
        query_rope[0],
        up_key,
        value_up_weight,
        lengths[None, :],
        seq_count,
        exponent_scale,
    )
    rows = head_dev * band_tokens
    attended = pl.pallas_call(
        functools.partial(decode_kernel, kv_rank, groups, exponent_scale),
        out_shape=jax.ShapeDtypeStruct(prefill_out.shape, jnp.bfloat16),
        grid_spec=pltpu.PrefetchScalarGridSpec(
            num_scalar_prefetch=2,
            grid=(req_dev,),
            in_specs=[
                pl.BlockSpec(memory_space=pl.ANY),
                pl.BlockSpec(memory_space=pl.ANY),
                pl.BlockSpec((band_tokens, width), lambda i, *_: (i, 0)),
                pl.BlockSpec(memory_space=pl.ANY),
                pl.BlockSpec(memory_space=pl.ANY),
            ],
            out_specs=pl.BlockSpec(memory_space=pl.ANY),
            scratch_shapes=[
                pltpu.VMEM((rows, kv_rank), jnp.float32),
                pltpu.VMEM((rows, LANES), jnp.float32),
                pltpu.VMEM((rows, LANES), jnp.float32),
                pltpu.VMEM((4, KEY_BLOCK, width), jnp.bfloat16),
                pltpu.VMEM((head_dev, tok_dev, kv_rank), jnp.bfloat16),
                pltpu.VMEM(value_up_weight.shape, jnp.bfloat16),
                pltpu.VMEM(prefill_out.shape, jnp.bfloat16),
                pltpu.VMEM((2, head_dev, band_tokens, width), jnp.bfloat16),
                pltpu.SemaphoreType.DMA((4,)),
                pltpu.SemaphoreType.DMA((2,)),
                pltpu.SemaphoreType.DMA((2,)),
            ],
        ),
        input_output_aliases={6: 0},
        compiler_params=pltpu.CompilerParams(vmem_limit_bytes=58 << 20),
    )(
        lengths,
        owner_request_table,
        queries,
        keys.reshape(-1, width),
        pair.reshape(-1, width),
        value_up_weight,
        prefill_out,
    )

    return attended.swapaxes(0, 1)[None]


def solution(mesh):
    in_specs = (
        P("section", "seq", "head", None),
        P("section", "seq", "head"),
        P("section", ("seq", "head"), None),
        P("head", None, None),
        P("head", None, None),
        P(),
        P(),
    )
    out_specs = P("section", "seq", "head", None)
    return jax.shard_map(shards, mesh=mesh, in_specs=in_specs, out_specs=out_specs, check_vma=False)
```

```python
import functools
import math

import jax
import jax.numpy as jnp
from jax import lax
from jax.experimental import pallas as pl
from jax.experimental.pallas import tpu as pltpu
from jax.sharding import PartitionSpec as P

SAMPLES = 8
STEPS = 4
BLOCK = 64

scale_top = 448.0
tiny_eps = 1e-06
masked_low = -1e30

KEY_BLOCK = 1024
EDGE_BLOCK = 512
FAR_HEADS = 8

CHAIN_STEPS = (0, 1, 3, 5)
ON_STEPS = (0, 2, 5, 8)
END_STEPS = (1, 3, 7, 10)
SIBLING_STEPS = (2, 5, 9, 13)
PAST_STEPS = (8, 10, 15)
LANES = 128


def prefill_kernel(
    z_count, y_count, kv_rank, exponent_scale, own_in, q_nope, q_rope, up_key, value_up, lengths,
    keys, own_out, q_out, out, block, nope, up, q, far_nope, far_rope, far_q, acc, top, total,
    held, bias, ready, far_send, far_recv,
    in_sems, out_sems, held_sems, x_send, x_recv, own_sems,
    z_send, z_recv, y_send, y_recv, sib_send, sib_recv,
):
    section = lax.axis_index("section")
    seq = lax.axis_index("seq")
    core = lax.axis_index("head")
    z = seq // (2 * y_count)
    y = seq // 2 % y_count
    hi = seq % 2
    half = z_count // 2
    heads, tokens, width = q.shape
    plane_blocks = 2 * y_count
    at_block = seq % plane_blocks
    plane_keys = plane_blocks * tokens
    nt = (((1,), (1,)), ((), ()))

    def plane_at(dz):
        return lax.rem(z + dz + z_count, z_count)

    def row_at(dy):
        return lax.rem(y + dy + y_count, y_count)

    def device(dz=0, dy=0, to_hi=None, to_section=None, to_core=None):
        th = hi if to_hi is None else to_hi
        return (
            section if to_section is None else to_section,
            (plane_at(dz) * y_count + row_at(dy)) * 2 + th,
            core if to_core is None else to_core,
        )

    loads = [
        pltpu.make_async_copy(q_nope, nope, in_sems.at[0]),
        pltpu.make_async_copy(up_key, up, in_sems.at[1]),
    ]
    for load in loads:
        load.start()

    barrier = pltpu.get_barrier_semaphore()
    peers = [
        device(to_core=1 - core),
        device(to_section=1 - section),
        device(to_hi=1 - hi),
        device(to_section=1 - section, to_hi=1 - hi),
        device(dz=1),
        device(dz=-1),
        device(dy=1),
        device(dy=-1),
    ]
    for peer in peers:
        pl.semaphore_signal(barrier, inc=1, device_id=peer, device_id_type=pl.DeviceIdType.MESH)

    @pl.when(section == 0)
    def _():
        rows = own_in[...].astype(jnp.float32)
        largest = jnp.max(jnp.abs(rows))
        spread = jnp.full((8, LANES), largest, jnp.float32)
        scale = ((spread + tiny_eps) / scale_top).astype(jnp.bfloat16).astype(jnp.float32)
        factor = scale[:1, :1]
        stored = (rows / factor).astype(jnp.bfloat16)
        block[...] = (stored.astype(jnp.float32) * factor).astype(jnp.bfloat16)

    @pl.when(section == 1)
    def _():
        block[...] = own_in[...]

    pl.semaphore_wait(barrier, len(peers))

    def remote(src, dst, to, send_sem, recv_sem):
        return pltpu.make_async_remote_copy(
            src_ref=src,
            dst_ref=dst,
            send_sem=send_sem,
            recv_sem=recv_sem,
            device_id=to,
            device_id_type=pl.DeviceIdType.MESH,
        )

    def arrive(dst, recv_sem):
        remote(dst, dst, device(to_core=1 - core), recv_sem, recv_sem).wait_recv()

    def own_local():
        return pltpu.make_async_copy(block, own_out.at[core], own_sems.at[0])

    def own_away():
        to = device(to_core=1 - core)
        return remote(block, own_out.at[core], to, own_sems.at[1], own_sems.at[2])

    def x_copies():
        spot = keys.at[z, y, hi, core]
        return [
            remote(block, spot, device(to_hi=1 - hi), x_send.at[2], x_recv.at[1]),
            remote(block, spot, device(to_section=1), x_send.at[0], x_recv.at[0]),
            remote(block, spot, device(to_section=1, to_hi=1 - hi), x_send.at[1], x_recv.at[1]),
        ]

    def x_local():
        return pltpu.make_async_copy(block, keys.at[z, y, hi, core], x_send.at[3])

    @pl.when(section == 0)
    def _():
        x_local().start()
        for copy in x_copies():
            copy.start()

    own_local().start()
    own_away().start()

    for load in loads:
        load.wait()

    near = heads - FAR_HEADS
    half_lanes = LANES // 2

    def far_copies():
        to = device(to_section=1 - section)
        rope_part = q_rope.at[:, pl.ds(near * half_lanes, FAR_HEADS * half_lanes)]
        return [
            remote(nope.at[pl.ds(near, FAR_HEADS)], far_nope, to, far_send.at[0], far_recv.at[0]),
            remote(rope_part, far_rope, to, far_send.at[1], far_recv.at[1]),
        ]

    def far_result():
        part = ready.at[pl.ds(near, FAR_HEADS)]
        return remote(part, part, device(to_section=1 - section), far_send.at[2], far_recv.at[2])

    @pl.when(section == 0)
    def _():
        for copy in far_copies():
            copy.start()

    def absorb(from_nope, from_rope, into, first, count):
        @pl.loop(0, count // 2)
        def _(pair):
            rope = from_rope[:, pl.ds(pl.multiple_of(pair * LANES, LANES), LANES)]
            for side in range(2):
                head = pair * 2 + side
                lifted = lax.dot_general(
                    from_nope[head], up[first + head], nt, preferred_element_type=jnp.float32
                )
                into[head, :, :kv_rank] = lifted.astype(jnp.bfloat16)
                into[head, :, kv_rank:] = rope[:, side * half_lanes : (side + 1) * half_lanes]

    @pl.when(section == 0)
    def _():
        absorb(nope, q_rope, q, 0, near)

    @pl.when(section == 1)
    def _():
        absorb(nope, q_rope, q, 0, heads)

    def load_value_up():
        return pltpu.make_async_copy(value_up, up, in_sems.at[1])

    @pl.when(section == 0)
    def _():
        load_value_up().start()

    @pl.when(section == 1)
    def _():
        pltpu.make_async_copy(q, q_out, out_sems.at[0]).start()

    @pl.when(section == 0)
    def _():
        x_local().wait()
        arrive(keys.at[z, y, 1 - hi, core], x_recv.at[1])

    @pl.when(section == 1)
    def _():
        arrive(keys.at[z, y, hi, core], x_recv.at[0])
        arrive(keys.at[z, y, 1 - hi, core], x_recv.at[1])

    low, high, far = row_at(-1), row_at(1), row_at(2)
    columns = [y, low, high, far]
    planes = [z]
    for s in range(1, half):
        planes += [plane_at(-s), plane_at(s)]
    planes.append(plane_at(half))
    steps = [[0]] + [[2 * s - 1, 2 * s] for s in range(1, half)] + [[z_count - 1]]

    def sender(went):
        def send(src, to, send_sem, recv_sem):
            copy = lambda: remote(src(), src(), to(), send_sem(), recv_sem())
            went.append(copy)
            copy().start()

        return send

    went = [[], [], []]

    def along_y(send, n, c, src, d, k):
        send(src, lambda: device(dy=d), lambda: y_send.at[n, k], lambda: y_recv.at[n, k])

    def spread(send, n, c):
        mine = lambda: keys.at[planes[n], y, :, c]
        along_y(send, n, c, mine, 1, 0)
        along_y(send, n, c, mine, -1, 1)

    def spread_on(send, n, c):
        arrive(keys.at[planes[n], low, :, c], y_recv.at[n, 0])
        along_y(send, n, c, lambda: keys.at[planes[n], low, 0, c], 1, 2)
        arrive(keys.at[planes[n], high, :, c], y_recv.at[n, 1])
        along_y(send, n, c, lambda: keys.at[planes[n], high, 1, c], -1, 3)

    def spread_end(n, c):
        arrive(keys.at[planes[n], far, 0, c], y_recv.at[n, 2])
        arrive(keys.at[planes[n], far, 1, c], y_recv.at[n, 3])

    def to_sibling(send, n, c):
        send(
            lambda: keys.at[planes[n], :, :, c],
            lambda: device(to_core=1 - c),
            lambda: sib_send.at[n],
            lambda: sib_recv.at[n],
        )

    def along_z(send, src, up_way, step, k):
        d, j = (1, 0) if up_way else (-1, 1)
        send(
            src,
            lambda: device(dz=d),
            lambda: z_send.at[j, step, k],
            lambda: z_recv.at[j, step, k],
        )

    ways = ((0, True), (1, False))

    def decode_a(stage):
        send = sender(went[1])

        def cell(n, k):
            return lambda: keys.at[planes[n], columns[k], :, 0]

        def column(k):
            for _, up_way in ways:
                along_z(send, cell(0, k), up_way, 0, k)

        if stage == 0:
            spread(send, 0, 0)
            column(0)
            arrive(keys.at[z, low, :, 0], y_recv.at[0, 0])
            along_y(send, 0, 0, lambda: keys.at[z, low, 0, 0], 1, 2)
            column(1)
            arrive(keys.at[z, high, :, 0], y_recv.at[0, 1])
            along_y(send, 0, 0, lambda: keys.at[z, high, 1, 0], -1, 3)
            column(2)
            spread_end(0, 0)
            column(3)
            to_sibling(send, 0, 0)
        elif stage < half:
            for k in range(y_count):
                for n, (j, up_way) in zip(steps[stage], ways):
                    arrive(cell(n, k)(), z_recv.at[j, stage - 1, k])
                    if stage < half - 1 or k // 2 == j:
                        along_z(send, cell(n, k), up_way, stage, k)
            for n in steps[stage]:
                to_sibling(send, n, 0)
        else:
            for k in range(y_count):
                arrive(cell(z_count - 1, k)(), z_recv.at[k // 2, half - 1, k])
            to_sibling(send, z_count - 1, 0)

    def decode_b(stage):
        send = sender(went[2])

        def ahead(n, s, j, up_way):
            if s < half - 1:
                part = lambda: keys.at[planes[n], y, :, 1]
            else:
                part = lambda: keys.at[planes[n], y, j, 1]
            along_z(send, part, up_way, s, 0)

        def chain(s):
            for n, (j, up_way) in zip(steps[s], ways):
                arrive(keys.at[planes[n], y, :, 1], z_recv.at[j, s - 1, 0])
                ahead(n, s, j, up_way)
                spread(send, n, 1)

        def finish(s):
            for n in steps[s]:
                spread_end(n, 1)
                to_sibling(send, n, 1)

        if stage == 0:
            for j, up_way in ways:
                ahead(0, 0, j, up_way)
            spread(send, 0, 1)
            chain(1)
            spread_on(send, 0, 1)
            return
        if stage + 1 < half:
            chain(stage + 1)
        elif stage + 1 == half:
            for j in range(2):
                arrive(keys.at[planes[-1], y, j, 1], z_recv.at[j, half - 1, 0])
            spread(send, z_count - 1, 1)
        for n in steps[stage]:
            spread_on(send, n, 1)
        finish(stage - 1)
        if stage == half:
            finish(stage)

    behind = [0] + [2 * s - 1 for s in range(1, half)] + [z_count - 1]
    past = planes[2 * (half - 1)]
    forward = sender(went[0])

    def ahead(n, s):
        along_z(forward, lambda: keys.at[planes[n], y, :, core], True, s, 0)

    def prefill_start():
        ahead(0, 0)
        spread(forward, 0, core)
        prefill_chain(1)
        spread_on(forward, 0, core)
        spread_end(0, core)
        to_sibling(forward, 0, core)
        prefill_on(1)
        from_sibling(0)

    def prefill_chain(s):
        n = behind[s]
        arrive(keys.at[planes[n], y, :, core], z_recv.at[0, s - 1, 0])
        if s < half:
            ahead(n, s)
        else:
            along_z(forward, lambda: keys.at[planes[n], y, 1, core], True, 0, 1)
        spread(forward, n, core)

    def prefill_on(s):
        spread_on(forward, behind[s], core)

    def prefill_end(s):
        spread_end(behind[s], core)
        to_sibling(forward, behind[s], core)

    def prefill_past():
        arrive(keys.at[past, y, 1, core], z_recv.at[0, 0, 1])
        n = 2 * (half - 1)
        along_y(forward, n, core, lambda: keys.at[past, y, 1, core], 1, 0)

    def prefill_past_end():
        n = 2 * (half - 1)
        spot = lambda: keys.at[past, low, 1, core]
        arrive(spot(), y_recv.at[n, 0])
        forward(
            spot,
            lambda: device(to_core=1 - core),
            lambda: sib_send.at[n],
            lambda: sib_recv.at[n],
        )

    def from_sibling(n):
        arrive(keys.at[planes[n], :, :, 1 - core], sib_recv.at[n])

    def on(at, event):
        @pl.when(at)
        def _():
            event()

    top[...] = jnp.full(top.shape, masked_low, jnp.float32)
    total[...] = jnp.zeros(total.shape, jnp.float32)
    acc[...] = jnp.zeros(acc.shape, jnp.float32)

    token = lax.broadcasted_iota(jnp.int32, (tokens, 1), 0)
    position = seq * tokens + token
    count = lengths.shape[1]
    before_it = lax.broadcasted_iota(jnp.int32, (count, count), 0) < lax.broadcasted_iota(
        jnp.int32, (count, count), 1
    )
    earlier = jnp.where(before_it, 1.0, 0.0).astype(jnp.bfloat16)
    wide = jnp.broadcast_to(lengths[...], (8, count))
    digits = [(wide // 64).astype(jnp.bfloat16), (wide % 64).astype(jnp.bfloat16)]
    upper, lower = [jnp.dot(d, earlier, preferred_element_type=jnp.float32) for d in digits]
    starts = (upper * 64.0 + lower)[:1]
    row_low = jnp.max(
        jnp.where(starts <= position.astype(jnp.float32), starts, 0.0), axis=1, keepdims=True
    ).astype(jnp.int32)

    chunk = plane_keys // 2
    tile_heads = near // 2

    def fold(asked_heads, tile, key_block):
        count = key_block.shape[0]
        tile_heads = asked_heads.shape[0]
        rows = tile_heads * tokens
        part = pl.ds(pl.multiple_of(tile * rows, rows), rows)
        asked = asked_heads[...].reshape(rows, width)
        s = lax.dot_general(asked, key_block, nt, preferred_element_type=jnp.float32)
        s = (s.reshape(tile_heads, tokens, count) + bias[:, :count][None]).reshape(rows, count)
        before = top[part, :]
        now = jnp.maximum(before, jnp.max(s, axis=1, keepdims=True))
        shrink = jnp.exp2((before - now) * exponent_scale)
        expo = jnp.exp2((s - over_lanes(now, count)) * exponent_scale)
        top[part, :] = now
        summed = total[part, :] * shrink
        for c in range(0, count, LANES):
            summed = summed + expo[:, c : c + LANES]
        total[part, :] = summed
        acc[part, :] = acc[part, :] * over_lanes(shrink, kv_rank) + jnp.dot(
            expo.astype(jnp.bfloat16),
            key_block[:, :kv_rank],
            preferred_element_type=jnp.float32,
        )

    def past_from_sibling():
        arrive(keys.at[past, low, 1, 1 - core], sib_recv.at[2 * (half - 1)])

    last_step = 4 * (half + 1)
    timetable = [
        (prefill_chain, CHAIN_STEPS),
        (prefill_on, ON_STEPS),
        (prefill_end, END_STEPS),
        (lambda s: from_sibling(behind[s]), SIBLING_STEPS),
    ]
    events = {0: [prefill_start]}
    for s in range(1, half + 1):
        for event, at_steps in timetable:
            if at_steps[s - 1] > 0:
                spot = events.setdefault(at_steps[s - 1], [])
                spot.append(functools.partial(event, s))
    for event, at_step in zip((prefill_past, prefill_past_end, past_from_sibling), PAST_STEPS):
        events.setdefault(at_step, []).append(event)

    @pl.when(section == 0)
    def _():
        mid = plane_blocks // 2
        at_first, at_mid = at_block == 0, at_block == mid
        reaches_past = at_first & (z > half)

        @pl.loop(0, last_step)
        def _(step):
            for at_step in sorted(events):
                for event in events[at_step]:
                    on(step == at_step, event)

            run = step // 2
            turn = step % 2
            rest = run == 2 * half + 1
            back = jnp.where(rest, 0, (run + 1) // 2)
            side = jnp.where(run == 0, 0, (run + 1) % 2)
            side = jnp.where(rest, 1, side)
            slot = jnp.where(rest, 1, back % 2)
            reached = z >= back

            def load(back, part, slot, into):
                plane = lax.rem(z - back + z_count, z_count)
                here = keys.at[plane, pl.ds(part * (y_count // 2), y_count // 2)]
                return pltpu.make_async_copy(here, held.at[slot, into], held_sems.at[slot, into])

            def load_first():
                return pltpu.make_async_copy(
                    keys.at[past, y_count - 1, 1], held.at[1, 0, 0, 0], held_sems.at[1, 0]
                )

            def load_mid():
                return pltpu.make_async_copy(
                    keys.at[planes[-1], y_count // 2 - 1, 1],
                    held.at[1, 1, y_count // 2 - 1, 1],
                    held_sems.at[1, 0],
                )

            @pl.when(step == 0)
            def _():
                load(0, 0, 0, 0).start()

            for s in range(1, half + 1):

                @pl.when((step == SIBLING_STEPS[s - 1]) & (z >= s))
                def _():
                    load(s, 0, s % 2, 0).start()
                    load(s, 1, s % 2, 1).start()

            @pl.when(step == last_step - 5)
            def _():
                @pl.when(reaches_past)
                def _():
                    load_first().start()

                @pl.when(at_block >= mid)
                def _():
                    rest_load = load(0, 1, 1, 1)
                    rest_load.start()
                    rest_load.wait()

                @pl.when(at_mid)
                def _():
                    load_mid().start()

            @pl.when(reached & (turn == 0) & jnp.logical_not(rest))
            def _():
                load(back, side, slot, side).wait()

            at_past = reaches_past & (run == 2 * half)

            @pl.when(at_past & (turn == 0))
            def _():
                load_first().wait()

            @pl.when((turn == 0) & rest & at_mid)
            def _():
                load_mid().wait()

            none = (rest & (at_block < mid)) | ((run == 2 * half - 1) & (at_block >= mid))
            first_spot = (z - back) * plane_keys + side * chunk

            @pl.when(reached & jnp.logical_not(none))
            def _():
                @pl.when(turn == 0)
                def _():
                    lane = lax.broadcasted_iota(jnp.int32, (1, chunk + tokens), 1)
                    spot = first_spot + lane
                    shift = (half * plane_keys) + chunk
                    spot = jnp.where(
                        rest & at_mid & (lane >= chunk - tokens), spot - shift, spot
                    )
                    spot = jnp.where(lane >= chunk, spot - plane_keys - tokens, spot)
                    seen = (spot >= row_low) & (spot <= position)
                    bias[...] = jnp.where(seen, 0.0, masked_low)

                here = held.at[slot, side]
                tile_q = q.at[pl.ds(turn * tile_heads, tile_heads)]

                @pl.when(at_past)
                def _():
                    behind_it = held[1, 0, 0, 0].reshape(tokens, width)
                    key_block = jnp.concatenate([here[...].reshape(chunk, width), behind_it])

                    fold(tile_q, turn, key_block)

                @pl.when(jnp.logical_not(at_past))
                def _():
                    fold(tile_q, turn, here[...].reshape(chunk, width))

    def far_run(run):
        rest, beyond = run == 2 * half + 1, run == 2 * half + 2
        back = jnp.where(rest, 0, jnp.where(beyond, half + 1, (run + 1) // 2))
        side = jnp.where(run == 0, 0, jnp.where(rest | beyond, 1, (run + 1) % 2))
        slot = run % 2
        middle = plane_blocks // 2
        wanted = z >= back
        wanted = wanted & jnp.logical_not(rest & (at_block < middle))
        wanted = wanted & jnp.logical_not((run == 2 * half - 1) & (at_block > middle))
        wanted = wanted & jnp.logical_not(beyond & (at_block > 0))
        plane = lax.rem(z - back + z_count, z_count)
        load = pltpu.make_async_copy(
            keys.at[plane, pl.ds(side * (y_count // 2), y_count // 2)],
            held.at[slot, 0],
            held_sems.at[slot, 0],
        )
        return wanted, load, (z - back) * plane_keys + side * chunk, slot

    def start_far(run):
        wanted, load, _, _ = far_run(run)

        @pl.when(wanted)
        def _():
            load.start()

    def far_runs(begin, end):
        start_far(jnp.int32(begin))

        @pl.loop(begin, end)
        def _(run):
            @pl.when(run + 1 < end)
            def _():
                start_far(run + 1)

            wanted, load, first_spot, slot = far_run(run)

            @pl.when(wanted)
            def _():
                load.wait()
                spot = first_spot + lax.broadcasted_iota(jnp.int32, (1, chunk), 1)
                seen = (spot >= row_low) & (spot <= position)
                bias[:, :chunk] = jnp.where(seen, 0.0, masked_low)
                fold(far_q, 0, held[slot, 0].reshape(chunk, width))

    def project(head, part):
        norm = 1.0 / jnp.sum(total[part, :], axis=1, keepdims=True)
        mixed = (acc[part, :] * norm).astype(jnp.bfloat16)
        ready[head] = jnp.dot(mixed, up[head], preferred_element_type=jnp.float32).astype(
            jnp.bfloat16
        )

    @pl.when(section == 1)
    def _():
        for stage in range(half + 1):
            on(core == 0, functools.partial(decode_a, stage))
            on(core == 1, functools.partial(decode_b, stage))
            if stage == 1:
                arrive(far_nope, far_recv.at[0])
                arrive(far_rope, far_recv.at[1])
                absorb(far_nope, far_rope, far_q, near, FAR_HEADS)
                load_value_up().start()
            if 0 < stage < half:
                for n in steps[stage - 1]:
                    from_sibling(n)
                far_runs(max(2 * stage - 3, 0), 2 * stage - 1)
        for n in steps[half - 1] + steps[half]:
            from_sibling(n)
        far_runs(2 * half - 3, 2 * half + 3)
        load_value_up().wait()

        @pl.loop(0, FAR_HEADS)
        def _(head):
            project(near + head, pl.ds(pl.multiple_of(head * tokens, tokens), tokens))

        far_result().start()

    @pl.when(section == 0)
    def _():
        load_value_up().wait()

        @pl.loop(0, near)
        def _(head):
            project(head, pl.ds(pl.multiple_of(head * tokens, tokens), tokens))

        arrive(ready.at[pl.ds(near, FAR_HEADS)], far_recv.at[2])
        done = pltpu.make_async_copy(ready, out, out_sems.at[1])
        done.start()
        done.wait()
        for copy in x_copies() + far_copies():
            copy.wait_send()

    @pl.when(section == 1)
    def _():
        pltpu.make_async_copy(q, q_out, out_sems.at[0]).wait()
        far_result().wait_send()

    groups = [section == 0, (section == 1) & (core == 0), (section == 1) & (core == 1)]
    for group, copies in zip(groups, went):

        @pl.when(group)
        def _():
            for copy in copies:
                copy().wait_send()

    arrive(own_out.at[1 - core], own_sems.at[2])
    own_away().wait_send()
    own_local().wait()


def prefill_part(own, q_nope, q_rope, up_key, value_up, lengths, seq_count, exponent_scale):
    rows, width = own.shape
    heads, tokens, _ = q_nope.shape
    kv_rank = up_key.shape[1]
    y_count = 4
    z_count = seq_count // (2 * y_count)
    dma = pltpu.SemaphoreType.DMA
    bf16 = own.dtype
    chunk = y_count * tokens
    vmem = pl.BlockSpec(memory_space=pltpu.VMEM)
    hbm = pl.BlockSpec(memory_space=pl.ANY)
    return pl.pallas_call(
        functools.partial(prefill_kernel, z_count, y_count, kv_rank, exponent_scale),
        out_shape=[
            jax.ShapeDtypeStruct((z_count, y_count, 2, 2, rows, width), bf16),
            jax.ShapeDtypeStruct((2, rows, width), bf16),
            jax.ShapeDtypeStruct((heads, tokens, width), bf16),
            jax.ShapeDtypeStruct((heads, tokens, value_up.shape[2]), bf16),
        ],
        in_specs=[vmem, hbm, vmem, hbm, hbm, vmem],
        out_specs=[hbm] * 4,
        scratch_shapes=[
            pltpu.VMEM((rows, width), bf16),
            pltpu.VMEM(q_nope.shape, bf16),
            pltpu.VMEM(up_key.shape, bf16),
            pltpu.VMEM((heads, tokens, width), bf16),
            pltpu.VMEM((FAR_HEADS,) + q_nope.shape[1:], bf16),
            pltpu.VMEM((tokens, FAR_HEADS * (width - kv_rank)), bf16),
            pltpu.VMEM((FAR_HEADS, tokens, width), bf16),
            pltpu.VMEM(((heads - FAR_HEADS) * tokens, kv_rank), jnp.float32),
            pltpu.VMEM(((heads - FAR_HEADS) * tokens, LANES), jnp.float32),
            pltpu.VMEM(((heads - FAR_HEADS) * tokens, LANES), jnp.float32),
            pltpu.VMEM((2, 2, y_count // 2, 2, 2, rows, width), bf16),
            pltpu.VMEM((tokens, chunk + tokens), jnp.float32),
            pltpu.VMEM((heads, tokens, value_up.shape[2]), bf16),
            dma((3,)),
            dma((3,)),
            dma((2,)),
            dma((2,)),
            dma((2, 2)),
            dma((4,)),
            dma((2,)),
            dma((3,)),
            dma((2, z_count // 2, y_count)),
            dma((2, z_count // 2, y_count)),
            dma((z_count, 4)),
            dma((z_count, 4)),
            dma((z_count,)),
            dma((z_count,)),
        ],
        compiler_params=pltpu.CompilerParams(
            collective_id=0, has_side_effects=True, vmem_limit_bytes=56 << 20
        ),
    )(own, q_nope, q_rope, up_key, value_up, lengths)


def over_lanes(value, width):
    return jnp.concatenate([value] * (width // LANES), axis=1)


def decode_kernel(
    kv_rank,
    groups,
    exponent_scale,
    lengths,
    table,
    q_ref,
    keys,
    own_keys,
    value_up,
    _,
    out_ref,
    acc,
    top,
    total,
    held,
    lat,
    up,
    ready,
    q_held,
    sems,
    q_sems,
    up_sems,
):
    band = pl.program_id(0)
    bands = pl.num_programs(0)
    _, heads, tokens, width = q_held.shape
    rows = heads * tokens
    all_keys = keys.shape[0]
    nt = (((1,), (1,)), ((), ()))

    @pl.when(lax.axis_index("section") == 1)
    def _():
        def prompt_range(which):
            prompt = table[lax.axis_index("seq") * bands + which] // groups
            low = lax.fori_loop(0, prompt, lambda k, at: at + lengths[k], jnp.int32(0))
            return low, low + lengths[prompt]

        def chunk_at(start, i):
            return pl.multiple_of(jnp.minimum(start + i * KEY_BLOCK, all_keys - KEY_BLOCK), 16)

        def fetch_from(start, i, slot):
            return pltpu.make_async_copy(
                keys.at[pl.ds(chunk_at(start, i), KEY_BLOCK), :], held.at[slot], sems.at[slot]
            )

        def band_rows(which):
            return pl.ds(pl.multiple_of(which * tokens, tokens), tokens)

        def fetch_q(which):
            slot = lax.rem(which, 2)
            return pltpu.make_async_copy(
                q_ref.at[:, band_rows(which), :], q_held.at[slot], q_sems.at[slot]
            )

        def load_up():
            return pltpu.make_async_copy(value_up, up, up_sems.at[0])

        low, last = prompt_range(band)
        first = low // 16 * 16
        chunks = (last - first + KEY_BLOCK - 1) // KEY_BLOCK

        def fetch(i):
            slot = jnp.where(i == 0, lax.rem(band, 2), 2 + lax.rem(i, 2))
            return fetch_from(first, i, slot)

        @pl.when(band == 0)
        def _():
            fetch_q(0).start()
            fetch(0).start()
            load_up().start()

        @pl.when(band + 1 < bands)
        def _():
            fetch_q(band + 1).start()
            next_low, _ = prompt_range(band + 1)
            fetch_from(next_low // 16 * 16, 0, lax.rem(band + 1, 2)).start()

        fetch_q(band).wait()
        q = q_held[lax.rem(band, 2)].reshape(rows, width)
        def score(key_block):
            return lax.dot_general(q, key_block, nt, preferred_element_type=jnp.float32)

        def in_range(at, count, low_spot):
            spot = at + lax.broadcasted_iota(jnp.int32, (1, count), 1)
            return jnp.where((spot >= jnp.maximum(low, low_spot)) & (spot < last), 0.0, masked_low)

        def weigh(scores, now):
            return jnp.exp2((scores - now) * exponent_scale)

        def mix(weights, key_block):
            return jnp.dot(
                weights.astype(jnp.bfloat16),
                key_block[:, :kv_rank],
                preferred_element_type=jnp.float32,
            )

        def begin(key_block, at):
            own = own_keys[...]
            asked = lax.broadcasted_iota(jnp.int32, (tokens, tokens), 0)
            key = lax.broadcasted_iota(jnp.int32, (tokens, tokens), 1)
            seen = (asked % SAMPLES == key % SAMPLES) & (key // SAMPLES <= asked // SAMPLES)
            bias = jnp.where(seen, 0.0, masked_low)
            bias = jnp.broadcast_to(bias[None], (heads, tokens, tokens)).reshape(rows, tokens)
            new = score(own) + bias
            count = key_block.shape[0]
            old = score(key_block) + in_range(at, count, low)
            now = jnp.maximum(
                jnp.max(new, axis=1, keepdims=True), jnp.max(old, axis=1, keepdims=True)
            )
            new = weigh(new, now)
            old = weigh(old, now)
            top[...] = jnp.broadcast_to(now, (rows, LANES))
            lane = lax.broadcasted_iota(jnp.int32, (rows, LANES), 1)
            summed = jnp.where(lane == 0, jnp.sum(new, axis=1, keepdims=True), 0.0)
            for c in range(0, count, LANES):
                summed = summed + old[:, c : c + LANES]
            total[...] = summed
            acc[...] = mix(new, own) + mix(old, key_block)

        def fold(key_block, low_spot, at):
            count = key_block.shape[0]
            s = score(key_block)
            if low_spot is not None:
                s = s + in_range(at, count, low_spot)
            before = top[...]
            now = jnp.maximum(before, jnp.max(s, axis=1, keepdims=True))
            shrink = jnp.exp2((before - now) * exponent_scale)
            expo = weigh(s, over_lanes(now, count))
            top[...] = now
            summed = total[...] * shrink
            for c in range(0, count, LANES):
                summed = summed + expo[:, c : c + LANES]
            total[...] = summed
            acc[...] = acc[...] * over_lanes(shrink, kv_rank) + mix(expo, key_block)

        @pl.loop(0, chunks)
        def _(i):
            slot = jnp.where(i == 0, lax.rem(band, 2), 2 + lax.rem(i, 2))
            fetch(i).wait()

            @pl.when(i + 1 < chunks)
            def _():
                fetch(i + 1).start()

            nominal = first + i * KEY_BLOCK
            at = chunk_at(first, i)
            whole = (i > 0) & (nominal + KEY_BLOCK <= last)
            skip = (nominal - at) // EDGE_BLOCK

            @pl.when(i == 0)
            def _():
                here = pl.multiple_of(skip * EDGE_BLOCK, EDGE_BLOCK)
                begin(held[slot, pl.ds(here, EDGE_BLOCK), :], at + here)

            @pl.when(whole)
            def _():
                fold(held[slot], None, None)

            @pl.when(jnp.logical_not(whole))
            def _():
                begun = skip + jnp.where(i == 0, 1, 0)

                @pl.loop(begun, (jnp.minimum(last - at, KEY_BLOCK) + EDGE_BLOCK - 1) // EDGE_BLOCK)
                def _(j):
                    here = pl.multiple_of(j * EDGE_BLOCK, EDGE_BLOCK)
                    fold(held[slot, pl.ds(here, EDGE_BLOCK), :], nominal, at + here)

        norm = 1.0 / jnp.sum(total[...], axis=1, keepdims=True)
        lat[:, band_rows(band), :] = (
            (acc[...] * norm).astype(jnp.bfloat16).reshape(heads, tokens, kv_rank)
        )

        @pl.when(band == bands - 1)
        def _():
            load_up().wait()

            @pl.loop(0, heads)
            def _(head):
                ready[head] = jnp.dot(
                    lat[head], up[head], preferred_element_type=jnp.float32
                ).astype(jnp.bfloat16)

            done = pltpu.make_async_copy(ready, out_ref, up_sems.at[1])
            done.start()
            done.wait()


def shards(query_nope, query_rope, latent, up_key, value_up_weight, lengths, owner_request_table):
    seq_count = lax.axis_size("seq")
    tok_dev, head_dev, nope_dim = query_nope.shape[1:]
    rope_dim = query_rope.shape[2] // head_dev
    kv_rank = up_key.shape[1]
    width = kv_rank + rope_dim
    req_dev = owner_request_table.shape[0] // seq_count
    groups = owner_request_table.shape[0] // lengths.shape[0]
    band_tokens = tok_dev // req_dev
    exponent_scale = math.log2(math.e) / math.sqrt(nope_dim + rope_dim)

    keys, pair, queries, prefill_out = prefill_part(
        latent[0],
        query_nope[0].swapaxes(0, 1),
        query_rope[0],
        up_key,
        value_up_weight,
        lengths[None, :],
        seq_count,
        exponent_scale,
    )
    rows = head_dev * band_tokens
    attended = pl.pallas_call(
        functools.partial(decode_kernel, kv_rank, groups, exponent_scale),
        out_shape=jax.ShapeDtypeStruct(prefill_out.shape, jnp.bfloat16),
        grid_spec=pltpu.PrefetchScalarGridSpec(
            num_scalar_prefetch=2,
            grid=(req_dev,),
            in_specs=[
                pl.BlockSpec(memory_space=pl.ANY),
                pl.BlockSpec(memory_space=pl.ANY),
                pl.BlockSpec((band_tokens, width), lambda i, *_: (i, 0)),
                pl.BlockSpec(memory_space=pl.ANY),
                pl.BlockSpec(memory_space=pl.ANY),
            ],
            out_specs=pl.BlockSpec(memory_space=pl.ANY),
            scratch_shapes=[
                pltpu.VMEM((rows, kv_rank), jnp.float32),
                pltpu.VMEM((rows, LANES), jnp.float32),
                pltpu.VMEM((rows, LANES), jnp.float32),
                pltpu.VMEM((4, KEY_BLOCK, width), jnp.bfloat16),
                pltpu.VMEM((head_dev, tok_dev, kv_rank), jnp.bfloat16),
                pltpu.VMEM(value_up_weight.shape, jnp.bfloat16),
                pltpu.VMEM(prefill_out.shape, jnp.bfloat16),
                pltpu.VMEM((2, head_dev, band_tokens, width), jnp.bfloat16),
                pltpu.SemaphoreType.DMA((4,)),
                pltpu.SemaphoreType.DMA((2,)),
                pltpu.SemaphoreType.DMA((2,)),
            ],
        ),
        input_output_aliases={6: 0},
        compiler_params=pltpu.CompilerParams(vmem_limit_bytes=58 << 20),
    )(
        lengths,
        owner_request_table,
        queries,
        keys.reshape(-1, width),
        pair.reshape(-1, width),
        value_up_weight,
        prefill_out,
    )

    return attended.swapaxes(0, 1)[None]


def solution(mesh):
    in_specs = (
        P("section", "seq", "head", None),
        P("section", "seq", "head"),
        P("section", ("seq", "head"), None),
        P("head", None, None),
        P("head", None, None),
        P(),
        P(),
    )
    out_specs = P("section", "seq", "head", None)
    return jax.shard_map(shards, mesh=mesh, in_specs=in_specs, out_specs=out_specs, check_vma=False)
```

```python
import functools
import math

import jax
import jax.numpy as jnp
from jax import lax
from jax.experimental import pallas as pl
from jax.experimental.pallas import tpu as pltpu
from jax.sharding import PartitionSpec as P

SAMPLES = 8
STEPS = 4
BLOCK = 64

scale_top = 448.0
tiny_eps = 1e-06
masked_low = -1e30

KEY_BLOCK = 1024
EDGE_BLOCK = 512
FAR_HEADS = 6

CHAIN_STEPS = (0, 1, 3, 5)
ON_STEPS = (0, 2, 5, 8)
END_STEPS = (1, 3, 7, 10)
SIBLING_STEPS = (2, 5, 9, 13)
PAST_STEPS = (8, 10, 15)
LANES = 128


def prefill_kernel(
    z_count, y_count, kv_rank, exponent_scale, own_in, q_nope, q_rope, up_key, value_up, lengths,
    keys, own_out, q_out, out, block, raw, nope, up, q, far_nope, far_rope, far_q, acc, top, total,
    held, bias, ready, far_send, far_recv,
    in_sems, out_sems, held_sems, x_send, x_recv, own_sems,
    z_send, z_recv, y_send, y_recv, sib_send, sib_recv,
):
    section = lax.axis_index("section")
    seq = lax.axis_index("seq")
    core = lax.axis_index("head")
    z = seq // (2 * y_count)
    y = seq // 2 % y_count
    hi = seq % 2
    half = z_count // 2
    heads, tokens, width = q.shape
    plane_blocks = 2 * y_count
    at_block = seq % plane_blocks
    plane_keys = plane_blocks * tokens
    nt = (((1,), (1,)), ((), ()))

    def plane_at(dz):
        return lax.rem(z + dz + z_count, z_count)

    def row_at(dy):
        return lax.rem(y + dy + y_count, y_count)

    def device(dz=0, dy=0, to_hi=None, to_section=None, to_core=None):
        th = hi if to_hi is None else to_hi
        return (
            section if to_section is None else to_section,
            (plane_at(dz) * y_count + row_at(dy)) * 2 + th,
            core if to_core is None else to_core,
        )

    loads = [
        pltpu.make_async_copy(q_nope, raw, in_sems.at[0]),
        pltpu.make_async_copy(up_key, up, in_sems.at[1]),
    ]
    for load in loads:
        load.start()

    barrier = pltpu.get_barrier_semaphore()
    peers = [
        device(to_core=1 - core),
        device(to_section=1 - section),
        device(to_hi=1 - hi),
        device(to_section=1 - section, to_hi=1 - hi),
        device(dz=1),
        device(dz=-1),
        device(dy=1),
        device(dy=-1),
    ]
    for peer in peers:
        pl.semaphore_signal(barrier, inc=1, device_id=peer, device_id_type=pl.DeviceIdType.MESH)

    @pl.when(section == 0)
    def _():
        rows = own_in[...].astype(jnp.float32)
        largest = jnp.max(jnp.abs(rows))
        spread = jnp.full((8, LANES), largest, jnp.float32)
        scale = ((spread + tiny_eps) / scale_top).astype(jnp.bfloat16).astype(jnp.float32)
        factor = scale[:1, :1]
        stored = (rows / factor).astype(jnp.bfloat16)
        block[...] = (stored.astype(jnp.float32) * factor).astype(jnp.bfloat16)

    @pl.when(section == 1)
    def _():
        block[...] = own_in[...]

    pl.semaphore_wait(barrier, len(peers))

    def remote(src, dst, to, send_sem, recv_sem):
        return pltpu.make_async_remote_copy(
            src_ref=src,
            dst_ref=dst,
            send_sem=send_sem,
            recv_sem=recv_sem,
            device_id=to,
            device_id_type=pl.DeviceIdType.MESH,
        )

    def arrive(dst, recv_sem):
        remote(dst, dst, device(to_core=1 - core), recv_sem, recv_sem).wait_recv()

    def own_local():
        return pltpu.make_async_copy(block, own_out.at[core], own_sems.at[0])

    def own_away():
        to = device(to_core=1 - core)
        return remote(block, own_out.at[core], to, own_sems.at[1], own_sems.at[2])

    def x_copies():
        spot = keys.at[z, y, hi, core]
        return [
            remote(block, spot, device(to_hi=1 - hi), x_send.at[2], x_recv.at[1]),
            remote(block, spot, device(to_section=1), x_send.at[0], x_recv.at[0]),
            remote(block, spot, device(to_section=1, to_hi=1 - hi), x_send.at[1], x_recv.at[1]),
        ]

    def x_local():
        return pltpu.make_async_copy(block, keys.at[z, y, hi, core], x_send.at[3])

    @pl.when(section == 0)
    def _():
        x_local().start()
        for copy in x_copies():
            copy.start()

    own_local().start()
    own_away().start()

    for load in loads:
        load.wait()
    nope[...] = jnp.swapaxes(raw[...], 0, 1)

    near = heads - FAR_HEADS
    half_lanes = LANES // 2

    def far_copies():
        to = device(to_section=1 - section)
        rope_part = q_rope.at[:, pl.ds(near * half_lanes, FAR_HEADS * half_lanes)]
        return [
            remote(nope.at[pl.ds(near, FAR_HEADS)], far_nope, to, far_send.at[0], far_recv.at[0]),
            remote(rope_part, far_rope, to, far_send.at[1], far_recv.at[1]),
        ]

    def far_result():
        part = ready.at[pl.ds(near, FAR_HEADS)]
        return remote(part, part, device(to_section=1 - section), far_send.at[2], far_recv.at[2])

    @pl.when(section == 0)
    def _():
        for copy in far_copies():
            copy.start()

    def absorb(from_nope, from_rope, into, first, count):
        @pl.loop(0, count // 2)
        def _(pair):
            rope = from_rope[:, pl.ds(pl.multiple_of(pair * LANES, LANES), LANES)]
            for side in range(2):
                head = pair * 2 + side
                lifted = lax.dot_general(
                    from_nope[head], up[first + head], nt, preferred_element_type=jnp.float32
                )
                into[head, :, :kv_rank] = lifted.astype(jnp.bfloat16)
                into[head, :, kv_rank:] = rope[:, side * half_lanes : (side + 1) * half_lanes]

    @pl.when(section == 0)
    def _():
        absorb(nope, q_rope, q, 0, near)

    @pl.when(section == 1)
    def _():
        absorb(nope, q_rope, q, 0, heads)

    def load_value_up():
        return pltpu.make_async_copy(value_up, up, in_sems.at[1])

    @pl.when(section == 0)
    def _():
        load_value_up().start()

    @pl.when(section == 1)
    def _():
        pltpu.make_async_copy(q, q_out, out_sems.at[0]).start()

    @pl.when(section == 0)
    def _():
        x_local().wait()
        arrive(keys.at[z, y, 1 - hi, core], x_recv.at[1])

    @pl.when(section == 1)
    def _():
        arrive(keys.at[z, y, hi, core], x_recv.at[0])
        arrive(keys.at[z, y, 1 - hi, core], x_recv.at[1])

    low, high, far = row_at(-1), row_at(1), row_at(2)
    columns = [y, low, high, far]
    planes = [z]
    for s in range(1, half):
        planes += [plane_at(-s), plane_at(s)]
    planes.append(plane_at(half))
    steps = [[0]] + [[2 * s - 1, 2 * s] for s in range(1, half)] + [[z_count - 1]]

    def sender(went):
        def send(src, to, send_sem, recv_sem):
            copy = lambda: remote(src(), src(), to(), send_sem(), recv_sem())
            went.append(copy)
            copy().start()

        return send

    went = [[], [], []]

    def along_y(send, n, c, src, d, k):
        send(src, lambda: device(dy=d), lambda: y_send.at[n, k], lambda: y_recv.at[n, k])

    def spread(send, n, c):
        mine = lambda: keys.at[planes[n], y, :, c]
        along_y(send, n, c, mine, 1, 0)
        along_y(send, n, c, mine, -1, 1)

    def spread_on(send, n, c):
        arrive(keys.at[planes[n], low, :, c], y_recv.at[n, 0])
        along_y(send, n, c, lambda: keys.at[planes[n], low, 0, c], 1, 2)
        arrive(keys.at[planes[n], high, :, c], y_recv.at[n, 1])
        along_y(send, n, c, lambda: keys.at[planes[n], high, 1, c], -1, 3)

    def spread_end(n, c):
        arrive(keys.at[planes[n], far, 0, c], y_recv.at[n, 2])
        arrive(keys.at[planes[n], far, 1, c], y_recv.at[n, 3])

    def to_sibling(send, n, c):
        send(
            lambda: keys.at[planes[n], :, :, c],
            lambda: device(to_core=1 - c),
            lambda: sib_send.at[n],
            lambda: sib_recv.at[n],
        )

    def along_z(send, src, up_way, step, k):
        d, j = (1, 0) if up_way else (-1, 1)
        send(
            src,
            lambda: device(dz=d),
            lambda: z_send.at[j, step, k],
            lambda: z_recv.at[j, step, k],
        )

    ways = ((0, True), (1, False))

    def decode_a(stage):
        send = sender(went[1])

        def cell(n, k):
            return lambda: keys.at[planes[n], columns[k], :, 0]

        def column(k):
            for _, up_way in ways:
                along_z(send, cell(0, k), up_way, 0, k)

        if stage == 0:
            spread(send, 0, 0)
            column(0)
            arrive(keys.at[z, low, :, 0], y_recv.at[0, 0])
            along_y(send, 0, 0, lambda: keys.at[z, low, 0, 0], 1, 2)
            column(1)
            arrive(keys.at[z, high, :, 0], y_recv.at[0, 1])
            along_y(send, 0, 0, lambda: keys.at[z, high, 1, 0], -1, 3)
            column(2)
            spread_end(0, 0)
            column(3)
            to_sibling(send, 0, 0)
        elif stage < half:
            for k in range(y_count):
                for n, (j, up_way) in zip(steps[stage], ways):
                    arrive(cell(n, k)(), z_recv.at[j, stage - 1, k])
                    if stage < half - 1 or k // 2 == j:
                        along_z(send, cell(n, k), up_way, stage, k)
            for n in steps[stage]:
                to_sibling(send, n, 0)
        else:
            for k in range(y_count):
                arrive(cell(z_count - 1, k)(), z_recv.at[k // 2, half - 1, k])
            to_sibling(send, z_count - 1, 0)

    def decode_b(stage):
        send = sender(went[2])

        def ahead(n, s, j, up_way):
            if s < half - 1:
                part = lambda: keys.at[planes[n], y, :, 1]
            else:
                part = lambda: keys.at[planes[n], y, j, 1]
            along_z(send, part, up_way, s, 0)

        def chain(s):
            for n, (j, up_way) in zip(steps[s], ways):
                arrive(keys.at[planes[n], y, :, 1], z_recv.at[j, s - 1, 0])
                ahead(n, s, j, up_way)
                spread(send, n, 1)

        def finish(s):
            for n in steps[s]:
                spread_end(n, 1)
                to_sibling(send, n, 1)

        if stage == 0:
            for j, up_way in ways:
                ahead(0, 0, j, up_way)
            spread(send, 0, 1)
            chain(1)
            spread_on(send, 0, 1)
            return
        if stage + 1 < half:
            chain(stage + 1)
        elif stage + 1 == half:
            for j in range(2):
                arrive(keys.at[planes[-1], y, j, 1], z_recv.at[j, half - 1, 0])
            spread(send, z_count - 1, 1)
        for n in steps[stage]:
            spread_on(send, n, 1)
        finish(stage - 1)
        if stage == half:
            finish(stage)

    behind = [0] + [2 * s - 1 for s in range(1, half)] + [z_count - 1]
    past = planes[2 * (half - 1)]
    forward = sender(went[0])

    def ahead(n, s):
        along_z(forward, lambda: keys.at[planes[n], y, :, core], True, s, 0)

    def prefill_start():
        ahead(0, 0)
        spread(forward, 0, core)
        prefill_chain(1)
        spread_on(forward, 0, core)
        spread_end(0, core)
        to_sibling(forward, 0, core)
        prefill_on(1)
        from_sibling(0)

    def prefill_chain(s):
        n = behind[s]
        arrive(keys.at[planes[n], y, :, core], z_recv.at[0, s - 1, 0])
        if s < half:
            ahead(n, s)
        else:
            along_z(forward, lambda: keys.at[planes[n], y, 1, core], True, 0, 1)
        spread(forward, n, core)

    def prefill_on(s):
        spread_on(forward, behind[s], core)

    def prefill_end(s):
        spread_end(behind[s], core)
        to_sibling(forward, behind[s], core)

    def prefill_past():
        arrive(keys.at[past, y, 1, core], z_recv.at[0, 0, 1])
        n = 2 * (half - 1)
        along_y(forward, n, core, lambda: keys.at[past, y, 1, core], 1, 0)

    def prefill_past_end():
        n = 2 * (half - 1)
        spot = lambda: keys.at[past, low, 1, core]
        arrive(spot(), y_recv.at[n, 0])
        forward(
            spot,
            lambda: device(to_core=1 - core),
            lambda: sib_send.at[n],
            lambda: sib_recv.at[n],
        )

    def from_sibling(n):
        arrive(keys.at[planes[n], :, :, 1 - core], sib_recv.at[n])

    def on(at, event):
        @pl.when(at)
        def _():
            event()

    top[...] = jnp.full(top.shape, masked_low, jnp.float32)
    total[...] = jnp.zeros(total.shape, jnp.float32)
    acc[...] = jnp.zeros(acc.shape, jnp.float32)

    token = lax.broadcasted_iota(jnp.int32, (tokens, 1), 0)
    position = seq * tokens + token
    count = lengths.shape[1]
    before_it = lax.broadcasted_iota(jnp.int32, (count, count), 0) < lax.broadcasted_iota(
        jnp.int32, (count, count), 1
    )
    earlier = jnp.where(before_it, 1.0, 0.0).astype(jnp.bfloat16)
    wide = jnp.broadcast_to(lengths[...], (8, count))
    digits = [(wide // 64).astype(jnp.bfloat16), (wide % 64).astype(jnp.bfloat16)]
    upper, lower = [jnp.dot(d, earlier, preferred_element_type=jnp.float32) for d in digits]
    starts = (upper * 64.0 + lower)[:1]
    row_low = jnp.max(
        jnp.where(starts <= position.astype(jnp.float32), starts, 0.0), axis=1, keepdims=True
    ).astype(jnp.int32)

    chunk = plane_keys // 2
    tile_heads = near // 2

    def fold(asked_heads, tile, key_block):
        count = key_block.shape[0]
        tile_heads = asked_heads.shape[0]
        rows = tile_heads * tokens
        part = pl.ds(pl.multiple_of(tile * rows, rows), rows)
        asked = asked_heads[...].reshape(rows, width)
        s = lax.dot_general(asked, key_block, nt, preferred_element_type=jnp.float32)
        s = (s.reshape(tile_heads, tokens, count) + bias[:, :count][None]).reshape(rows, count)
        before = top[part, :]
        now = jnp.maximum(before, jnp.max(s, axis=1, keepdims=True))
        shrink = jnp.exp2((before - now) * exponent_scale)
        expo = jnp.exp2((s - over_lanes(now, count)) * exponent_scale)
        top[part, :] = now
        summed = total[part, :] * shrink
        for c in range(0, count, LANES):
            summed = summed + expo[:, c : c + LANES]
        total[part, :] = summed
        acc[part, :] = acc[part, :] * over_lanes(shrink, kv_rank) + jnp.dot(
            expo.astype(jnp.bfloat16),
            key_block[:, :kv_rank],
            preferred_element_type=jnp.float32,
        )

    def past_from_sibling():
        arrive(keys.at[past, low, 1, 1 - core], sib_recv.at[2 * (half - 1)])

    last_step = 4 * (half + 1)
    timetable = [
        (prefill_chain, CHAIN_STEPS),
        (prefill_on, ON_STEPS),
        (prefill_end, END_STEPS),
        (lambda s: from_sibling(behind[s]), SIBLING_STEPS),
    ]
    events = {0: [prefill_start]}
    for s in range(1, half + 1):
        for event, at_steps in timetable:
            if at_steps[s - 1] > 0:
                spot = events.setdefault(at_steps[s - 1], [])
                spot.append(functools.partial(event, s))
    for event, at_step in zip((prefill_past, prefill_past_end, past_from_sibling), PAST_STEPS):
        events.setdefault(at_step, []).append(event)

    @pl.when(section == 0)
    def _():
        mid = plane_blocks // 2
        at_first, at_mid = at_block == 0, at_block == mid
        reaches_past = at_first & (z > half)

        @pl.loop(0, last_step)
        def _(step):
            for at_step in sorted(events):
                for event in events[at_step]:
                    on(step == at_step, event)

            run = step // 2
            turn = step % 2
            rest = run == 2 * half + 1
            back = jnp.where(rest, 0, (run + 1) // 2)
            side = jnp.where(run == 0, 0, (run + 1) % 2)
            side = jnp.where(rest, 1, side)
            slot = jnp.where(rest, 1, back % 2)
            reached = z >= back

            def load(back, part, slot, into):
                plane = lax.rem(z - back + z_count, z_count)
                here = keys.at[plane, pl.ds(part * (y_count // 2), y_count // 2)]
                return pltpu.make_async_copy(here, held.at[slot, into], held_sems.at[slot, into])

            def load_first():
                return pltpu.make_async_copy(
                    keys.at[past, y_count - 1, 1], held.at[1, 0, 0, 0], held_sems.at[1, 0]
                )

            def load_mid():
                return pltpu.make_async_copy(
                    keys.at[planes[-1], y_count // 2 - 1, 1],
                    held.at[1, 1, y_count // 2 - 1, 1],
                    held_sems.at[1, 0],
                )

            @pl.when(step == 0)
            def _():
                load(0, 0, 0, 0).start()

            for s in range(1, half + 1):

                @pl.when((step == SIBLING_STEPS[s - 1]) & (z >= s))
                def _():
                    load(s, 0, s % 2, 0).start()
                    load(s, 1, s % 2, 1).start()

            @pl.when(step == last_step - 5)
            def _():
                @pl.when(reaches_past)
                def _():
                    load_first().start()

                @pl.when(at_block >= mid)
                def _():
                    rest_load = load(0, 1, 1, 1)
                    rest_load.start()
                    rest_load.wait()

                @pl.when(at_mid)
                def _():
                    load_mid().start()

            @pl.when(reached & (turn == 0) & jnp.logical_not(rest))
            def _():
                load(back, side, slot, side).wait()

            at_past = reaches_past & (run == 2 * half)

            @pl.when(at_past & (turn == 0))
            def _():
                load_first().wait()

            @pl.when((turn == 0) & rest & at_mid)
            def _():
                load_mid().wait()

            none = (rest & (at_block < mid)) | ((run == 2 * half - 1) & (at_block >= mid))
            first_spot = (z - back) * plane_keys + side * chunk

            @pl.when(reached & jnp.logical_not(none))
            def _():
                @pl.when(turn == 0)
                def _():
                    lane = lax.broadcasted_iota(jnp.int32, (1, chunk + tokens), 1)
                    spot = first_spot + lane
                    shift = (half * plane_keys) + chunk
                    spot = jnp.where(
                        rest & at_mid & (lane >= chunk - tokens), spot - shift, spot
                    )
                    spot = jnp.where(lane >= chunk, spot - plane_keys - tokens, spot)
                    seen = (spot >= row_low) & (spot <= position)
                    bias[...] = jnp.where(seen, 0.0, masked_low)

                here = held.at[slot, side]
                tile_q = q.at[pl.ds(turn * tile_heads, tile_heads)]

                @pl.when(at_past)
                def _():
                    behind_it = held[1, 0, 0, 0].reshape(tokens, width)
                    key_block = jnp.concatenate([here[...].reshape(chunk, width), behind_it])

                    fold(tile_q, turn, key_block)

                @pl.when(jnp.logical_not(at_past))
                def _():
                    fold(tile_q, turn, here[...].reshape(chunk, width))

    def far_run(run):
        rest, beyond = run == 2 * half + 1, run == 2 * half + 2
        back = jnp.where(rest, 0, jnp.where(beyond, half + 1, (run + 1) // 2))
        side = jnp.where(run == 0, 0, jnp.where(rest | beyond, 1, (run + 1) % 2))
        slot = run % 2
        middle = plane_blocks // 2
        wanted = z >= back
        wanted = wanted & jnp.logical_not(rest & (at_block < middle))
        wanted = wanted & jnp.logical_not((run == 2 * half - 1) & (at_block > middle))
        wanted = wanted & jnp.logical_not(beyond & (at_block > 0))
        plane = lax.rem(z - back + z_count, z_count)
        load = pltpu.make_async_copy(
            keys.at[plane, pl.ds(side * (y_count // 2), y_count // 2)],
            held.at[slot, 0],
            held_sems.at[slot, 0],
        )
        return wanted, load, (z - back) * plane_keys + side * chunk, slot

    def start_far(run):
        wanted, load, _, _ = far_run(run)

        @pl.when(wanted)
        def _():
            load.start()

    def far_runs(begin, end):
        start_far(jnp.int32(begin))

        @pl.loop(begin, end)
        def _(run):
            @pl.when(run + 1 < end)
            def _():
                start_far(run + 1)

            wanted, load, first_spot, slot = far_run(run)

            @pl.when(wanted)
            def _():
                load.wait()
                spot = first_spot + lax.broadcasted_iota(jnp.int32, (1, chunk), 1)
                seen = (spot >= row_low) & (spot <= position)
                bias[:, :chunk] = jnp.where(seen, 0.0, masked_low)
                fold(far_q, 0, held[slot, 0].reshape(chunk, width))

    def project(head, part):
        norm = 1.0 / jnp.sum(total[part, :], axis=1, keepdims=True)
        mixed = (acc[part, :] * norm).astype(jnp.bfloat16)
        ready[head] = jnp.dot(mixed, up[head], preferred_element_type=jnp.float32).astype(
            jnp.bfloat16
        )

    @pl.when(section == 1)
    def _():
        for stage in range(half + 1):
            on(core == 0, functools.partial(decode_a, stage))
            on(core == 1, functools.partial(decode_b, stage))
            if stage == 1:
                arrive(far_nope, far_recv.at[0])
                arrive(far_rope, far_recv.at[1])
                absorb(far_nope, far_rope, far_q, near, FAR_HEADS)
                load_value_up().start()
            if 0 < stage < half:
                for n in steps[stage - 1]:
                    from_sibling(n)
                far_runs(max(2 * stage - 3, 0), 2 * stage - 1)
        for n in steps[half - 1] + steps[half]:
            from_sibling(n)
        far_runs(2 * half - 3, 2 * half + 3)
        load_value_up().wait()

        @pl.loop(0, FAR_HEADS // 2)
        def _(pair):
            for side in range(2):
                head = pair * 2 + side
                project(near + head, pl.ds(pl.multiple_of(head * tokens, tokens), tokens))

        far_result().start()

    @pl.when(section == 0)
    def _():
        load_value_up().wait()

        @pl.loop(0, near // 2)
        def _(pair):
            for side in range(2):
                head = pair * 2 + side
                project(head, pl.ds(pl.multiple_of(head * tokens, tokens), tokens))

        arrive(ready.at[pl.ds(near, FAR_HEADS)], far_recv.at[2])
        raw[...] = jnp.swapaxes(ready[...], 0, 1)
        done = pltpu.make_async_copy(raw, out, out_sems.at[1])
        done.start()
        done.wait()
        for copy in x_copies() + far_copies():
            copy.wait_send()

    @pl.when(section == 1)
    def _():
        pltpu.make_async_copy(q, q_out, out_sems.at[0]).wait()
        far_result().wait_send()

    groups = [section == 0, (section == 1) & (core == 0), (section == 1) & (core == 1)]
    for group, copies in zip(groups, went):

        @pl.when(group)
        def _():
            for copy in copies:
                copy().wait_send()

    arrive(own_out.at[1 - core], own_sems.at[2])
    own_away().wait_send()
    own_local().wait()


def prefill_part(own, q_nope, q_rope, up_key, value_up, lengths, seq_count, exponent_scale):
    rows, width = own.shape
    tokens, heads, nope_dim = q_nope.shape
    kv_rank = up_key.shape[1]
    y_count = 4
    z_count = seq_count // (2 * y_count)
    dma = pltpu.SemaphoreType.DMA
    bf16 = own.dtype
    chunk = y_count * tokens
    vmem = pl.BlockSpec(memory_space=pltpu.VMEM)
    hbm = pl.BlockSpec(memory_space=pl.ANY)
    return pl.pallas_call(
        functools.partial(prefill_kernel, z_count, y_count, kv_rank, exponent_scale),
        out_shape=[
            jax.ShapeDtypeStruct((z_count, y_count, 2, 2, rows, width), bf16),
            jax.ShapeDtypeStruct((2, rows, width), bf16),
            jax.ShapeDtypeStruct((heads, tokens, width), bf16),
            jax.ShapeDtypeStruct((tokens, heads, value_up.shape[2]), bf16),
        ],
        in_specs=[vmem, hbm, vmem, hbm, hbm, vmem],
        out_specs=[hbm] * 4,
        scratch_shapes=[
            pltpu.VMEM((rows, width), bf16),
            pltpu.VMEM(q_nope.shape, bf16),
            pltpu.VMEM((heads, tokens, nope_dim), bf16),
            pltpu.VMEM(up_key.shape, bf16),
            pltpu.VMEM((heads, tokens, width), bf16),
            pltpu.VMEM((FAR_HEADS, tokens, nope_dim), bf16),
            pltpu.VMEM((tokens, FAR_HEADS * (width - kv_rank)), bf16),
            pltpu.VMEM((FAR_HEADS, tokens, width), bf16),
            pltpu.VMEM(((heads - FAR_HEADS) * tokens, kv_rank), jnp.float32),
            pltpu.VMEM(((heads - FAR_HEADS) * tokens, LANES), jnp.float32),
            pltpu.VMEM(((heads - FAR_HEADS) * tokens, LANES), jnp.float32),
            pltpu.VMEM((2, 2, y_count // 2, 2, 2, rows, width), bf16),
            pltpu.VMEM((tokens, chunk + tokens), jnp.float32),
            pltpu.VMEM((heads, tokens, value_up.shape[2]), bf16),
            dma((3,)),
            dma((3,)),
            dma((2,)),
            dma((2,)),
            dma((2, 2)),
            dma((4,)),
            dma((2,)),
            dma((3,)),
            dma((2, z_count // 2, y_count)),
            dma((2, z_count // 2, y_count)),
            dma((z_count, 4)),
            dma((z_count, 4)),
            dma((z_count,)),
            dma((z_count,)),
        ],
        compiler_params=pltpu.CompilerParams(
            collective_id=0, has_side_effects=True, vmem_limit_bytes=56 << 20
        ),
    )(own, q_nope, q_rope, up_key, value_up, lengths)


def over_lanes(value, width):
    return jnp.concatenate([value] * (width // LANES), axis=1)


def decode_kernel(
    kv_rank,
    groups,
    exponent_scale,
    lengths,
    table,
    q_ref,
    keys,
    own_keys,
    value_up,
    prefill_out,
    out_ref,
    acc,
    top,
    total,
    held,
    lat,
    up,
    ready,
    turned,
    q_held,
    sems,
    q_sems,
    up_sems,
):
    band = pl.program_id(0)
    bands = pl.num_programs(0)
    _, heads, tokens, width = q_held.shape
    rows = heads * tokens
    all_keys = keys.shape[0]
    nt = (((1,), (1,)), ((), ()))

    @pl.when(lax.axis_index("section") == 0)
    def _():
        handed = pltpu.make_async_copy(prefill_out, out_ref, up_sems.at[1])

        @pl.when(band == 0)
        def _():
            handed.start()

        @pl.when(band == bands - 1)
        def _():
            handed.wait()

    @pl.when(lax.axis_index("section") == 1)
    def _():
        def prompt_range(which):
            prompt = table[lax.axis_index("seq") * bands + which] // groups
            low = lax.fori_loop(0, prompt, lambda k, at: at + lengths[k], jnp.int32(0))
            return low, low + lengths[prompt]

        def chunk_at(start, i):
            return pl.multiple_of(jnp.minimum(start + i * KEY_BLOCK, all_keys - KEY_BLOCK), 16)

        def fetch_from(start, i, slot):
            return pltpu.make_async_copy(
                keys.at[pl.ds(chunk_at(start, i), KEY_BLOCK), :], held.at[slot], sems.at[slot]
            )

        def band_rows(which):
            return pl.ds(pl.multiple_of(which * tokens, tokens), tokens)

        def fetch_q(which):
            slot = lax.rem(which, 2)
            return pltpu.make_async_copy(
                q_ref.at[:, band_rows(which), :], q_held.at[slot], q_sems.at[slot]
            )

        def load_up():
            return pltpu.make_async_copy(value_up, up, up_sems.at[0])

        low, last = prompt_range(band)
        first = low // 16 * 16
        chunks = (last - first + KEY_BLOCK - 1) // KEY_BLOCK

        def fetch(i):
            slot = jnp.where(i == 0, lax.rem(band, 2), 2 + lax.rem(i, 2))
            return fetch_from(first, i, slot)

        @pl.when(band == 0)
        def _():
            fetch_q(0).start()
            fetch(0).start()
            load_up().start()

        @pl.when(band + 1 < bands)
        def _():
            fetch_q(band + 1).start()
            next_low, _ = prompt_range(band + 1)
            fetch_from(next_low // 16 * 16, 0, lax.rem(band + 1, 2)).start()

        fetch_q(band).wait()
        q = q_held[lax.rem(band, 2)].reshape(rows, width)
        def score(key_block):
            return lax.dot_general(q, key_block, nt, preferred_element_type=jnp.float32)

        def in_range(at, count, low_spot):
            spot = at + lax.broadcasted_iota(jnp.int32, (1, count), 1)
            return jnp.where((spot >= jnp.maximum(low, low_spot)) & (spot < last), 0.0, masked_low)

        def weigh(scores, now):
            return jnp.exp2((scores - now) * exponent_scale)

        def mix(weights, key_block):
            return jnp.dot(
                weights.astype(jnp.bfloat16),
                key_block[:, :kv_rank],
                preferred_element_type=jnp.float32,
            )

        def begin(key_block, at):
            own = own_keys[...]
            asked = lax.broadcasted_iota(jnp.int32, (tokens, tokens), 0)
            key = lax.broadcasted_iota(jnp.int32, (tokens, tokens), 1)
            seen = (asked % SAMPLES == key % SAMPLES) & (key // SAMPLES <= asked // SAMPLES)
            bias = jnp.where(seen, 0.0, masked_low)
            bias = jnp.broadcast_to(bias[None], (heads, tokens, tokens)).reshape(rows, tokens)
            new = score(own) + bias
            count = key_block.shape[0]
            old = score(key_block) + in_range(at, count, low)
            now = jnp.maximum(
                jnp.max(new, axis=1, keepdims=True), jnp.max(old, axis=1, keepdims=True)
            )
            new = weigh(new, now)
            old = weigh(old, now)
            top[...] = jnp.broadcast_to(now, (rows, LANES))
            lane = lax.broadcasted_iota(jnp.int32, (rows, LANES), 1)
            summed = jnp.where(lane == 0, jnp.sum(new, axis=1, keepdims=True), 0.0)
            for c in range(0, count, LANES):
                summed = summed + old[:, c : c + LANES]
            total[...] = summed
            acc[...] = mix(new, own) + mix(old, key_block)

        def fold(key_block, low_spot, at):
            count = key_block.shape[0]
            s = score(key_block)
            if low_spot is not None:
                s = s + in_range(at, count, low_spot)
            before = top[...]
            now = jnp.maximum(before, jnp.max(s, axis=1, keepdims=True))
            shrink = jnp.exp2((before - now) * exponent_scale)
            expo = weigh(s, over_lanes(now, count))
            top[...] = now
            summed = total[...] * shrink
            for c in range(0, count, LANES):
                summed = summed + expo[:, c : c + LANES]
            total[...] = summed
            acc[...] = acc[...] * over_lanes(shrink, kv_rank) + mix(expo, key_block)

        @pl.loop(0, chunks)
        def _(i):
            slot = jnp.where(i == 0, lax.rem(band, 2), 2 + lax.rem(i, 2))
            fetch(i).wait()

            @pl.when(i + 1 < chunks)
            def _():
                fetch(i + 1).start()

            nominal = first + i * KEY_BLOCK
            at = chunk_at(first, i)
            whole = (i > 0) & (nominal + KEY_BLOCK <= last)
            skip = (nominal - at) // EDGE_BLOCK

            @pl.when(i == 0)
            def _():
                here = pl.multiple_of(skip * EDGE_BLOCK, EDGE_BLOCK)
                begin(held[slot, pl.ds(here, EDGE_BLOCK), :], at + here)

            @pl.when(whole)
            def _():
                fold(held[slot], None, None)

            @pl.when(jnp.logical_not(whole))
            def _():
                begun = skip + jnp.where(i == 0, 1, 0)

                @pl.loop(begun, (jnp.minimum(last - at, KEY_BLOCK) + EDGE_BLOCK - 1) // EDGE_BLOCK)
                def _(j):
                    here = pl.multiple_of(j * EDGE_BLOCK, EDGE_BLOCK)
                    fold(held[slot, pl.ds(here, EDGE_BLOCK), :], nominal, at + here)

        norm = 1.0 / jnp.sum(total[...], axis=1, keepdims=True)
        lat[:, band_rows(band), :] = (
            (acc[...] * norm).astype(jnp.bfloat16).reshape(heads, tokens, kv_rank)
        )

        @pl.when(band == bands - 1)
        def _():
            load_up().wait()

            @pl.loop(0, heads // 4)
            def _(four):
                picked = [four * 4 + k for k in range(4)]
                products = [
                    jnp.dot(lat[head], up[head], preferred_element_type=jnp.float32)
                    for head in picked
                ]
                for head, product in zip(picked, products):
                    ready[head] = product.astype(jnp.bfloat16)

            turned[...] = jnp.swapaxes(ready[...], 0, 1)
            done = pltpu.make_async_copy(turned, out_ref, up_sems.at[1])
            done.start()
            done.wait()


def shards(query_nope, query_rope, latent, up_key, value_up_weight, lengths, owner_request_table):
    seq_count = lax.axis_size("seq")
    tok_dev, head_dev, nope_dim = query_nope.shape[1:]
    rope_dim = query_rope.shape[2] // head_dev
    kv_rank = up_key.shape[1]
    width = kv_rank + rope_dim
    v_dim = value_up_weight.shape[2]
    req_dev = owner_request_table.shape[0] // seq_count
    groups = owner_request_table.shape[0] // lengths.shape[0]
    band_tokens = tok_dev // req_dev
    exponent_scale = math.log2(math.e) / math.sqrt(nope_dim + rope_dim)

    keys, pair, queries, prefill_out = prefill_part(
        latent[0],
        query_nope[0],
        query_rope[0],
        up_key,
        value_up_weight,
        lengths[None, :],
        seq_count,
        exponent_scale,
    )
    rows = head_dev * band_tokens
    attended = pl.pallas_call(
        functools.partial(decode_kernel, kv_rank, groups, exponent_scale),
        out_shape=jax.ShapeDtypeStruct(prefill_out.shape, jnp.bfloat16),
        grid_spec=pltpu.PrefetchScalarGridSpec(
            num_scalar_prefetch=2,
            grid=(req_dev,),
            in_specs=[
                pl.BlockSpec(memory_space=pl.ANY),
                pl.BlockSpec(memory_space=pl.ANY),
                pl.BlockSpec((band_tokens, width), lambda i, *_: (i, 0)),
                pl.BlockSpec(memory_space=pl.ANY),
                pl.BlockSpec(memory_space=pl.ANY),
            ],
            out_specs=pl.BlockSpec(memory_space=pl.ANY),
            scratch_shapes=[
                pltpu.VMEM((rows, kv_rank), jnp.float32),
                pltpu.VMEM((rows, LANES), jnp.float32),
                pltpu.VMEM((rows, LANES), jnp.float32),
                pltpu.VMEM((4, KEY_BLOCK, width), jnp.bfloat16),
                pltpu.VMEM((head_dev, tok_dev, kv_rank), jnp.bfloat16),
                pltpu.VMEM(value_up_weight.shape, jnp.bfloat16),
                pltpu.VMEM((head_dev, tok_dev, v_dim), jnp.bfloat16),
                pltpu.VMEM(prefill_out.shape, jnp.bfloat16),
                pltpu.VMEM((2, head_dev, band_tokens, width), jnp.bfloat16),
                pltpu.SemaphoreType.DMA((4,)),
                pltpu.SemaphoreType.DMA((2,)),
                pltpu.SemaphoreType.DMA((2,)),
            ],
        ),
        compiler_params=pltpu.CompilerParams(vmem_limit_bytes=58 << 20),
    )(
        lengths,
        owner_request_table,
        queries,
        keys.reshape(-1, width),
        pair.reshape(-1, width),
        value_up_weight,
        prefill_out,
    )

    return attended[None]


def solution(mesh):
    in_specs = (
        P("section", "seq", "head", None),
        P("section", "seq", "head"),
        P("section", ("seq", "head"), None),
        P("head", None, None),
        P("head", None, None),
        P(),
        P(),
    )
    out_specs = P("section", "seq", "head", None)
    return jax.shard_map(shards, mesh=mesh, in_specs=in_specs, out_specs=out_specs, check_vma=False)
```

```python
import functools
import math

import jax
import jax.numpy as jnp
from jax import lax
from jax.experimental import pallas as pl
from jax.experimental.pallas import tpu as pltpu
from jax.sharding import PartitionSpec as P

SAMPLES = 8
STEPS = 4
BLOCK = 64

scale_top = 448.0
tiny_eps = 1e-06
masked_low = -1e30

KEY_BLOCK = 1024
EDGE_BLOCK = 512
FAR_HEADS = 6

CHAIN_STEPS = (0, 1, 3, 5)
ON_STEPS = (0, 2, 5, 8)
END_STEPS = (1, 3, 7, 10)
SIBLING_STEPS = (2, 5, 9, 13)
PAST_STEPS = (8, 10, 15)
LANES = 128


def prefill_kernel(
    z_count, y_count, kv_rank, exponent_scale, own_in, q_nope, q_rope, up_key, value_up, lengths,
    keys, own_out, q_out, out, block, raw, nope, up, q, far_nope, far_rope, far_q, acc, top, total,
    held, bias, ready, far_send, far_recv,
    in_sems, out_sems, held_sems, x_send, x_recv, own_sems,
    z_send, z_recv, y_send, y_recv, sib_send, sib_recv,
):
    section = lax.axis_index("section")
    seq = lax.axis_index("seq")
    core = lax.axis_index("head")
    z = seq // (2 * y_count)
    y = seq // 2 % y_count
    hi = seq % 2
    half = z_count // 2
    heads, tokens, width = q.shape
    plane_blocks = 2 * y_count
    at_block = seq % plane_blocks
    plane_keys = plane_blocks * tokens
    nt = (((1,), (1,)), ((), ()))

    def plane_at(dz):
        return lax.rem(z + dz + z_count, z_count)

    def row_at(dy):
        return lax.rem(y + dy + y_count, y_count)

    def device(dz=0, dy=0, to_hi=None, to_section=None, to_core=None):
        th = hi if to_hi is None else to_hi
        return (
            section if to_section is None else to_section,
            (plane_at(dz) * y_count + row_at(dy)) * 2 + th,
            core if to_core is None else to_core,
        )

    loads = [
        pltpu.make_async_copy(q_nope, raw, in_sems.at[0]),
        pltpu.make_async_copy(up_key, up, in_sems.at[1]),
    ]
    for load in loads:
        load.start()

    barrier = pltpu.get_barrier_semaphore()
    peers = [
        device(to_core=1 - core),
        device(to_section=1 - section),
        device(to_hi=1 - hi),
        device(to_section=1 - section, to_hi=1 - hi),
        device(dz=1),
        device(dz=-1),
        device(dy=1),
        device(dy=-1),
    ]
    for peer in peers:
        pl.semaphore_signal(barrier, inc=1, device_id=peer, device_id_type=pl.DeviceIdType.MESH)

    @pl.when(section == 0)
    def _():
        rows = own_in[...].astype(jnp.float32)
        largest = jnp.max(jnp.abs(rows))
        spread = jnp.full((8, LANES), largest, jnp.float32)
        scale = ((spread + tiny_eps) / scale_top).astype(jnp.bfloat16).astype(jnp.float32)
        factor = scale[:1, :1]
        stored = (rows / factor).astype(jnp.bfloat16)
        block[...] = (stored.astype(jnp.float32) * factor).astype(jnp.bfloat16)

    @pl.when(section == 1)
    def _():
        block[...] = own_in[...]

    pl.semaphore_wait(barrier, len(peers))

    def remote(src, dst, to, send_sem, recv_sem):
        return pltpu.make_async_remote_copy(
            src_ref=src,
            dst_ref=dst,
            send_sem=send_sem,
            recv_sem=recv_sem,
            device_id=to,
            device_id_type=pl.DeviceIdType.MESH,
        )

    def arrive(dst, recv_sem):
        remote(dst, dst, device(to_core=1 - core), recv_sem, recv_sem).wait_recv()

    def own_local():
        return pltpu.make_async_copy(block, own_out.at[core], own_sems.at[0])

    def own_away():
        to = device(to_core=1 - core)
        return remote(block, own_out.at[core], to, own_sems.at[1], own_sems.at[2])

    def x_copies():
        spot = keys.at[z, y, hi, core]
        return [
            remote(block, spot, device(to_hi=1 - hi), x_send.at[2], x_recv.at[1]),
            remote(block, spot, device(to_section=1), x_send.at[0], x_recv.at[0]),
            remote(block, spot, device(to_section=1, to_hi=1 - hi), x_send.at[1], x_recv.at[1]),
        ]

    def x_local():
        return pltpu.make_async_copy(block, keys.at[z, y, hi, core], x_send.at[3])

    @pl.when(section == 0)
    def _():
        x_local().start()
        for copy in x_copies():
            copy.start()

    own_local().start()
    own_away().start()

    for load in loads:
        load.wait()
    nope[...] = jnp.swapaxes(raw[...], 0, 1)

    near = heads - FAR_HEADS
    half_lanes = LANES // 2

    def far_copies():
        to = device(to_section=1 - section)
        rope_part = q_rope.at[:, pl.ds(near * half_lanes, FAR_HEADS * half_lanes)]
        return [
            remote(nope.at[pl.ds(near, FAR_HEADS)], far_nope, to, far_send.at[0], far_recv.at[0]),
            remote(rope_part, far_rope, to, far_send.at[1], far_recv.at[1]),
        ]

    def far_result():
        part = ready.at[pl.ds(near, FAR_HEADS)]
        return remote(part, part, device(to_section=1 - section), far_send.at[2], far_recv.at[2])

    @pl.when(section == 0)
    def _():
        for copy in far_copies():
            copy.start()

    def absorb(from_nope, from_rope, into, first, count):
        @pl.loop(0, count // 2)
        def _(pair):
            rope = from_rope[:, pl.ds(pl.multiple_of(pair * LANES, LANES), LANES)]
            for side in range(2):
                head = pair * 2 + side
                lifted = lax.dot_general(
                    from_nope[head], up[first + head], nt, preferred_element_type=jnp.float32
                )
                into[head, :, :kv_rank] = lifted.astype(jnp.bfloat16)
                into[head, :, kv_rank:] = rope[:, side * half_lanes : (side + 1) * half_lanes]

    @pl.when(section == 0)
    def _():
        absorb(nope, q_rope, q, 0, near)

    @pl.when(section == 1)
    def _():
        absorb(nope, q_rope, q, 0, heads)

    def load_value_up():
        return pltpu.make_async_copy(value_up, up, in_sems.at[1])

    @pl.when(section == 0)
    def _():
        load_value_up().start()

    @pl.when(section == 1)
    def _():
        pltpu.make_async_copy(q, q_out, out_sems.at[0]).start()

    @pl.when(section == 0)
    def _():
        x_local().wait()
        arrive(keys.at[z, y, 1 - hi, core], x_recv.at[1])

    @pl.when(section == 1)
    def _():
        arrive(keys.at[z, y, hi, core], x_recv.at[0])
        arrive(keys.at[z, y, 1 - hi, core], x_recv.at[1])

    low, high, far = row_at(-1), row_at(1), row_at(2)
    columns = [y, low, high, far]
    planes = [z]
    for s in range(1, half):
        planes += [plane_at(-s), plane_at(s)]
    planes.append(plane_at(half))
    steps = [[0]] + [[2 * s - 1, 2 * s] for s in range(1, half)] + [[z_count - 1]]

    def sender(went):
        def send(src, to, send_sem, recv_sem):
            copy = lambda: remote(src(), src(), to(), send_sem(), recv_sem())
            went.append(copy)
            copy().start()

        return send

    went = [[], [], []]

    def along_y(send, n, c, src, d, k):
        send(src, lambda: device(dy=d), lambda: y_send.at[n, k], lambda: y_recv.at[n, k])

    def spread(send, n, c):
        mine = lambda: keys.at[planes[n], y, :, c]
        along_y(send, n, c, mine, 1, 0)
        along_y(send, n, c, mine, -1, 1)

    def spread_on(send, n, c):
        arrive(keys.at[planes[n], low, :, c], y_recv.at[n, 0])
        along_y(send, n, c, lambda: keys.at[planes[n], low, 0, c], 1, 2)
        arrive(keys.at[planes[n], high, :, c], y_recv.at[n, 1])
        along_y(send, n, c, lambda: keys.at[planes[n], high, 1, c], -1, 3)

    def spread_end(n, c):
        arrive(keys.at[planes[n], far, 0, c], y_recv.at[n, 2])
        arrive(keys.at[planes[n], far, 1, c], y_recv.at[n, 3])

    def to_sibling(send, n, c):
        send(
            lambda: keys.at[planes[n], :, :, c],
            lambda: device(to_core=1 - c),
            lambda: sib_send.at[n],
            lambda: sib_recv.at[n],
        )

    def along_z(send, src, up_way, step, k):
        d, j = (1, 0) if up_way else (-1, 1)
        send(
            src,
            lambda: device(dz=d),
            lambda: z_send.at[j, step, k],
            lambda: z_recv.at[j, step, k],
        )

    ways = ((0, True), (1, False))

    def decode_a(stage):
        send = sender(went[1])

        def cell(n, k):
            return lambda: keys.at[planes[n], columns[k], :, 0]

        def column(k):
            for _, up_way in ways:
                along_z(send, cell(0, k), up_way, 0, k)

        if stage == 0:
            spread(send, 0, 0)
            column(0)
            arrive(keys.at[z, low, :, 0], y_recv.at[0, 0])
            along_y(send, 0, 0, lambda: keys.at[z, low, 0, 0], 1, 2)
            column(1)
            arrive(keys.at[z, high, :, 0], y_recv.at[0, 1])
            along_y(send, 0, 0, lambda: keys.at[z, high, 1, 0], -1, 3)
            column(2)
            spread_end(0, 0)
            column(3)
            to_sibling(send, 0, 0)
        elif stage < half:
            for k in range(y_count):
                for n, (j, up_way) in zip(steps[stage], ways):
                    arrive(cell(n, k)(), z_recv.at[j, stage - 1, k])
                    if stage < half - 1 or k // 2 == j:
                        along_z(send, cell(n, k), up_way, stage, k)
            for n in steps[stage]:
                to_sibling(send, n, 0)
        else:
            for k in range(y_count):
                arrive(cell(z_count - 1, k)(), z_recv.at[k // 2, half - 1, k])
            to_sibling(send, z_count - 1, 0)

    def decode_b(stage):
        send = sender(went[2])

        def ahead(n, s, j, up_way):
            if s < half - 1:
                part = lambda: keys.at[planes[n], y, :, 1]
            else:
                part = lambda: keys.at[planes[n], y, j, 1]
            along_z(send, part, up_way, s, 0)

        def chain(s):
            for n, (j, up_way) in zip(steps[s], ways):
                arrive(keys.at[planes[n], y, :, 1], z_recv.at[j, s - 1, 0])
                ahead(n, s, j, up_way)
                spread(send, n, 1)

        def finish(s):
            for n in steps[s]:
                spread_end(n, 1)
                to_sibling(send, n, 1)

        if stage == 0:
            for j, up_way in ways:
                ahead(0, 0, j, up_way)
            spread(send, 0, 1)
            chain(1)
            spread_on(send, 0, 1)
            return
        if stage + 1 < half:
            chain(stage + 1)
        elif stage + 1 == half:
            for j in range(2):
                arrive(keys.at[planes[-1], y, j, 1], z_recv.at[j, half - 1, 0])
            spread(send, z_count - 1, 1)
        for n in steps[stage]:
            spread_on(send, n, 1)
        finish(stage - 1)
        if stage == half:
            finish(stage)

    behind = [0] + [2 * s - 1 for s in range(1, half)] + [z_count - 1]
    past = planes[2 * (half - 1)]
    forward = sender(went[0])

    def ahead(n, s):
        along_z(forward, lambda: keys.at[planes[n], y, :, core], True, s, 0)

    def prefill_start():
        ahead(0, 0)
        spread(forward, 0, core)
        prefill_chain(1)
        spread_on(forward, 0, core)
        spread_end(0, core)
        to_sibling(forward, 0, core)
        prefill_on(1)
        from_sibling(0)

    def prefill_chain(s):
        n = behind[s]
        arrive(keys.at[planes[n], y, :, core], z_recv.at[0, s - 1, 0])
        if s < half:
            ahead(n, s)
        else:
            along_z(forward, lambda: keys.at[planes[n], y, 1, core], True, 0, 1)
        spread(forward, n, core)

    def prefill_on(s):
        spread_on(forward, behind[s], core)

    def prefill_end(s):
        spread_end(behind[s], core)
        to_sibling(forward, behind[s], core)

    def prefill_past():
        arrive(keys.at[past, y, 1, core], z_recv.at[0, 0, 1])
        n = 2 * (half - 1)
        along_y(forward, n, core, lambda: keys.at[past, y, 1, core], 1, 0)

    def prefill_past_end():
        n = 2 * (half - 1)
        spot = lambda: keys.at[past, low, 1, core]
        arrive(spot(), y_recv.at[n, 0])
        forward(
            spot,
            lambda: device(to_core=1 - core),
            lambda: sib_send.at[n],
            lambda: sib_recv.at[n],
        )

    def from_sibling(n):
        arrive(keys.at[planes[n], :, :, 1 - core], sib_recv.at[n])

    def on(at, event):
        @pl.when(at)
        def _():
            event()

    top[...] = jnp.full(top.shape, masked_low, jnp.float32)
    total[...] = jnp.zeros(total.shape, jnp.float32)
    acc[...] = jnp.zeros(acc.shape, jnp.float32)

    token = lax.broadcasted_iota(jnp.int32, (tokens, 1), 0)
    position = seq * tokens + token
    count = lengths.shape[1]
    before_it = lax.broadcasted_iota(jnp.int32, (count, count), 0) < lax.broadcasted_iota(
        jnp.int32, (count, count), 1
    )
    earlier = jnp.where(before_it, 1.0, 0.0).astype(jnp.bfloat16)
    wide = jnp.broadcast_to(lengths[...], (8, count))
    digits = [(wide // 64).astype(jnp.bfloat16), (wide % 64).astype(jnp.bfloat16)]
    upper, lower = [jnp.dot(d, earlier, preferred_element_type=jnp.float32) for d in digits]
    starts = (upper * 64.0 + lower)[:1]
    row_low = jnp.max(
        jnp.where(starts <= position.astype(jnp.float32), starts, 0.0), axis=1, keepdims=True
    ).astype(jnp.int32)

    chunk = plane_keys // 2
    tile_heads = near // 2

    def fold(asked_heads, tile, key_block):
        count = key_block.shape[0]
        tile_heads = asked_heads.shape[0]
        rows = tile_heads * tokens
        part = pl.ds(pl.multiple_of(tile * rows, rows), rows)
        asked = asked_heads[...].reshape(rows, width)
        s = lax.dot_general(asked, key_block, nt, preferred_element_type=jnp.float32)
        s = (s.reshape(tile_heads, tokens, count) + bias[:, :count][None]).reshape(rows, count)
        before = top[part, :]
        now = jnp.maximum(before, jnp.max(s, axis=1, keepdims=True))
        shrink = jnp.exp2((before - now) * exponent_scale)
        expo = jnp.exp2((s - over_lanes(now, count)) * exponent_scale)
        top[part, :] = now
        summed = total[part, :] * shrink
        for c in range(0, count, LANES):
            summed = summed + expo[:, c : c + LANES]
        total[part, :] = summed
        acc[part, :] = acc[part, :] * over_lanes(shrink, kv_rank) + jnp.dot(
            expo.astype(jnp.bfloat16),
            key_block[:, :kv_rank],
            preferred_element_type=jnp.float32,
        )

    def past_from_sibling():
        arrive(keys.at[past, low, 1, 1 - core], sib_recv.at[2 * (half - 1)])

    last_step = 4 * (half + 1)
    timetable = [
        (prefill_chain, CHAIN_STEPS),
        (prefill_on, ON_STEPS),
        (prefill_end, END_STEPS),
        (lambda s: from_sibling(behind[s]), SIBLING_STEPS),
    ]
    events = {0: [prefill_start]}
    for s in range(1, half + 1):
        for event, at_steps in timetable:
            if at_steps[s - 1] > 0:
                spot = events.setdefault(at_steps[s - 1], [])
                spot.append(functools.partial(event, s))
    for event, at_step in zip((prefill_past, prefill_past_end, past_from_sibling), PAST_STEPS):
        events.setdefault(at_step, []).append(event)

    @pl.when(section == 0)
    def _():
        mid = plane_blocks // 2
        at_first, at_mid = at_block == 0, at_block == mid
        reaches_past = at_first & (z > half)

        @pl.loop(0, last_step)
        def _(step):
            for at_step in sorted(events):
                for event in events[at_step]:
                    on(step == at_step, event)

            run = step // 2
            turn = step % 2
            rest = run == 2 * half + 1
            back = jnp.where(rest, 0, (run + 1) // 2)
            side = jnp.where(run == 0, 0, (run + 1) % 2)
            side = jnp.where(rest, 1, side)
            slot = jnp.where(rest, 1, back % 2)
            reached = z >= back

            def load(back, part, slot, into):
                plane = lax.rem(z - back + z_count, z_count)
                here = keys.at[plane, pl.ds(part * (y_count // 2), y_count // 2)]
                return pltpu.make_async_copy(here, held.at[slot, into], held_sems.at[slot, into])

            def load_first():
                return pltpu.make_async_copy(
                    keys.at[past, y_count - 1, 1], held.at[1, 0, 0, 0], held_sems.at[1, 0]
                )

            def load_mid():
                return pltpu.make_async_copy(
                    keys.at[planes[-1], y_count // 2 - 1, 1],
                    held.at[1, 1, y_count // 2 - 1, 1],
                    held_sems.at[1, 0],
                )

            @pl.when(step == 0)
            def _():
                load(0, 0, 0, 0).start()

            for s in range(1, half + 1):

                @pl.when((step == SIBLING_STEPS[s - 1]) & (z >= s))
                def _():
                    load(s, 0, s % 2, 0).start()
                    load(s, 1, s % 2, 1).start()

            @pl.when(step == last_step - 5)
            def _():
                @pl.when(reaches_past)
                def _():
                    load_first().start()

                @pl.when(at_block >= mid)
                def _():
                    rest_load = load(0, 1, 1, 1)
                    rest_load.start()
                    rest_load.wait()

                @pl.when(at_mid)
                def _():
                    load_mid().start()

            @pl.when(reached & (turn == 0) & jnp.logical_not(rest))
            def _():
                load(back, side, slot, side).wait()

            at_past = reaches_past & (run == 2 * half)

            @pl.when(at_past & (turn == 0))
            def _():
                load_first().wait()

            @pl.when((turn == 0) & rest & at_mid)
            def _():
                load_mid().wait()

            none = (rest & (at_block < mid)) | ((run == 2 * half - 1) & (at_block >= mid))
            first_spot = (z - back) * plane_keys + side * chunk

            @pl.when(reached & jnp.logical_not(none))
            def _():
                @pl.when(turn == 0)
                def _():
                    lane = lax.broadcasted_iota(jnp.int32, (1, chunk + tokens), 1)
                    spot = first_spot + lane
                    shift = (half * plane_keys) + chunk
                    spot = jnp.where(
                        rest & at_mid & (lane >= chunk - tokens), spot - shift, spot
                    )
                    spot = jnp.where(lane >= chunk, spot - plane_keys - tokens, spot)
                    seen = (spot >= row_low) & (spot <= position)
                    bias[...] = jnp.where(seen, 0.0, masked_low)

                here = held.at[slot, side]
                tile_q = q.at[pl.ds(turn * tile_heads, tile_heads)]

                @pl.when(at_past)
                def _():
                    behind_it = held[1, 0, 0, 0].reshape(tokens, width)
                    key_block = jnp.concatenate([here[...].reshape(chunk, width), behind_it])

                    fold(tile_q, turn, key_block)

                @pl.when(jnp.logical_not(at_past))
                def _():
                    fold(tile_q, turn, here[...].reshape(chunk, width))

    def far_run(run):
        rest, beyond = run == 2 * half + 1, run == 2 * half + 2
        back = jnp.where(rest, 0, jnp.where(beyond, half + 1, (run + 1) // 2))
        side = jnp.where(run == 0, 0, jnp.where(rest | beyond, 1, (run + 1) % 2))
        slot = run % 2
        middle = plane_blocks // 2
        wanted = z >= back
        wanted = wanted & jnp.logical_not(rest & (at_block < middle))
        wanted = wanted & jnp.logical_not((run == 2 * half - 1) & (at_block > middle))
        wanted = wanted & jnp.logical_not(beyond & (at_block > 0))
        plane = lax.rem(z - back + z_count, z_count)
        load = pltpu.make_async_copy(
            keys.at[plane, pl.ds(side * (y_count // 2), y_count // 2)],
            held.at[slot, 0],
            held_sems.at[slot, 0],
        )
        return wanted, load, (z - back) * plane_keys + side * chunk, slot

    def start_far(run):
        wanted, load, _, _ = far_run(run)

        @pl.when(wanted)
        def _():
            load.start()

    def far_runs(begin, end):
        start_far(jnp.int32(begin))

        @pl.loop(begin, end)
        def _(run):
            @pl.when(run + 1 < end)
            def _():
                start_far(run + 1)

            wanted, load, first_spot, slot = far_run(run)

            @pl.when(wanted)
            def _():
                load.wait()
                spot = first_spot + lax.broadcasted_iota(jnp.int32, (1, chunk), 1)
                seen = (spot >= row_low) & (spot <= position)
                bias[:, :chunk] = jnp.where(seen, 0.0, masked_low)
                fold(far_q, 0, held[slot, 0].reshape(chunk, width))

    def project(head, part):
        norm = 1.0 / jnp.sum(total[part, :], axis=1, keepdims=True)
        mixed = (acc[part, :] * norm).astype(jnp.bfloat16)
        ready[head] = jnp.dot(mixed, up[head], preferred_element_type=jnp.float32).astype(
            jnp.bfloat16
        )

    @pl.when(section == 1)
    def _():
        for stage in range(half + 1):
            on(core == 0, functools.partial(decode_a, stage))
            on(core == 1, functools.partial(decode_b, stage))
            if stage == 1:
                arrive(far_nope, far_recv.at[0])
                arrive(far_rope, far_recv.at[1])
                absorb(far_nope, far_rope, far_q, near, FAR_HEADS)
                load_value_up().start()
            if 0 < stage < half:
                for n in steps[stage - 1]:
                    from_sibling(n)
                far_runs(max(2 * stage - 3, 0), 2 * stage - 1)
        for n in steps[half - 1] + steps[half]:
            from_sibling(n)
        far_runs(2 * half - 3, 2 * half + 3)
        load_value_up().wait()

        @pl.loop(0, FAR_HEADS // 2)
        def _(pair):
            for side in range(2):
                head = pair * 2 + side
                project(near + head, pl.ds(pl.multiple_of(head * tokens, tokens), tokens))

        far_result().start()

    @pl.when(section == 0)
    def _():
        load_value_up().wait()

        @pl.loop(0, near // 2)
        def _(pair):
            for side in range(2):
                head = pair * 2 + side
                project(head, pl.ds(pl.multiple_of(head * tokens, tokens), tokens))

        arrive(ready.at[pl.ds(near, FAR_HEADS)], far_recv.at[2])
        raw[...] = jnp.swapaxes(ready[...], 0, 1)
        done = pltpu.make_async_copy(raw, out, out_sems.at[1])
        done.start()
        done.wait()
        for copy in x_copies() + far_copies():
            copy.wait_send()

    @pl.when(section == 1)
    def _():
        pltpu.make_async_copy(q, q_out, out_sems.at[0]).wait()
        far_result().wait_send()

    groups = [section == 0, (section == 1) & (core == 0), (section == 1) & (core == 1)]
    for group, copies in zip(groups, went):

        @pl.when(group)
        def _():
            for copy in copies:
                copy().wait_send()

    arrive(own_out.at[1 - core], own_sems.at[2])
    own_away().wait_send()
    own_local().wait()


def prefill_part(own, q_nope, q_rope, up_key, value_up, lengths, seq_count, exponent_scale):
    rows, width = own.shape
    tokens, heads, nope_dim = q_nope.shape
    kv_rank = up_key.shape[1]
    y_count = 4
    z_count = seq_count // (2 * y_count)
    dma = pltpu.SemaphoreType.DMA
    bf16 = own.dtype
    chunk = y_count * tokens
    vmem = pl.BlockSpec(memory_space=pltpu.VMEM)
    hbm = pl.BlockSpec(memory_space=pl.ANY)
    return pl.pallas_call(
        functools.partial(prefill_kernel, z_count, y_count, kv_rank, exponent_scale),
        out_shape=[
            jax.ShapeDtypeStruct((z_count, y_count, 2, 2, rows, width), bf16),
            jax.ShapeDtypeStruct((2, rows, width), bf16),
            jax.ShapeDtypeStruct((heads, tokens, width), bf16),
            jax.ShapeDtypeStruct((tokens, heads, value_up.shape[2]), bf16),
        ],
        in_specs=[vmem, hbm, vmem, hbm, hbm, vmem],
        out_specs=[hbm] * 4,
        scratch_shapes=[
            pltpu.VMEM((rows, width), bf16),
            pltpu.VMEM(q_nope.shape, bf16),
            pltpu.VMEM((heads, tokens, nope_dim), bf16),
            pltpu.VMEM(up_key.shape, bf16),
            pltpu.VMEM((heads, tokens, width), bf16),
            pltpu.VMEM((FAR_HEADS, tokens, nope_dim), bf16),
            pltpu.VMEM((tokens, FAR_HEADS * (width - kv_rank)), bf16),
            pltpu.VMEM((FAR_HEADS, tokens, width), bf16),
            pltpu.VMEM(((heads - FAR_HEADS) * tokens, kv_rank), jnp.float32),
            pltpu.VMEM(((heads - FAR_HEADS) * tokens, LANES), jnp.float32),
            pltpu.VMEM(((heads - FAR_HEADS) * tokens, LANES), jnp.float32),
            pltpu.VMEM((2, 2, y_count // 2, 2, 2, rows, width), bf16),
            pltpu.VMEM((tokens, chunk + tokens), jnp.float32),
            pltpu.VMEM((heads, tokens, value_up.shape[2]), bf16),
            dma((3,)),
            dma((3,)),
            dma((2,)),
            dma((2,)),
            dma((2, 2)),
            dma((4,)),
            dma((2,)),
            dma((3,)),
            dma((2, z_count // 2, y_count)),
            dma((2, z_count // 2, y_count)),
            dma((z_count, 4)),
            dma((z_count, 4)),
            dma((z_count,)),
            dma((z_count,)),
        ],
        compiler_params=pltpu.CompilerParams(
            collective_id=0, has_side_effects=True, vmem_limit_bytes=56 << 20
        ),
    )(own, q_nope, q_rope, up_key, value_up, lengths)


def over_lanes(value, width):
    return jnp.concatenate([value] * (width // LANES), axis=1)


def decode_kernel(
    kv_rank,
    groups,
    exponent_scale,
    lengths,
    table,
    q_ref,
    keys,
    own_keys,
    value_up,
    prefill_out,
    out_ref,
    acc,
    top,
    total,
    held,
    lat,
    up,
    ready,
    turned,
    q_held,
    sems,
    q_sems,
    up_sems,
):
    band = pl.program_id(0)
    bands = pl.num_programs(0)
    _, heads, tokens, width = q_held.shape
    rows = heads * tokens
    all_keys = keys.shape[0]
    nt = (((1,), (1,)), ((), ()))

    @pl.when(lax.axis_index("section") == 0)
    def _():
        taken = pltpu.make_async_copy(prefill_out, turned, up_sems.at[0])
        handed = pltpu.make_async_copy(turned, out_ref, up_sems.at[1])

        @pl.when(band == 0)
        def _():
            taken.start()
            taken.wait()
            handed.start()

        @pl.when(band == bands - 1)
        def _():
            handed.wait()

    @pl.when(lax.axis_index("section") == 1)
    def _():
        def prompt_range(which):
            prompt = table[lax.axis_index("seq") * bands + which] // groups
            low = lax.fori_loop(0, prompt, lambda k, at: at + lengths[k], jnp.int32(0))
            return low, low + lengths[prompt]

        def chunk_at(start, i):
            return pl.multiple_of(jnp.minimum(start + i * KEY_BLOCK, all_keys - KEY_BLOCK), 16)

        def fetch_from(start, i, slot):
            return pltpu.make_async_copy(
                keys.at[pl.ds(chunk_at(start, i), KEY_BLOCK), :], held.at[slot], sems.at[slot]
            )

        def band_rows(which):
            return pl.ds(pl.multiple_of(which * tokens, tokens), tokens)

        def fetch_q(which):
            slot = lax.rem(which, 2)
            return pltpu.make_async_copy(
                q_ref.at[:, band_rows(which), :], q_held.at[slot], q_sems.at[slot]
            )

        def load_up():
            return pltpu.make_async_copy(value_up, up, up_sems.at[0])

        low, last = prompt_range(band)
        first = low // 16 * 16
        chunks = (last - first + KEY_BLOCK - 1) // KEY_BLOCK

        def fetch(i):
            slot = jnp.where(i == 0, lax.rem(band, 2), 2 + lax.rem(i, 2))
            return fetch_from(first, i, slot)

        @pl.when(band == 0)
        def _():
            fetch_q(0).start()
            fetch(0).start()
            load_up().start()

        @pl.when(band + 1 < bands)
        def _():
            fetch_q(band + 1).start()
            next_low, _ = prompt_range(band + 1)
            fetch_from(next_low // 16 * 16, 0, lax.rem(band + 1, 2)).start()

        fetch_q(band).wait()
        q = q_held[lax.rem(band, 2)].reshape(rows, width)
        def score(key_block):
            return lax.dot_general(q, key_block, nt, preferred_element_type=jnp.float32)

        def in_range(at, count, low_spot):
            spot = at + lax.broadcasted_iota(jnp.int32, (1, count), 1)
            return jnp.where((spot >= jnp.maximum(low, low_spot)) & (spot < last), 0.0, masked_low)

        def weigh(scores, now):
            return jnp.exp2((scores - now) * exponent_scale)

        def mix(weights, key_block):
            return jnp.dot(
                weights.astype(jnp.bfloat16),
                key_block[:, :kv_rank],
                preferred_element_type=jnp.float32,
            )

        def begin(key_block, at):
            own = own_keys[...]
            asked = lax.broadcasted_iota(jnp.int32, (tokens, tokens), 0)
            key = lax.broadcasted_iota(jnp.int32, (tokens, tokens), 1)
            seen = (asked % SAMPLES == key % SAMPLES) & (key // SAMPLES <= asked // SAMPLES)
            bias = jnp.where(seen, 0.0, masked_low)
            bias = jnp.broadcast_to(bias[None], (heads, tokens, tokens)).reshape(rows, tokens)
            new = score(own) + bias
            count = key_block.shape[0]
            old = score(key_block) + in_range(at, count, low)
            now = jnp.maximum(
                jnp.max(new, axis=1, keepdims=True), jnp.max(old, axis=1, keepdims=True)
            )
            new = weigh(new, now)
            old = weigh(old, now)
            top[...] = jnp.broadcast_to(now, (rows, LANES))
            lane = lax.broadcasted_iota(jnp.int32, (rows, LANES), 1)
            summed = jnp.where(lane == 0, jnp.sum(new, axis=1, keepdims=True), 0.0)
            for c in range(0, count, LANES):
                summed = summed + old[:, c : c + LANES]
            total[...] = summed
            acc[...] = mix(new, own) + mix(old, key_block)

        def fold(key_block, low_spot, at):
            count = key_block.shape[0]
            s = score(key_block)
            if low_spot is not None:
                s = s + in_range(at, count, low_spot)
            before = top[...]
            now = jnp.maximum(before, jnp.max(s, axis=1, keepdims=True))
            shrink = jnp.exp2((before - now) * exponent_scale)
            expo = weigh(s, over_lanes(now, count))
            top[...] = now
            summed = total[...] * shrink
            for c in range(0, count, LANES):
                summed = summed + expo[:, c : c + LANES]
            total[...] = summed
            acc[...] = acc[...] * over_lanes(shrink, kv_rank) + mix(expo, key_block)

        @pl.loop(0, chunks)
        def _(i):
            slot = jnp.where(i == 0, lax.rem(band, 2), 2 + lax.rem(i, 2))
            fetch(i).wait()

            @pl.when(i + 1 < chunks)
            def _():
                fetch(i + 1).start()

            nominal = first + i * KEY_BLOCK
            at = chunk_at(first, i)
            whole = (i > 0) & (nominal + KEY_BLOCK <= last)
            skip = (nominal - at) // EDGE_BLOCK

            @pl.when(i == 0)
            def _():
                here = pl.multiple_of(skip * EDGE_BLOCK, EDGE_BLOCK)
                begin(held[slot, pl.ds(here, EDGE_BLOCK), :], at + here)

            @pl.when(whole)
            def _():
                fold(held[slot], None, None)

            @pl.when(jnp.logical_not(whole))
            def _():
                begun = skip + jnp.where(i == 0, 1, 0)

                @pl.loop(begun, (jnp.minimum(last - at, KEY_BLOCK) + EDGE_BLOCK - 1) // EDGE_BLOCK)
                def _(j):
                    here = pl.multiple_of(j * EDGE_BLOCK, EDGE_BLOCK)
                    fold(held[slot, pl.ds(here, EDGE_BLOCK), :], nominal, at + here)

        norm = 1.0 / jnp.sum(total[...], axis=1, keepdims=True)
        lat[:, band_rows(band), :] = (
            (acc[...] * norm).astype(jnp.bfloat16).reshape(heads, tokens, kv_rank)
        )

        @pl.when(band == bands - 1)
        def _():
            load_up().wait()

            @pl.loop(0, heads // 4)
            def _(four):
                picked = [four * 4 + k for k in range(4)]
                products = [
                    jnp.dot(lat[head], up[head], preferred_element_type=jnp.float32)
                    for head in picked
                ]
                for head, product in zip(picked, products):
                    ready[head] = product.astype(jnp.bfloat16)

            turned[...] = jnp.swapaxes(ready[...], 0, 1)
            done = pltpu.make_async_copy(turned, out_ref, up_sems.at[1])
            done.start()
            done.wait()


def shards(query_nope, query_rope, latent, up_key, value_up_weight, lengths, owner_request_table):
    seq_count = lax.axis_size("seq")
    tok_dev, head_dev, nope_dim = query_nope.shape[1:]
    rope_dim = query_rope.shape[2] // head_dev
    kv_rank = up_key.shape[1]
    width = kv_rank + rope_dim
    v_dim = value_up_weight.shape[2]
    req_dev = owner_request_table.shape[0] // seq_count
    groups = owner_request_table.shape[0] // lengths.shape[0]
    band_tokens = tok_dev // req_dev
    exponent_scale = math.log2(math.e) / math.sqrt(nope_dim + rope_dim)

    keys, pair, queries, prefill_out = prefill_part(
        latent[0],
        query_nope[0],
        query_rope[0],
        up_key,
        value_up_weight,
        lengths[None, :],
        seq_count,
        exponent_scale,
    )
    rows = head_dev * band_tokens
    attended = pl.pallas_call(
        functools.partial(decode_kernel, kv_rank, groups, exponent_scale),
        out_shape=jax.ShapeDtypeStruct(prefill_out.shape, jnp.bfloat16),
        grid_spec=pltpu.PrefetchScalarGridSpec(
            num_scalar_prefetch=2,
            grid=(req_dev,),
            in_specs=[
                pl.BlockSpec(memory_space=pl.ANY),
                pl.BlockSpec(memory_space=pl.ANY),
                pl.BlockSpec((band_tokens, width), lambda i, *_: (i, 0)),
                pl.BlockSpec(memory_space=pl.ANY),
                pl.BlockSpec(memory_space=pl.ANY),
            ],
            out_specs=pl.BlockSpec(memory_space=pl.ANY),
            scratch_shapes=[
                pltpu.VMEM((rows, kv_rank), jnp.float32),
                pltpu.VMEM((rows, LANES), jnp.float32),
                pltpu.VMEM((rows, LANES), jnp.float32),
                pltpu.VMEM((4, KEY_BLOCK, width), jnp.bfloat16),
                pltpu.VMEM((head_dev, tok_dev, kv_rank), jnp.bfloat16),
                pltpu.VMEM(value_up_weight.shape, jnp.bfloat16),
                pltpu.VMEM((head_dev, tok_dev, v_dim), jnp.bfloat16),
                pltpu.VMEM(prefill_out.shape, jnp.bfloat16),
                pltpu.VMEM((2, head_dev, band_tokens, width), jnp.bfloat16),
                pltpu.SemaphoreType.DMA((4,)),
                pltpu.SemaphoreType.DMA((2,)),
                pltpu.SemaphoreType.DMA((2,)),
            ],
        ),
        compiler_params=pltpu.CompilerParams(vmem_limit_bytes=58 << 20),
    )(
        lengths,
        owner_request_table,
        queries,
        keys.reshape(-1, width),
        pair.reshape(-1, width),
        value_up_weight,
        prefill_out,
    )

    return attended[None]


def solution(mesh):
    in_specs = (
        P("section", "seq", "head", None),
        P("section", "seq", "head"),
        P("section", ("seq", "head"), None),
        P("head", None, None),
        P("head", None, None),
        P(),
        P(),
    )
    out_specs = P("section", "seq", "head", None)
    return jax.shard_map(shards, mesh=mesh, in_specs=in_specs, out_specs=out_specs, check_vma=False)
```

```python
import functools
import math

import jax
import jax.numpy as jnp
from jax import lax
from jax.experimental import pallas as pl
from jax.experimental.pallas import tpu as pltpu
from jax.sharding import PartitionSpec as P

SAMPLES = 8
STEPS = 4
BLOCK = 64

scale_top = 448.0
tiny_eps = 1e-06
masked_low = -1e30

KEY_BLOCK = 1024
EDGE_BLOCK = 512
FAR_HEADS = 6

CHAIN_STEPS = (0, 1, 3, 5)
ON_STEPS = (0, 2, 5, 8)
END_STEPS = (1, 3, 7, 10)
SIBLING_STEPS = (2, 5, 9, 13)
PAST_STEPS = (8, 10, 15)
LANES = 128


def prefill_kernel(
    z_count, y_count, kv_rank, exponent_scale, own_in, q_nope, q_rope, up_key, value_up, lengths,
    keys, own_out, q_out, out, block, raw, nope, up, q, far_nope, far_rope, far_q, acc, top, total,
    held, bias, ready, far_send, far_recv,
    in_sems, out_sems, held_sems, x_send, x_recv, own_sems,
    z_send, z_recv, y_send, y_recv, sib_send, sib_recv,
):
    section = lax.axis_index("section")
    seq = lax.axis_index("seq")
    core = lax.axis_index("head")
    z = seq // (2 * y_count)
    y = seq // 2 % y_count
    hi = seq % 2
    half = z_count // 2
    heads, tokens, width = q.shape
    plane_blocks = 2 * y_count
    at_block = seq % plane_blocks
    plane_keys = plane_blocks * tokens
    nt = (((1,), (1,)), ((), ()))

    def plane_at(dz):
        return lax.rem(z + dz + z_count, z_count)

    def row_at(dy):
        return lax.rem(y + dy + y_count, y_count)

    def device(dz=0, dy=0, to_hi=None, to_section=None, to_core=None):
        th = hi if to_hi is None else to_hi
        return (
            section if to_section is None else to_section,
            (plane_at(dz) * y_count + row_at(dy)) * 2 + th,
            core if to_core is None else to_core,
        )

    loads = [
        pltpu.make_async_copy(q_nope, raw, in_sems.at[0]),
        pltpu.make_async_copy(up_key, up, in_sems.at[1]),
    ]
    for load in loads:
        load.start()

    barrier = pltpu.get_barrier_semaphore()
    peers = [
        device(to_core=1 - core),
        device(to_section=1 - section),
        device(to_hi=1 - hi),
        device(to_section=1 - section, to_hi=1 - hi),
        device(dz=1),
        device(dz=-1),
        device(dy=1),
        device(dy=-1),
    ]
    for peer in peers:
        pl.semaphore_signal(barrier, inc=1, device_id=peer, device_id_type=pl.DeviceIdType.MESH)

    @pl.when(section == 0)
    def _():
        rows = own_in[...].astype(jnp.float32)
        largest = jnp.max(jnp.abs(rows))
        spread = jnp.full((8, LANES), largest, jnp.float32)
        scale = ((spread + tiny_eps) / scale_top).astype(jnp.bfloat16).astype(jnp.float32)
        factor = scale[:1, :1]
        stored = (rows / factor).astype(jnp.bfloat16)
        block[...] = (stored.astype(jnp.float32) * factor).astype(jnp.bfloat16)

    @pl.when(section == 1)
    def _():
        block[...] = own_in[...]

    pl.semaphore_wait(barrier, len(peers))

    def remote(src, dst, to, send_sem, recv_sem):
        return pltpu.make_async_remote_copy(
            src_ref=src,
            dst_ref=dst,
            send_sem=send_sem,
            recv_sem=recv_sem,
            device_id=to,
            device_id_type=pl.DeviceIdType.MESH,
        )

    def arrive(dst, recv_sem):
        remote(dst, dst, device(to_core=1 - core), recv_sem, recv_sem).wait_recv()

    def own_local():
        return pltpu.make_async_copy(block, own_out.at[core], own_sems.at[0])

    def own_away():
        to = device(to_core=1 - core)
        return remote(block, own_out.at[core], to, own_sems.at[1], own_sems.at[2])

    def x_copies():
        spot = keys.at[z, y, hi, core]
        return [
            remote(block, spot, device(to_hi=1 - hi), x_send.at[2], x_recv.at[1]),
            remote(block, spot, device(to_section=1), x_send.at[0], x_recv.at[0]),
            remote(block, spot, device(to_section=1, to_hi=1 - hi), x_send.at[1], x_recv.at[1]),
        ]

    def x_local():
        return pltpu.make_async_copy(block, keys.at[z, y, hi, core], x_send.at[3])

    @pl.when(section == 0)
    def _():
        x_local().start()
        for copy in x_copies():
            copy.start()

    own_local().start()
    own_away().start()

    for load in loads:
        load.wait()
    nope[...] = jnp.swapaxes(raw[...], 0, 1)

    near = heads - FAR_HEADS
    half_lanes = LANES // 2

    def far_copies():
        to = device(to_section=1 - section)
        rope_part = q_rope.at[:, pl.ds(near * half_lanes, FAR_HEADS * half_lanes)]
        return [
            remote(nope.at[pl.ds(near, FAR_HEADS)], far_nope, to, far_send.at[0], far_recv.at[0]),
            remote(rope_part, far_rope, to, far_send.at[1], far_recv.at[1]),
        ]

    def far_result():
        part = ready.at[pl.ds(near, FAR_HEADS)]
        return remote(part, part, device(to_section=1 - section), far_send.at[2], far_recv.at[2])

    @pl.when(section == 0)
    def _():
        for copy in far_copies():
            copy.start()

    def absorb(from_nope, from_rope, into, first, count):
        @pl.loop(0, count // 2)
        def _(pair):
            rope = from_rope[:, pl.ds(pl.multiple_of(pair * LANES, LANES), LANES)]
            for side in range(2):
                head = pair * 2 + side
                lifted = lax.dot_general(
                    from_nope[head], up[first + head], nt, preferred_element_type=jnp.float32
                )
                into[head, :, :kv_rank] = lifted.astype(jnp.bfloat16)
                into[head, :, kv_rank:] = rope[:, side * half_lanes : (side + 1) * half_lanes]

    @pl.when(section == 0)
    def _():
        absorb(nope, q_rope, q, 0, near)

    @pl.when(section == 1)
    def _():
        absorb(nope, q_rope, q, 0, heads)

    def load_value_up():
        return pltpu.make_async_copy(value_up, up, in_sems.at[1])

    @pl.when(section == 0)
    def _():
        load_value_up().start()

    @pl.when(section == 1)
    def _():
        pltpu.make_async_copy(q, q_out, out_sems.at[0]).start()

    @pl.when(section == 0)
    def _():
        x_local().wait()
        arrive(keys.at[z, y, 1 - hi, core], x_recv.at[1])

    @pl.when(section == 1)
    def _():
        arrive(keys.at[z, y, hi, core], x_recv.at[0])
        arrive(keys.at[z, y, 1 - hi, core], x_recv.at[1])

    low, high, far = row_at(-1), row_at(1), row_at(2)
    columns = [y, low, high, far]
    planes = [z]
    for s in range(1, half):
        planes += [plane_at(-s), plane_at(s)]
    planes.append(plane_at(half))
    steps = [[0]] + [[2 * s - 1, 2 * s] for s in range(1, half)] + [[z_count - 1]]

    def sender(went):
        def send(src, to, send_sem, recv_sem):
            copy = lambda: remote(src(), src(), to(), send_sem(), recv_sem())
            went.append(copy)
            copy().start()

        return send

    went = [[], [], []]

    def along_y(send, n, c, src, d, k):
        send(src, lambda: device(dy=d), lambda: y_send.at[n, k], lambda: y_recv.at[n, k])

    def spread(send, n, c):
        mine = lambda: keys.at[planes[n], y, :, c]
        along_y(send, n, c, mine, 1, 0)
        along_y(send, n, c, mine, -1, 1)

    def spread_on(send, n, c):
        arrive(keys.at[planes[n], low, :, c], y_recv.at[n, 0])
        along_y(send, n, c, lambda: keys.at[planes[n], low, 0, c], 1, 2)
        arrive(keys.at[planes[n], high, :, c], y_recv.at[n, 1])
        along_y(send, n, c, lambda: keys.at[planes[n], high, 1, c], -1, 3)

    def spread_end(n, c):
        arrive(keys.at[planes[n], far, 0, c], y_recv.at[n, 2])
        arrive(keys.at[planes[n], far, 1, c], y_recv.at[n, 3])

    def to_sibling(send, n, c):
        send(
            lambda: keys.at[planes[n], :, :, c],
            lambda: device(to_core=1 - c),
            lambda: sib_send.at[n],
            lambda: sib_recv.at[n],
        )

    def along_z(send, src, up_way, step, k):
        d, j = (1, 0) if up_way else (-1, 1)
        send(
            src,
            lambda: device(dz=d),
            lambda: z_send.at[j, step, k],
            lambda: z_recv.at[j, step, k],
        )

    ways = ((0, True), (1, False))

    def decode_a(stage):
        send = sender(went[1])

        def cell(n, k):
            return lambda: keys.at[planes[n], columns[k], :, 0]

        def column(k):
            for _, up_way in ways:
                along_z(send, cell(0, k), up_way, 0, k)

        if stage == 0:
            spread(send, 0, 0)
            column(0)
            arrive(keys.at[z, low, :, 0], y_recv.at[0, 0])
            along_y(send, 0, 0, lambda: keys.at[z, low, 0, 0], 1, 2)
            column(1)
            arrive(keys.at[z, high, :, 0], y_recv.at[0, 1])
            along_y(send, 0, 0, lambda: keys.at[z, high, 1, 0], -1, 3)
            column(2)
            spread_end(0, 0)
            column(3)
            to_sibling(send, 0, 0)
        elif stage < half:
            for k in range(y_count):
                for n, (j, up_way) in zip(steps[stage], ways):
                    arrive(cell(n, k)(), z_recv.at[j, stage - 1, k])
                    if stage < half - 1 or k // 2 == j:
                        along_z(send, cell(n, k), up_way, stage, k)
            for n in steps[stage]:
                to_sibling(send, n, 0)
        else:
            for k in range(y_count):
                arrive(cell(z_count - 1, k)(), z_recv.at[k // 2, half - 1, k])
            to_sibling(send, z_count - 1, 0)

    def decode_b(stage):
        send = sender(went[2])

        def ahead(n, s, j, up_way):
            if s < half - 1:
                part = lambda: keys.at[planes[n], y, :, 1]
            else:
                part = lambda: keys.at[planes[n], y, j, 1]
            along_z(send, part, up_way, s, 0)

        def chain(s):
            for n, (j, up_way) in zip(steps[s], ways):
                arrive(keys.at[planes[n], y, :, 1], z_recv.at[j, s - 1, 0])
                ahead(n, s, j, up_way)
                spread(send, n, 1)

        def finish(s):
            for n in steps[s]:
                spread_end(n, 1)
                to_sibling(send, n, 1)

        if stage == 0:
            for j, up_way in ways:
                ahead(0, 0, j, up_way)
            spread(send, 0, 1)
            chain(1)
            spread_on(send, 0, 1)
            return
        if stage + 1 < half:
            chain(stage + 1)
        elif stage + 1 == half:
            for j in range(2):
                arrive(keys.at[planes[-1], y, j, 1], z_recv.at[j, half - 1, 0])
            spread(send, z_count - 1, 1)
        for n in steps[stage]:
            spread_on(send, n, 1)
        finish(stage - 1)
        if stage == half:
            finish(stage)

    behind = [0] + [2 * s - 1 for s in range(1, half)] + [z_count - 1]
    past = planes[2 * (half - 1)]
    forward = sender(went[0])

    def ahead(n, s):
        along_z(forward, lambda: keys.at[planes[n], y, :, core], True, s, 0)

    def prefill_start():
        ahead(0, 0)
        spread(forward, 0, core)
        prefill_chain(1)
        spread_on(forward, 0, core)
        spread_end(0, core)
        to_sibling(forward, 0, core)
        prefill_on(1)
        from_sibling(0)

    def prefill_chain(s):
        n = behind[s]
        arrive(keys.at[planes[n], y, :, core], z_recv.at[0, s - 1, 0])
        if s < half:
            ahead(n, s)
        else:
            along_z(forward, lambda: keys.at[planes[n], y, 1, core], True, 0, 1)
        spread(forward, n, core)

    def prefill_on(s):
        spread_on(forward, behind[s], core)

    def prefill_end(s):
        spread_end(behind[s], core)
        to_sibling(forward, behind[s], core)

    def prefill_past():
        arrive(keys.at[past, y, 1, core], z_recv.at[0, 0, 1])
        n = 2 * (half - 1)
        along_y(forward, n, core, lambda: keys.at[past, y, 1, core], 1, 0)

    def prefill_past_end():
        n = 2 * (half - 1)
        spot = lambda: keys.at[past, low, 1, core]
        arrive(spot(), y_recv.at[n, 0])
        forward(
            spot,
            lambda: device(to_core=1 - core),
            lambda: sib_send.at[n],
            lambda: sib_recv.at[n],
        )

    def from_sibling(n):
        arrive(keys.at[planes[n], :, :, 1 - core], sib_recv.at[n])

    def on(at, event):
        @pl.when(at)
        def _():
            event()

    top[...] = jnp.full(top.shape, masked_low, jnp.float32)
    total[...] = jnp.zeros(total.shape, jnp.float32)
    acc[...] = jnp.zeros(acc.shape, jnp.float32)

    token = lax.broadcasted_iota(jnp.int32, (tokens, 1), 0)
    position = seq * tokens + token
    count = lengths.shape[1]
    before_it = lax.broadcasted_iota(jnp.int32, (count, count), 0) < lax.broadcasted_iota(
        jnp.int32, (count, count), 1
    )
    earlier = jnp.where(before_it, 1.0, 0.0).astype(jnp.bfloat16)
    wide = jnp.broadcast_to(lengths[...], (8, count))
    digits = [(wide // 64).astype(jnp.bfloat16), (wide % 64).astype(jnp.bfloat16)]
    upper, lower = [jnp.dot(d, earlier, preferred_element_type=jnp.float32) for d in digits]
    starts = (upper * 64.0 + lower)[:1]
    row_low = jnp.max(
        jnp.where(starts <= position.astype(jnp.float32), starts, 0.0), axis=1, keepdims=True
    ).astype(jnp.int32)

    chunk = plane_keys // 2
    tile_heads = near // 2

    def fold(asked_heads, tile, key_block):
        count = key_block.shape[0]
        tile_heads = asked_heads.shape[0]
        rows = tile_heads * tokens
        part = pl.ds(pl.multiple_of(tile * rows, rows), rows)
        asked = asked_heads[...].reshape(rows, width)
        s = lax.dot_general(asked, key_block, nt, preferred_element_type=jnp.float32)
        s = (s.reshape(tile_heads, tokens, count) + bias[:, :count][None]).reshape(rows, count)
        before = top[part, :]
        now = jnp.maximum(before, jnp.max(s, axis=1, keepdims=True))
        shrink = jnp.exp2((before - now) * exponent_scale)
        expo = jnp.exp2((s - over_lanes(now, count)) * exponent_scale)
        top[part, :] = now
        summed = total[part, :] * shrink
        for c in range(0, count, LANES):
            summed = summed + expo[:, c : c + LANES]
        total[part, :] = summed
        acc[part, :] = acc[part, :] * over_lanes(shrink, kv_rank) + jnp.dot(
            expo.astype(jnp.bfloat16),
            key_block[:, :kv_rank],
            preferred_element_type=jnp.float32,
        )

    def past_from_sibling():
        arrive(keys.at[past, low, 1, 1 - core], sib_recv.at[2 * (half - 1)])

    last_step = 4 * (half + 1)
    timetable = [
        (prefill_chain, CHAIN_STEPS),
        (prefill_on, ON_STEPS),
        (prefill_end, END_STEPS),
        (lambda s: from_sibling(behind[s]), SIBLING_STEPS),
    ]
    events = {0: [prefill_start]}
    for s in range(1, half + 1):
        for event, at_steps in timetable:
            if at_steps[s - 1] > 0:
                spot = events.setdefault(at_steps[s - 1], [])
                spot.append(functools.partial(event, s))
    for event, at_step in zip((prefill_past, prefill_past_end, past_from_sibling), PAST_STEPS):
        events.setdefault(at_step, []).append(event)

    @pl.when(section == 0)
    def _():
        mid = plane_blocks // 2
        at_first, at_mid = at_block == 0, at_block == mid
        reaches_past = at_first & (z > half)

        @pl.loop(0, last_step)
        def _(step):
            for at_step in sorted(events):
                for event in events[at_step]:
                    on(step == at_step, event)

            run = step // 2
            turn = step % 2
            rest = run == 2 * half + 1
            back = jnp.where(rest, 0, (run + 1) // 2)
            side = jnp.where(run == 0, 0, (run + 1) % 2)
            side = jnp.where(rest, 1, side)
            slot = jnp.where(rest, 1, back % 2)
            reached = z >= back

            def load(back, part, slot, into):
                plane = lax.rem(z - back + z_count, z_count)
                here = keys.at[plane, pl.ds(part * (y_count // 2), y_count // 2)]
                return pltpu.make_async_copy(here, held.at[slot, into], held_sems.at[slot, into])

            def load_first():
                return pltpu.make_async_copy(
                    keys.at[past, y_count - 1, 1], held.at[1, 0, 0, 0], held_sems.at[1, 0]
                )

            def load_mid():
                return pltpu.make_async_copy(
                    keys.at[planes[-1], y_count // 2 - 1, 1],
                    held.at[1, 1, y_count // 2 - 1, 1],
                    held_sems.at[1, 0],
                )

            @pl.when(step == 0)
            def _():
                load(0, 0, 0, 0).start()

            for s in range(1, half + 1):

                @pl.when((step == SIBLING_STEPS[s - 1]) & (z >= s))
                def _():
                    load(s, 0, s % 2, 0).start()
                    load(s, 1, s % 2, 1).start()

            @pl.when(step == last_step - 5)
            def _():
                @pl.when(reaches_past)
                def _():
                    load_first().start()

                @pl.when(at_block >= mid)
                def _():
                    rest_load = load(0, 1, 1, 1)
                    rest_load.start()
                    rest_load.wait()

                @pl.when(at_mid)
                def _():
                    load_mid().start()

            @pl.when(reached & (turn == 0) & jnp.logical_not(rest))
            def _():
                load(back, side, slot, side).wait()

            at_past = reaches_past & (run == 2 * half)

            @pl.when(at_past & (turn == 0))
            def _():
                load_first().wait()

            @pl.when((turn == 0) & rest & at_mid)
            def _():
                load_mid().wait()

            none = (rest & (at_block < mid)) | ((run == 2 * half - 1) & (at_block >= mid))
            first_spot = (z - back) * plane_keys + side * chunk

            @pl.when(reached & jnp.logical_not(none))
            def _():
                @pl.when(turn == 0)
                def _():
                    lane = lax.broadcasted_iota(jnp.int32, (1, chunk + tokens), 1)
                    spot = first_spot + lane
                    shift = (half * plane_keys) + chunk
                    spot = jnp.where(
                        rest & at_mid & (lane >= chunk - tokens), spot - shift, spot
                    )
                    spot = jnp.where(lane >= chunk, spot - plane_keys - tokens, spot)
                    seen = (spot >= row_low) & (spot <= position)
                    bias[...] = jnp.where(seen, 0.0, masked_low)

                here = held.at[slot, side]
                tile_q = q.at[pl.ds(turn * tile_heads, tile_heads)]

                @pl.when(at_past)
                def _():
                    behind_it = held[1, 0, 0, 0].reshape(tokens, width)
                    key_block = jnp.concatenate([here[...].reshape(chunk, width), behind_it])

                    fold(tile_q, turn, key_block)

                @pl.when(jnp.logical_not(at_past))
                def _():
                    fold(tile_q, turn, here[...].reshape(chunk, width))

    def far_run(run):
        rest, beyond = run == 2 * half + 1, run == 2 * half + 2
        back = jnp.where(rest, 0, jnp.where(beyond, half + 1, (run + 1) // 2))
        side = jnp.where(run == 0, 0, jnp.where(rest | beyond, 1, (run + 1) % 2))
        slot = run % 2
        middle = plane_blocks // 2
        wanted = z >= back
        wanted = wanted & jnp.logical_not(rest & (at_block < middle))
        wanted = wanted & jnp.logical_not((run == 2 * half - 1) & (at_block > middle))
        wanted = wanted & jnp.logical_not(beyond & (at_block > 0))
        plane = lax.rem(z - back + z_count, z_count)
        load = pltpu.make_async_copy(
            keys.at[plane, pl.ds(side * (y_count // 2), y_count // 2)],
            held.at[slot, 0],
            held_sems.at[slot, 0],
        )
        return wanted, load, (z - back) * plane_keys + side * chunk, slot

    def start_far(run):
        wanted, load, _, _ = far_run(run)

        @pl.when(wanted)
        def _():
            load.start()

    def far_runs(begin, end):
        start_far(jnp.int32(begin))

        @pl.loop(begin, end)
        def _(run):
            @pl.when(run + 1 < end)
            def _():
                start_far(run + 1)

            wanted, load, first_spot, slot = far_run(run)

            @pl.when(wanted)
            def _():
                load.wait()
                spot = first_spot + lax.broadcasted_iota(jnp.int32, (1, chunk), 1)
                seen = (spot >= row_low) & (spot <= position)
                bias[:, :chunk] = jnp.where(seen, 0.0, masked_low)
                fold(far_q, 0, held[slot, 0].reshape(chunk, width))

    def project(head, part):
        norm = 1.0 / jnp.sum(total[part, :], axis=1, keepdims=True)
        mixed = (acc[part, :] * norm).astype(jnp.bfloat16)
        ready[head] = jnp.dot(mixed, up[head], preferred_element_type=jnp.float32).astype(
            jnp.bfloat16
        )

    @pl.when(section == 1)
    def _():
        for stage in range(half + 1):
            on(core == 0, functools.partial(decode_a, stage))
            on(core == 1, functools.partial(decode_b, stage))
            if stage == 1:
                arrive(far_nope, far_recv.at[0])
                arrive(far_rope, far_recv.at[1])
                absorb(far_nope, far_rope, far_q, near, FAR_HEADS)
                load_value_up().start()
            if 0 < stage < half:
                for n in steps[stage - 1]:
                    from_sibling(n)
                far_runs(max(2 * stage - 3, 0), 2 * stage - 1)
        for n in steps[half - 1] + steps[half]:
            from_sibling(n)
        far_runs(2 * half - 3, 2 * half + 3)
        load_value_up().wait()

        for head in range(FAR_HEADS):
            project(near + head, pl.ds(head * tokens, tokens))

        far_result().start()

    @pl.when(section == 0)
    def _():
        load_value_up().wait()

        @pl.loop(0, 2)
        def _(part):
            for place in range(near // 2):
                head = part * (near // 2) + place
                project(head, pl.ds(pl.multiple_of(head * tokens, tokens), tokens))

        arrive(ready.at[pl.ds(near, FAR_HEADS)], far_recv.at[2])
        raw[...] = jnp.swapaxes(ready[...], 0, 1)
        done = pltpu.make_async_copy(raw, out, out_sems.at[1])
        done.start()
        done.wait()
        for copy in x_copies() + far_copies():
            copy.wait_send()

    @pl.when(section == 1)
    def _():
        pltpu.make_async_copy(q, q_out, out_sems.at[0]).wait()
        far_result().wait_send()

    groups = [section == 0, (section == 1) & (core == 0), (section == 1) & (core == 1)]
    for group, copies in zip(groups, went):

        @pl.when(group)
        def _():
            for copy in copies:
                copy().wait_send()

    arrive(own_out.at[1 - core], own_sems.at[2])
    own_away().wait_send()
    own_local().wait()


def prefill_part(own, q_nope, q_rope, up_key, value_up, lengths, seq_count, exponent_scale):
    rows, width = own.shape
    tokens, heads, nope_dim = q_nope.shape
    kv_rank = up_key.shape[1]
    y_count = 4
    z_count = seq_count // (2 * y_count)
    dma = pltpu.SemaphoreType.DMA
    bf16 = own.dtype
    chunk = y_count * tokens
    vmem = pl.BlockSpec(memory_space=pltpu.VMEM)
    hbm = pl.BlockSpec(memory_space=pl.ANY)
    return pl.pallas_call(
        functools.partial(prefill_kernel, z_count, y_count, kv_rank, exponent_scale),
        out_shape=[
            jax.ShapeDtypeStruct((z_count, y_count, 2, 2, rows, width), bf16),
            jax.ShapeDtypeStruct((2, rows, width), bf16),
            jax.ShapeDtypeStruct((heads, tokens, width), bf16),
            jax.ShapeDtypeStruct((tokens, heads, value_up.shape[2]), bf16),
        ],
        in_specs=[vmem, hbm, vmem, hbm, hbm, vmem],
        out_specs=[hbm] * 4,
        scratch_shapes=[
            pltpu.VMEM((rows, width), bf16),
            pltpu.VMEM(q_nope.shape, bf16),
            pltpu.VMEM((heads, tokens, nope_dim), bf16),
            pltpu.VMEM(up_key.shape, bf16),
            pltpu.VMEM((heads, tokens, width), bf16),
            pltpu.VMEM((FAR_HEADS, tokens, nope_dim), bf16),
            pltpu.VMEM((tokens, FAR_HEADS * (width - kv_rank)), bf16),
            pltpu.VMEM((FAR_HEADS, tokens, width), bf16),
            pltpu.VMEM(((heads - FAR_HEADS) * tokens, kv_rank), jnp.float32),
            pltpu.VMEM(((heads - FAR_HEADS) * tokens, LANES), jnp.float32),
            pltpu.VMEM(((heads - FAR_HEADS) * tokens, LANES), jnp.float32),
            pltpu.VMEM((2, 2, y_count // 2, 2, 2, rows, width), bf16),
            pltpu.VMEM((tokens, chunk + tokens), jnp.float32),
            pltpu.VMEM((heads, tokens, value_up.shape[2]), bf16),
            dma((3,)),
            dma((3,)),
            dma((2,)),
            dma((2,)),
            dma((2, 2)),
            dma((4,)),
            dma((2,)),
            dma((3,)),
            dma((2, z_count // 2, y_count)),
            dma((2, z_count // 2, y_count)),
            dma((z_count, 4)),
            dma((z_count, 4)),
            dma((z_count,)),
            dma((z_count,)),
        ],
        compiler_params=pltpu.CompilerParams(
            collective_id=0, has_side_effects=True, vmem_limit_bytes=56 << 20
        ),
    )(own, q_nope, q_rope, up_key, value_up, lengths)


def over_lanes(value, width):
    return jnp.concatenate([value] * (width // LANES), axis=1)


def decode_kernel(
    kv_rank,
    groups,
    exponent_scale,
    lengths,
    table,
    q_ref,
    keys,
    own_keys,
    value_up,
    prefill_out,
    out_ref,
    acc,
    top,
    total,
    held,
    lat,
    up,
    ready,
    turned,
    q_held,
    sems,
    q_sems,
    up_sems,
):
    band = pl.program_id(0)
    bands = pl.num_programs(0)
    _, heads, tokens, width = q_held.shape
    rows = heads * tokens
    all_keys = keys.shape[0]
    nt = (((1,), (1,)), ((), ()))

    @pl.when(lax.axis_index("section") == 0)
    def _():
        taken = pltpu.make_async_copy(prefill_out, turned, up_sems.at[0])
        handed = pltpu.make_async_copy(turned, out_ref, up_sems.at[1])

        @pl.when(band == 0)
        def _():
            taken.start()
            taken.wait()
            handed.start()

        @pl.when(band == bands - 1)
        def _():
            handed.wait()

    @pl.when(lax.axis_index("section") == 1)
    def _():
        def prompt_range(which):
            prompt = table[lax.axis_index("seq") * bands + which] // groups
            low = lax.fori_loop(0, prompt, lambda k, at: at + lengths[k], jnp.int32(0))
            return low, low + lengths[prompt]

        def chunk_at(start, i):
            return pl.multiple_of(jnp.minimum(start + i * KEY_BLOCK, all_keys - KEY_BLOCK), 16)

        def fetch_from(start, i, slot):
            return pltpu.make_async_copy(
                keys.at[pl.ds(chunk_at(start, i), KEY_BLOCK), :], held.at[slot], sems.at[slot]
            )

        def band_rows(which):
            return pl.ds(pl.multiple_of(which * tokens, tokens), tokens)

        def fetch_q(which):
            slot = lax.rem(which, 2)
            return pltpu.make_async_copy(
                q_ref.at[:, band_rows(which), :], q_held.at[slot], q_sems.at[slot]
            )

        def load_up():
            return pltpu.make_async_copy(value_up, up, up_sems.at[0])

        low, last = prompt_range(band)
        first = low // 16 * 16
        chunks = (last - first + KEY_BLOCK - 1) // KEY_BLOCK

        def fetch(i):
            slot = jnp.where(i == 0, lax.rem(band, 2), 2 + lax.rem(i, 2))
            return fetch_from(first, i, slot)

        @pl.when(band == 0)
        def _():
            fetch_q(0).start()
            fetch(0).start()
            load_up().start()

        @pl.when(band + 1 < bands)
        def _():
            fetch_q(band + 1).start()
            next_low, _ = prompt_range(band + 1)
            fetch_from(next_low // 16 * 16, 0, lax.rem(band + 1, 2)).start()

        fetch_q(band).wait()
        q = q_held[lax.rem(band, 2)].reshape(rows, width)
        def score(key_block):
            return lax.dot_general(q, key_block, nt, preferred_element_type=jnp.float32)

        def in_range(at, count, low_spot):
            spot = at + lax.broadcasted_iota(jnp.int32, (1, count), 1)
            return jnp.where((spot >= jnp.maximum(low, low_spot)) & (spot < last), 0.0, masked_low)

        def weigh(scores, now):
            return jnp.exp2((scores - now) * exponent_scale)

        def mix(weights, key_block):
            return jnp.dot(
                weights.astype(jnp.bfloat16),
                key_block[:, :kv_rank],
                preferred_element_type=jnp.float32,
            )

        def begin(key_block, at):
            own = own_keys[...]
            asked = lax.broadcasted_iota(jnp.int32, (tokens, tokens), 0)
            key = lax.broadcasted_iota(jnp.int32, (tokens, tokens), 1)
            seen = (asked % SAMPLES == key % SAMPLES) & (key // SAMPLES <= asked // SAMPLES)
            bias = jnp.where(seen, 0.0, masked_low)
            bias = jnp.broadcast_to(bias[None], (heads, tokens, tokens)).reshape(rows, tokens)
            new = score(own) + bias
            count = key_block.shape[0]
            old = score(key_block) + in_range(at, count, low)
            now = jnp.maximum(
                jnp.max(new, axis=1, keepdims=True), jnp.max(old, axis=1, keepdims=True)
            )
            new = weigh(new, now)
            old = weigh(old, now)
            top[...] = jnp.broadcast_to(now, (rows, LANES))
            lane = lax.broadcasted_iota(jnp.int32, (rows, LANES), 1)
            summed = jnp.where(lane == 0, jnp.sum(new, axis=1, keepdims=True), 0.0)
            for c in range(0, count, LANES):
                summed = summed + old[:, c : c + LANES]
            total[...] = summed
            acc[...] = mix(new, own) + mix(old, key_block)

        def fold(key_block, low_spot, at):
            count = key_block.shape[0]
            s = score(key_block)
            if low_spot is not None:
                s = s + in_range(at, count, low_spot)
            before = top[...]
            now = jnp.maximum(before, jnp.max(s, axis=1, keepdims=True))
            shrink = jnp.exp2((before - now) * exponent_scale)
            expo = weigh(s, over_lanes(now, count))
            top[...] = now
            summed = total[...] * shrink
            for c in range(0, count, LANES):
                summed = summed + expo[:, c : c + LANES]
            total[...] = summed
            acc[...] = acc[...] * over_lanes(shrink, kv_rank) + mix(expo, key_block)

        @pl.loop(0, chunks)
        def _(i):
            slot = jnp.where(i == 0, lax.rem(band, 2), 2 + lax.rem(i, 2))
            fetch(i).wait()

            @pl.when(i + 1 < chunks)
            def _():
                fetch(i + 1).start()

            nominal = first + i * KEY_BLOCK
            at = chunk_at(first, i)
            whole = (i > 0) & (nominal + KEY_BLOCK <= last)
            skip = (nominal - at) // EDGE_BLOCK

            @pl.when(i == 0)
            def _():
                here = pl.multiple_of(skip * EDGE_BLOCK, EDGE_BLOCK)
                begin(held[slot, pl.ds(here, EDGE_BLOCK), :], at + here)

            @pl.when(whole)
            def _():
                fold(held[slot], None, None)

            @pl.when(jnp.logical_not(whole))
            def _():
                begun = skip + jnp.where(i == 0, 1, 0)

                @pl.loop(begun, (jnp.minimum(last - at, KEY_BLOCK) + EDGE_BLOCK - 1) // EDGE_BLOCK)
                def _(j):
                    here = pl.multiple_of(j * EDGE_BLOCK, EDGE_BLOCK)
                    fold(held[slot, pl.ds(here, EDGE_BLOCK), :], nominal, at + here)

        norm = 1.0 / jnp.sum(total[...], axis=1, keepdims=True)
        lat[:, band_rows(band), :] = (
            (acc[...] * norm).astype(jnp.bfloat16).reshape(heads, tokens, kv_rank)
        )

        @pl.when(band == bands - 1)
        def _():
            load_up().wait()

            @pl.loop(0, heads // 8)
            def _(eight):
                picked = [eight * 8 + k for k in range(8)]
                products = [
                    jnp.dot(lat[head], up[head], preferred_element_type=jnp.float32)
                    for head in picked
                ]
                for head, product in zip(picked, products):
                    ready[head] = product.astype(jnp.bfloat16)

            turned[...] = jnp.swapaxes(ready[...], 0, 1)
            done = pltpu.make_async_copy(turned, out_ref, up_sems.at[1])
            done.start()
            done.wait()


def shards(query_nope, query_rope, latent, up_key, value_up_weight, lengths, owner_request_table):
    seq_count = lax.axis_size("seq")
    tok_dev, head_dev, nope_dim = query_nope.shape[1:]
    rope_dim = query_rope.shape[2] // head_dev
    kv_rank = up_key.shape[1]
    width = kv_rank + rope_dim
    v_dim = value_up_weight.shape[2]
    req_dev = owner_request_table.shape[0] // seq_count
    groups = owner_request_table.shape[0] // lengths.shape[0]
    band_tokens = tok_dev // req_dev
    exponent_scale = math.log2(math.e) / math.sqrt(nope_dim + rope_dim)

    keys, pair, queries, prefill_out = prefill_part(
        latent[0],
        query_nope[0],
        query_rope[0],
        up_key,
        value_up_weight,
        lengths[None, :],
        seq_count,
        exponent_scale,
    )
    rows = head_dev * band_tokens
    attended = pl.pallas_call(
        functools.partial(decode_kernel, kv_rank, groups, exponent_scale),
        out_shape=jax.ShapeDtypeStruct(prefill_out.shape, jnp.bfloat16),
        grid_spec=pltpu.PrefetchScalarGridSpec(
            num_scalar_prefetch=2,
            grid=(req_dev,),
            in_specs=[
                pl.BlockSpec(memory_space=pl.ANY),
                pl.BlockSpec(memory_space=pl.ANY),
                pl.BlockSpec((band_tokens, width), lambda i, *_: (i, 0)),
                pl.BlockSpec(memory_space=pl.ANY),
                pl.BlockSpec(memory_space=pl.ANY),
            ],
            out_specs=pl.BlockSpec(memory_space=pl.ANY),
            scratch_shapes=[
                pltpu.VMEM((rows, kv_rank), jnp.float32),
                pltpu.VMEM((rows, LANES), jnp.float32),
                pltpu.VMEM((rows, LANES), jnp.float32),
                pltpu.VMEM((4, KEY_BLOCK, width), jnp.bfloat16),
                pltpu.VMEM((head_dev, tok_dev, kv_rank), jnp.bfloat16),
                pltpu.VMEM(value_up_weight.shape, jnp.bfloat16),
                pltpu.VMEM((head_dev, tok_dev, v_dim), jnp.bfloat16),
                pltpu.VMEM(prefill_out.shape, jnp.bfloat16),
                pltpu.VMEM((2, head_dev, band_tokens, width), jnp.bfloat16),
                pltpu.SemaphoreType.DMA((4,)),
                pltpu.SemaphoreType.DMA((2,)),
                pltpu.SemaphoreType.DMA((2,)),
            ],
        ),
        compiler_params=pltpu.CompilerParams(vmem_limit_bytes=58 << 20),
    )(
        lengths,
        owner_request_table,
        queries,
        keys.reshape(-1, width),
        pair.reshape(-1, width),
        value_up_weight,
        prefill_out,
    )

    return attended[None]


def solution(mesh):
    in_specs = (
        P("section", "seq", "head", None),
        P("section", "seq", "head"),
        P("section", ("seq", "head"), None),
        P("head", None, None),
        P("head", None, None),
        P(),
        P(),
    )
    out_specs = P("section", "seq", "head", None)
    return jax.shard_map(shards, mesh=mesh, in_specs=in_specs, out_specs=out_specs, check_vma=False)
```

```python
import functools
import math

import jax
import jax.numpy as jnp
from jax import lax
from jax.experimental import pallas as pl
from jax.experimental.pallas import tpu as pltpu
from jax.sharding import PartitionSpec as P

SAMPLES = 8
STEPS = 4
BLOCK = 64

scale_top = 448.0
tiny_eps = 1e-06
masked_low = -1e30

KEY_BLOCK = 1024
EDGE_BLOCK = 512
FAR_HEADS = 6

CHAIN_STEPS = (0, 1, 3, 5)
ON_STEPS = (0, 2, 5, 8)
END_STEPS = (1, 3, 7, 10)
SIBLING_STEPS = (2, 5, 9, 13)
PAST_STEPS = (8, 10, 15)
LANES = 128


def prefill_kernel(
    z_count, y_count, kv_rank, exponent_scale, own_in, q_nope, q_rope, up_key, value_up, lengths,
    keys, own_out, q_out, out, block, raw, nope, up, q, far_nope, far_rope, far_q, acc, top, total,
    held, bias, ready, far_send, far_recv,
    in_sems, out_sems, held_sems, x_send, x_recv, own_sems,
    z_send, z_recv, y_send, y_recv, sib_send, sib_recv,
):
    section = lax.axis_index("section")
    seq = lax.axis_index("seq")
    core = lax.axis_index("head")
    z = seq // (2 * y_count)
    y = seq // 2 % y_count
    hi = seq % 2
    half = z_count // 2
    heads, tokens, width = q.shape
    plane_blocks = 2 * y_count
    at_block = seq % plane_blocks
    plane_keys = plane_blocks * tokens
    nt = (((1,), (1,)), ((), ()))

    def plane_at(dz):
        return lax.rem(z + dz + z_count, z_count)

    def row_at(dy):
        return lax.rem(y + dy + y_count, y_count)

    def device(dz=0, dy=0, to_hi=None, to_section=None, to_core=None):
        th = hi if to_hi is None else to_hi
        return (
            section if to_section is None else to_section,
            (plane_at(dz) * y_count + row_at(dy)) * 2 + th,
            core if to_core is None else to_core,
        )

    loads = [
        pltpu.make_async_copy(q_nope, raw, in_sems.at[0]),
        pltpu.make_async_copy(up_key, up, in_sems.at[1]),
    ]
    for load in loads:
        load.start()

    barrier = pltpu.get_barrier_semaphore()
    peers = [
        device(to_core=1 - core),
        device(to_section=1 - section),
        device(to_hi=1 - hi),
        device(to_section=1 - section, to_hi=1 - hi),
        device(dz=1),
        device(dz=-1),
        device(dy=1),
        device(dy=-1),
    ]
    for peer in peers:
        pl.semaphore_signal(barrier, inc=1, device_id=peer, device_id_type=pl.DeviceIdType.MESH)

    @pl.when(section == 0)
    def _():
        rows = own_in[...].astype(jnp.float32)
        largest = jnp.max(jnp.abs(rows))
        spread = jnp.full((8, LANES), largest, jnp.float32)
        scale = ((spread + tiny_eps) / scale_top).astype(jnp.bfloat16).astype(jnp.float32)
        factor = scale[:1, :1]
        stored = (rows / factor).astype(jnp.bfloat16)
        block[...] = (stored.astype(jnp.float32) * factor).astype(jnp.bfloat16)

    @pl.when(section == 1)
    def _():
        block[...] = own_in[...]

    pl.semaphore_wait(barrier, len(peers))

    def remote(src, dst, to, send_sem, recv_sem):
        return pltpu.make_async_remote_copy(
            src_ref=src,
            dst_ref=dst,
            send_sem=send_sem,
            recv_sem=recv_sem,
            device_id=to,
            device_id_type=pl.DeviceIdType.MESH,
        )

    def arrive(dst, recv_sem):
        remote(dst, dst, device(to_core=1 - core), recv_sem, recv_sem).wait_recv()

    def own_local():
        return pltpu.make_async_copy(block, own_out.at[core], own_sems.at[0])

    def own_away():
        to = device(to_core=1 - core)
        return remote(block, own_out.at[core], to, own_sems.at[1], own_sems.at[2])

    def x_copies():
        spot = keys.at[z, y, hi, core]
        return [
            remote(block, spot, device(to_hi=1 - hi), x_send.at[2], x_recv.at[1]),
            remote(block, spot, device(to_section=1), x_send.at[0], x_recv.at[0]),
            remote(block, spot, device(to_section=1, to_hi=1 - hi), x_send.at[1], x_recv.at[1]),
        ]

    def x_local():
        return pltpu.make_async_copy(block, keys.at[z, y, hi, core], x_send.at[3])

    @pl.when(section == 0)
    def _():
        x_local().start()
        for copy in x_copies():
            copy.start()

    own_local().start()
    own_away().start()

    for load in loads:
        load.wait()
    nope[...] = jnp.swapaxes(raw[...], 0, 1)

    near = heads - FAR_HEADS
    half_lanes = LANES // 2

    def far_copies():
        to = device(to_section=1 - section)
        rope_part = q_rope.at[:, pl.ds(near * half_lanes, FAR_HEADS * half_lanes)]
        return [
            remote(nope.at[pl.ds(near, FAR_HEADS)], far_nope, to, far_send.at[0], far_recv.at[0]),
            remote(rope_part, far_rope, to, far_send.at[1], far_recv.at[1]),
        ]

    def far_result():
        part = ready.at[pl.ds(near, FAR_HEADS)]
        return remote(part, part, device(to_section=1 - section), far_send.at[2], far_recv.at[2])

    @pl.when(section == 0)
    def _():
        for copy in far_copies():
            copy.start()

    def absorb(from_nope, from_rope, into, first, count):
        @pl.loop(0, count // 2)
        def _(pair):
            rope = from_rope[:, pl.ds(pl.multiple_of(pair * LANES, LANES), LANES)]
            for side in range(2):
                head = pair * 2 + side
                lifted = lax.dot_general(
                    from_nope[head], up[first + head], nt, preferred_element_type=jnp.float32
                )
                into[head, :, :kv_rank] = lifted.astype(jnp.bfloat16)
                into[head, :, kv_rank:] = rope[:, side * half_lanes : (side + 1) * half_lanes]

    @pl.when(section == 0)
    def _():
        absorb(nope, q_rope, q, 0, near)

    @pl.when(section == 1)
    def _():
        absorb(nope, q_rope, q, 0, heads)

    def load_value_up():
        return pltpu.make_async_copy(value_up, up, in_sems.at[1])

    @pl.when(section == 0)
    def _():
        load_value_up().start()

    @pl.when(section == 1)
    def _():
        pltpu.make_async_copy(q, q_out, out_sems.at[0]).start()

    @pl.when(section == 0)
    def _():
        x_local().wait()
        arrive(keys.at[z, y, 1 - hi, core], x_recv.at[1])

    @pl.when(section == 1)
    def _():
        arrive(keys.at[z, y, hi, core], x_recv.at[0])
        arrive(keys.at[z, y, 1 - hi, core], x_recv.at[1])

    low, high, far = row_at(-1), row_at(1), row_at(2)
    columns = [y, low, high, far]
    planes = [z]
    for s in range(1, half):
        planes += [plane_at(-s), plane_at(s)]
    planes.append(plane_at(half))
    steps = [[0]] + [[2 * s - 1, 2 * s] for s in range(1, half)] + [[z_count - 1]]

    def sender(went):
        def send(src, to, send_sem, recv_sem):
            copy = lambda: remote(src(), src(), to(), send_sem(), recv_sem())
            went.append(copy)
            copy().start()

        return send

    went = [[], [], []]

    def along_y(send, n, c, src, d, k):
        send(src, lambda: device(dy=d), lambda: y_send.at[n, k], lambda: y_recv.at[n, k])

    def spread(send, n, c):
        mine = lambda: keys.at[planes[n], y, :, c]
        along_y(send, n, c, mine, 1, 0)
        along_y(send, n, c, mine, -1, 1)

    def spread_on(send, n, c):
        arrive(keys.at[planes[n], low, :, c], y_recv.at[n, 0])
        along_y(send, n, c, lambda: keys.at[planes[n], low, 0, c], 1, 2)
        arrive(keys.at[planes[n], high, :, c], y_recv.at[n, 1])
        along_y(send, n, c, lambda: keys.at[planes[n], high, 1, c], -1, 3)

    def spread_end(n, c):
        arrive(keys.at[planes[n], far, 0, c], y_recv.at[n, 2])
        arrive(keys.at[planes[n], far, 1, c], y_recv.at[n, 3])

    def to_sibling(send, n, c):
        send(
            lambda: keys.at[planes[n], :, :, c],
            lambda: device(to_core=1 - c),
            lambda: sib_send.at[n],
            lambda: sib_recv.at[n],
        )

    def along_z(send, src, up_way, step, k):
        d, j = (1, 0) if up_way else (-1, 1)
        send(
            src,
            lambda: device(dz=d),
            lambda: z_send.at[j, step, k],
            lambda: z_recv.at[j, step, k],
        )

    ways = ((0, True), (1, False))

    def decode_a(stage):
        send = sender(went[1])

        def cell(n, k):
            return lambda: keys.at[planes[n], columns[k], :, 0]

        def column(k):
            for _, up_way in ways:
                along_z(send, cell(0, k), up_way, 0, k)

        if stage == 0:
            spread(send, 0, 0)
            column(0)
            arrive(keys.at[z, low, :, 0], y_recv.at[0, 0])
            along_y(send, 0, 0, lambda: keys.at[z, low, 0, 0], 1, 2)
            column(1)
            arrive(keys.at[z, high, :, 0], y_recv.at[0, 1])
            along_y(send, 0, 0, lambda: keys.at[z, high, 1, 0], -1, 3)
            column(2)
            spread_end(0, 0)
            column(3)
            to_sibling(send, 0, 0)
        elif stage < half:
            for k in range(y_count):
                for n, (j, up_way) in zip(steps[stage], ways):
                    arrive(cell(n, k)(), z_recv.at[j, stage - 1, k])
                    if stage < half - 1 or k // 2 == j:
                        along_z(send, cell(n, k), up_way, stage, k)
            for n in steps[stage]:
                to_sibling(send, n, 0)
        else:
            for k in range(y_count):
                arrive(cell(z_count - 1, k)(), z_recv.at[k // 2, half - 1, k])
            to_sibling(send, z_count - 1, 0)

    def decode_b(stage):
        send = sender(went[2])

        def ahead(n, s, j, up_way):
            if s < half - 1:
                part = lambda: keys.at[planes[n], y, :, 1]
            else:
                part = lambda: keys.at[planes[n], y, j, 1]
            along_z(send, part, up_way, s, 0)

        def chain(s):
            for n, (j, up_way) in zip(steps[s], ways):
                arrive(keys.at[planes[n], y, :, 1], z_recv.at[j, s - 1, 0])
                ahead(n, s, j, up_way)
                spread(send, n, 1)

        def finish(s):
            for n in steps[s]:
                spread_end(n, 1)
                to_sibling(send, n, 1)

        if stage == 0:
            for j, up_way in ways:
                ahead(0, 0, j, up_way)
            spread(send, 0, 1)
            chain(1)
            spread_on(send, 0, 1)
            return
        if stage + 1 < half:
            chain(stage + 1)
        elif stage + 1 == half:
            for j in range(2):
                arrive(keys.at[planes[-1], y, j, 1], z_recv.at[j, half - 1, 0])
            spread(send, z_count - 1, 1)
        for n in steps[stage]:
            spread_on(send, n, 1)
        finish(stage - 1)
        if stage == half:
            finish(stage)

    behind = [0] + [2 * s - 1 for s in range(1, half)] + [z_count - 1]
    past = planes[2 * (half - 1)]
    forward = sender(went[0])

    def ahead(n, s):
        along_z(forward, lambda: keys.at[planes[n], y, :, core], True, s, 0)

    def prefill_start():
        ahead(0, 0)
        spread(forward, 0, core)
        prefill_chain(1)
        spread_on(forward, 0, core)
        spread_end(0, core)
        to_sibling(forward, 0, core)
        prefill_on(1)
        from_sibling(0)

    def prefill_chain(s):
        n = behind[s]
        arrive(keys.at[planes[n], y, :, core], z_recv.at[0, s - 1, 0])
        if s < half:
            ahead(n, s)
        else:
            along_z(forward, lambda: keys.at[planes[n], y, 1, core], True, 0, 1)
        spread(forward, n, core)

    def prefill_on(s):
        spread_on(forward, behind[s], core)

    def prefill_end(s):
        spread_end(behind[s], core)
        to_sibling(forward, behind[s], core)

    def prefill_past():
        arrive(keys.at[past, y, 1, core], z_recv.at[0, 0, 1])
        n = 2 * (half - 1)
        along_y(forward, n, core, lambda: keys.at[past, y, 1, core], 1, 0)

    def prefill_past_end():
        n = 2 * (half - 1)
        spot = lambda: keys.at[past, low, 1, core]
        arrive(spot(), y_recv.at[n, 0])
        forward(
            spot,
            lambda: device(to_core=1 - core),
            lambda: sib_send.at[n],
            lambda: sib_recv.at[n],
        )

    def from_sibling(n):
        arrive(keys.at[planes[n], :, :, 1 - core], sib_recv.at[n])

    def on(at, event):
        @pl.when(at)
        def _():
            event()

    top[...] = jnp.full(top.shape, masked_low, jnp.float32)
    total[...] = jnp.zeros(total.shape, jnp.float32)
    acc[...] = jnp.zeros(acc.shape, jnp.float32)

    token = lax.broadcasted_iota(jnp.int32, (tokens, 1), 0)
    position = seq * tokens + token
    count = lengths.shape[1]
    before_it = lax.broadcasted_iota(jnp.int32, (count, count), 0) < lax.broadcasted_iota(
        jnp.int32, (count, count), 1
    )
    earlier = jnp.where(before_it, 1.0, 0.0).astype(jnp.bfloat16)
    wide = jnp.broadcast_to(lengths[...], (8, count))
    digits = [(wide // 64).astype(jnp.bfloat16), (wide % 64).astype(jnp.bfloat16)]
    upper, lower = [jnp.dot(d, earlier, preferred_element_type=jnp.float32) for d in digits]
    starts = (upper * 64.0 + lower)[:1]
    row_low = jnp.max(
        jnp.where(starts <= position.astype(jnp.float32), starts, 0.0), axis=1, keepdims=True
    ).astype(jnp.int32)

    chunk = plane_keys // 2
    tile_heads = near // 2

    def fold(asked_heads, tile, key_block):
        count = key_block.shape[0]
        tile_heads = asked_heads.shape[0]
        rows = tile_heads * tokens
        part = pl.ds(pl.multiple_of(tile * rows, rows), rows)
        asked = asked_heads[...].reshape(rows, width)
        s = lax.dot_general(asked, key_block, nt, preferred_element_type=jnp.float32)
        s = (s.reshape(tile_heads, tokens, count) + bias[:, :count][None]).reshape(rows, count)
        before = top[part, :]
        now = jnp.maximum(before, jnp.max(s, axis=1, keepdims=True))
        shrink = jnp.exp2((before - now) * exponent_scale)
        expo = jnp.exp2((s - over_lanes(now, count)) * exponent_scale)
        top[part, :] = now
        summed = total[part, :] * shrink
        for c in range(0, count, LANES):
            summed = summed + expo[:, c : c + LANES]
        total[part, :] = summed
        acc[part, :] = acc[part, :] * over_lanes(shrink, kv_rank) + jnp.dot(
            expo.astype(jnp.bfloat16),
            key_block[:, :kv_rank],
            preferred_element_type=jnp.float32,
        )

    def past_from_sibling():
        arrive(keys.at[past, low, 1, 1 - core], sib_recv.at[2 * (half - 1)])

    last_step = 4 * (half + 1)
    timetable = [
        (prefill_chain, CHAIN_STEPS),
        (prefill_on, ON_STEPS),
        (prefill_end, END_STEPS),
        (lambda s: from_sibling(behind[s]), SIBLING_STEPS),
    ]
    events = {0: [prefill_start]}
    for s in range(1, half + 1):
        for event, at_steps in timetable:
            if at_steps[s - 1] > 0:
                spot = events.setdefault(at_steps[s - 1], [])
                spot.append(functools.partial(event, s))
    for event, at_step in zip((prefill_past, prefill_past_end, past_from_sibling), PAST_STEPS):
        events.setdefault(at_step, []).append(event)

    @pl.when(section == 0)
    def _():
        mid = plane_blocks // 2
        at_first, at_mid = at_block == 0, at_block == mid
        reaches_past = at_first & (z > half)

        @pl.loop(0, last_step)
        def _(step):
            for at_step in sorted(events):
                for event in events[at_step]:
                    on(step == at_step, event)

            run = step // 2
            turn = step % 2
            rest = run == 2 * half + 1
            back = jnp.where(rest, 0, (run + 1) // 2)
            side = jnp.where(run == 0, 0, (run + 1) % 2)
            side = jnp.where(rest, 1, side)
            slot = jnp.where(rest, 1, back % 2)
            reached = z >= back

            def load(back, part, slot, into):
                plane = lax.rem(z - back + z_count, z_count)
                here = keys.at[plane, pl.ds(part * (y_count // 2), y_count // 2)]
                return pltpu.make_async_copy(here, held.at[slot, into], held_sems.at[slot, into])

            def load_first():
                return pltpu.make_async_copy(
                    keys.at[past, y_count - 1, 1], held.at[1, 0, 0, 0], held_sems.at[1, 0]
                )

            def load_mid():
                return pltpu.make_async_copy(
                    keys.at[planes[-1], y_count // 2 - 1, 1],
                    held.at[1, 1, y_count // 2 - 1, 1],
                    held_sems.at[1, 0],
                )

            @pl.when(step == 0)
            def _():
                load(0, 0, 0, 0).start()

            for s in range(1, half + 1):

                @pl.when((step == SIBLING_STEPS[s - 1]) & (z >= s))
                def _():
                    load(s, 0, s % 2, 0).start()
                    load(s, 1, s % 2, 1).start()

            @pl.when(step == last_step - 5)
            def _():
                @pl.when(reaches_past)
                def _():
                    load_first().start()

                @pl.when(at_block >= mid)
                def _():
                    rest_load = load(0, 1, 1, 1)
                    rest_load.start()
                    rest_load.wait()

                @pl.when(at_mid)
                def _():
                    load_mid().start()

            @pl.when(reached & (turn == 0) & jnp.logical_not(rest))
            def _():
                load(back, side, slot, side).wait()

            at_past = reaches_past & (run == 2 * half)

            @pl.when(at_past & (turn == 0))
            def _():
                load_first().wait()

            @pl.when((turn == 0) & rest & at_mid)
            def _():
                load_mid().wait()

            none = (rest & (at_block < mid)) | ((run == 2 * half - 1) & (at_block >= mid))
            first_spot = (z - back) * plane_keys + side * chunk

            @pl.when(reached & jnp.logical_not(none))
            def _():
                @pl.when(turn == 0)
                def _():
                    lane = lax.broadcasted_iota(jnp.int32, (1, chunk + tokens), 1)
                    spot = first_spot + lane
                    shift = (half * plane_keys) + chunk
                    spot = jnp.where(
                        rest & at_mid & (lane >= chunk - tokens), spot - shift, spot
                    )
                    spot = jnp.where(lane >= chunk, spot - plane_keys - tokens, spot)
                    seen = (spot >= row_low) & (spot <= position)
                    bias[...] = jnp.where(seen, 0.0, masked_low)

                here = held.at[slot, side]
                tile_q = q.at[pl.ds(turn * tile_heads, tile_heads)]

                @pl.when(at_past)
                def _():
                    behind_it = held[1, 0, 0, 0].reshape(tokens, width)
                    key_block = jnp.concatenate([here[...].reshape(chunk, width), behind_it])

                    fold(tile_q, turn, key_block)

                @pl.when(jnp.logical_not(at_past))
                def _():
                    fold(tile_q, turn, here[...].reshape(chunk, width))

    def far_run(run):
        rest, beyond = run == 2 * half + 1, run == 2 * half + 2
        back = jnp.where(rest, 0, jnp.where(beyond, half + 1, (run + 1) // 2))
        side = jnp.where(run == 0, 0, jnp.where(rest | beyond, 1, (run + 1) % 2))
        slot = run % 2
        middle = plane_blocks // 2
        wanted = z >= back
        wanted = wanted & jnp.logical_not(rest & (at_block < middle))
        wanted = wanted & jnp.logical_not((run == 2 * half - 1) & (at_block > middle))
        wanted = wanted & jnp.logical_not(beyond & (at_block > 0))
        plane = lax.rem(z - back + z_count, z_count)
        load = pltpu.make_async_copy(
            keys.at[plane, pl.ds(side * (y_count // 2), y_count // 2)],
            held.at[slot, 0],
            held_sems.at[slot, 0],
        )
        return wanted, load, (z - back) * plane_keys + side * chunk, slot

    def start_far(run):
        wanted, load, _, _ = far_run(run)

        @pl.when(wanted)
        def _():
            load.start()

    def far_runs(begin, end):
        start_far(jnp.int32(begin))

        @pl.loop(begin, end)
        def _(run):
            @pl.when(run + 1 < end)
            def _():
                start_far(run + 1)

            wanted, load, first_spot, slot = far_run(run)

            @pl.when(wanted)
            def _():
                load.wait()
                spot = first_spot + lax.broadcasted_iota(jnp.int32, (1, chunk), 1)
                seen = (spot >= row_low) & (spot <= position)
                bias[:, :chunk] = jnp.where(seen, 0.0, masked_low)
                fold(far_q, 0, held[slot, 0].reshape(chunk, width))

    def project(head, part):
        norm = 1.0 / jnp.sum(total[part, :], axis=1, keepdims=True)
        mixed = (acc[part, :] * norm).astype(jnp.bfloat16)
        ready[head] = jnp.dot(mixed, up[head], preferred_element_type=jnp.float32).astype(
            jnp.bfloat16
        )

    @pl.when(section == 1)
    def _():
        for stage in range(half + 1):
            on(core == 0, functools.partial(decode_a, stage))
            on(core == 1, functools.partial(decode_b, stage))
            if stage == 1:
                arrive(far_nope, far_recv.at[0])
                arrive(far_rope, far_recv.at[1])
                absorb(far_nope, far_rope, far_q, near, FAR_HEADS)
                load_value_up().start()
            if 0 < stage < half:
                for n in steps[stage - 1]:
                    from_sibling(n)
                far_runs(max(2 * stage - 3, 0), 2 * stage - 1)
        for n in steps[half - 1] + steps[half]:
            from_sibling(n)
        far_runs(2 * half - 3, 2 * half + 3)
        load_value_up().wait()

        for head in range(FAR_HEADS):
            project(near + head, pl.ds(head * tokens, tokens))

        far_result().start()

    @pl.when(section == 0)
    def _():
        load_value_up().wait()

        @pl.loop(0, 2)
        def _(part):
            for place in range(near // 2):
                head = part * (near // 2) + place
                project(head, pl.ds(pl.multiple_of(head * tokens, tokens), tokens))

        arrive(ready.at[pl.ds(near, FAR_HEADS)], far_recv.at[2])
        raw[...] = jnp.swapaxes(ready[...], 0, 1)
        done = pltpu.make_async_copy(raw, out, out_sems.at[1])
        done.start()
        done.wait()
        for copy in x_copies() + far_copies():
            copy.wait_send()

    @pl.when(section == 1)
    def _():
        pltpu.make_async_copy(q, q_out, out_sems.at[0]).wait()
        far_result().wait_send()

    groups = [section == 0, (section == 1) & (core == 0), (section == 1) & (core == 1)]
    for group, copies in zip(groups, went):

        @pl.when(group)
        def _():
            for copy in copies:
                copy().wait_send()

    arrive(own_out.at[1 - core], own_sems.at[2])
    own_away().wait_send()
    own_local().wait()


def prefill_part(own, q_nope, q_rope, up_key, value_up, lengths, seq_count, exponent_scale):
    rows, width = own.shape
    tokens, heads, nope_dim = q_nope.shape
    kv_rank = up_key.shape[1]
    y_count = 4
    z_count = seq_count // (2 * y_count)
    dma = pltpu.SemaphoreType.DMA
    bf16 = own.dtype
    chunk = y_count * tokens
    vmem = pl.BlockSpec(memory_space=pltpu.VMEM)
    hbm = pl.BlockSpec(memory_space=pl.ANY)
    return pl.pallas_call(
        functools.partial(prefill_kernel, z_count, y_count, kv_rank, exponent_scale),
        out_shape=[
            jax.ShapeDtypeStruct((z_count, y_count, 2, 2, rows, width), bf16),
            jax.ShapeDtypeStruct((2, rows, width), bf16),
            jax.ShapeDtypeStruct((heads, tokens, width), bf16),
            jax.ShapeDtypeStruct((tokens, heads, value_up.shape[2]), bf16),
        ],
        in_specs=[vmem, hbm, vmem, hbm, hbm, vmem],
        out_specs=[hbm] * 4,
        scratch_shapes=[
            pltpu.VMEM((rows, width), bf16),
            pltpu.VMEM(q_nope.shape, bf16),
            pltpu.VMEM((heads, tokens, nope_dim), bf16),
            pltpu.VMEM(up_key.shape, bf16),
            pltpu.VMEM((heads, tokens, width), bf16),
            pltpu.VMEM((FAR_HEADS, tokens, nope_dim), bf16),
            pltpu.VMEM((tokens, FAR_HEADS * (width - kv_rank)), bf16),
            pltpu.VMEM((FAR_HEADS, tokens, width), bf16),
            pltpu.VMEM(((heads - FAR_HEADS) * tokens, kv_rank), jnp.float32),
            pltpu.VMEM(((heads - FAR_HEADS) * tokens, LANES), jnp.float32),
            pltpu.VMEM(((heads - FAR_HEADS) * tokens, LANES), jnp.float32),
            pltpu.VMEM((2, 2, y_count // 2, 2, 2, rows, width), bf16),
            pltpu.VMEM((tokens, chunk + tokens), jnp.float32),
            pltpu.VMEM((heads, tokens, value_up.shape[2]), bf16),
            dma((3,)),
            dma((3,)),
            dma((2,)),
            dma((2,)),
            dma((2, 2)),
            dma((4,)),
            dma((2,)),
            dma((3,)),
            dma((2, z_count // 2, y_count)),
            dma((2, z_count // 2, y_count)),
            dma((z_count, 4)),
            dma((z_count, 4)),
            dma((z_count,)),
            dma((z_count,)),
        ],
        compiler_params=pltpu.CompilerParams(
            collective_id=0, has_side_effects=True, vmem_limit_bytes=56 << 20
        ),
    )(own, q_nope, q_rope, up_key, value_up, lengths)


def over_lanes(value, width):
    return jnp.concatenate([value] * (width // LANES), axis=1)


def decode_kernel(
    kv_rank,
    groups,
    exponent_scale,
    lengths,
    table,
    q_ref,
    keys,
    own_keys,
    value_up,
    prefill_out,
    out_ref,
    acc,
    top,
    total,
    held,
    lat,
    up,
    ready,
    turned,
    q_held,
    own_held,
    sems,
    q_sems,
    up_sems,
):
    band = pl.program_id(0)
    bands = pl.num_programs(0)
    _, heads, tokens, width = q_held.shape
    rows = heads * tokens
    all_keys = keys.shape[0]
    nt = (((1,), (1,)), ((), ()))

    @pl.when(lax.axis_index("section") == 0)
    def _():
        taken = pltpu.make_async_copy(prefill_out, turned, up_sems.at[0])
        handed = pltpu.make_async_copy(turned, out_ref, up_sems.at[1])

        @pl.when(band == 0)
        def _():
            taken.start()
            taken.wait()
            handed.start()

        @pl.when(band == bands - 1)
        def _():
            handed.wait()

    @pl.when(lax.axis_index("section") == 1)
    def _():
        def prompt_range(which):
            prompt = table[lax.axis_index("seq") * bands + which] // groups
            low = lax.fori_loop(0, prompt, lambda k, at: at + lengths[k], jnp.int32(0))
            return low, low + lengths[prompt]

        def chunk_at(start, i):
            return pl.multiple_of(jnp.minimum(start + i * KEY_BLOCK, all_keys - KEY_BLOCK), 16)

        def fetch_from(start, i, slot):
            return pltpu.make_async_copy(
                keys.at[pl.ds(chunk_at(start, i), KEY_BLOCK), :], held.at[slot], sems.at[slot]
            )

        def band_rows(which):
            return pl.ds(pl.multiple_of(which * tokens, tokens), tokens)

        def fetch_q(which):
            slot = lax.rem(which, 2)
            return pltpu.make_async_copy(
                q_ref.at[:, band_rows(which), :], q_held.at[slot], q_sems.at[slot]
            )

        def load_up():
            return pltpu.make_async_copy(value_up, up, up_sems.at[0])

        def load_own():
            return pltpu.make_async_copy(own_keys, own_held, up_sems.at[2])

        low, last = prompt_range(band)
        first = low // 16 * 16
        chunks = (last - first + KEY_BLOCK - 1) // KEY_BLOCK

        def fetch(i):
            slot = jnp.where(i == 0, lax.rem(band, 2), 2 + lax.rem(i, 2))
            return fetch_from(first, i, slot)

        @pl.when(band == 0)
        def _():
            load_own().start()
            fetch_q(0).start()
            fetch(0).start()
            load_up().start()
            load_own().wait()

        @pl.when(band + 1 < bands)
        def _():
            fetch_q(band + 1).start()
            next_low, _ = prompt_range(band + 1)
            fetch_from(next_low // 16 * 16, 0, lax.rem(band + 1, 2)).start()

        fetch_q(band).wait()
        q = q_held[lax.rem(band, 2)].reshape(rows, width)
        def score(key_block):
            return lax.dot_general(q, key_block, nt, preferred_element_type=jnp.float32)

        def in_range(at, count, low_spot):
            spot = at + lax.broadcasted_iota(jnp.int32, (1, count), 1)
            return jnp.where((spot >= jnp.maximum(low, low_spot)) & (spot < last), 0.0, masked_low)

        def weigh(scores, now):
            return jnp.exp2((scores - now) * exponent_scale)

        def mix(weights, key_block):
            return jnp.dot(
                weights.astype(jnp.bfloat16),
                key_block[:, :kv_rank],
                preferred_element_type=jnp.float32,
            )

        def begin(key_block, at):
            own = own_held[band_rows(band), :]
            asked = lax.broadcasted_iota(jnp.int32, (tokens, tokens), 0)
            key = lax.broadcasted_iota(jnp.int32, (tokens, tokens), 1)
            seen = (asked % SAMPLES == key % SAMPLES) & (key // SAMPLES <= asked // SAMPLES)
            bias = jnp.where(seen, 0.0, masked_low)
            bias = jnp.broadcast_to(bias[None], (heads, tokens, tokens)).reshape(rows, tokens)
            new = score(own) + bias
            count = key_block.shape[0]
            old = score(key_block) + in_range(at, count, low)
            now = jnp.maximum(
                jnp.max(new, axis=1, keepdims=True), jnp.max(old, axis=1, keepdims=True)
            )
            new = weigh(new, now)
            old = weigh(old, now)
            top[...] = jnp.broadcast_to(now, (rows, LANES))
            lane = lax.broadcasted_iota(jnp.int32, (rows, LANES), 1)
            summed = jnp.where(lane == 0, jnp.sum(new, axis=1, keepdims=True), 0.0)
            for c in range(0, count, LANES):
                summed = summed + old[:, c : c + LANES]
            total[...] = summed
            acc[...] = mix(new, own) + mix(old, key_block)

        def fold(key_block, low_spot, at):
            count = key_block.shape[0]
            s = score(key_block)
            if low_spot is not None:
                s = s + in_range(at, count, low_spot)
            before = top[...]
            now = jnp.maximum(before, jnp.max(s, axis=1, keepdims=True))
            shrink = jnp.exp2((before - now) * exponent_scale)
            expo = weigh(s, over_lanes(now, count))
            top[...] = now
            summed = total[...] * shrink
            for c in range(0, count, LANES):
                summed = summed + expo[:, c : c + LANES]
            total[...] = summed
            acc[...] = acc[...] * over_lanes(shrink, kv_rank) + mix(expo, key_block)

        @pl.loop(0, chunks)
        def _(i):
            slot = jnp.where(i == 0, lax.rem(band, 2), 2 + lax.rem(i, 2))
            fetch(i).wait()

            @pl.when(i + 1 < chunks)
            def _():
                fetch(i + 1).start()

            nominal = first + i * KEY_BLOCK
            at = chunk_at(first, i)
            whole = (i > 0) & (nominal + KEY_BLOCK <= last)
            skip = (nominal - at) // EDGE_BLOCK

            @pl.when(i == 0)
            def _():
                here = pl.multiple_of(skip * EDGE_BLOCK, EDGE_BLOCK)
                begin(held[slot, pl.ds(here, EDGE_BLOCK), :], at + here)

            @pl.when(whole)
            def _():
                fold(held[slot], None, None)

            @pl.when(jnp.logical_not(whole))
            def _():
                begun = skip + jnp.where(i == 0, 1, 0)

                @pl.loop(begun, (jnp.minimum(last - at, KEY_BLOCK) + EDGE_BLOCK - 1) // EDGE_BLOCK)
                def _(j):
                    here = pl.multiple_of(j * EDGE_BLOCK, EDGE_BLOCK)
                    fold(held[slot, pl.ds(here, EDGE_BLOCK), :], nominal, at + here)

        norm = 1.0 / jnp.sum(total[...], axis=1, keepdims=True)
        lat[:, band_rows(band), :] = (
            (acc[...] * norm).astype(jnp.bfloat16).reshape(heads, tokens, kv_rank)
        )

        @pl.when(band == bands - 1)
        def _():
            load_up().wait()

            @pl.loop(0, heads // 8)
            def _(eight):
                picked = [eight * 8 + k for k in range(8)]
                products = [
                    jnp.dot(lat[head], up[head], preferred_element_type=jnp.float32)
                    for head in picked
                ]
                for head, product in zip(picked, products):
                    ready[head] = product.astype(jnp.bfloat16)

            turned[...] = jnp.swapaxes(ready[...], 0, 1)
            done = pltpu.make_async_copy(turned, out_ref, up_sems.at[1])
            done.start()
            done.wait()


def shards(query_nope, query_rope, latent, up_key, value_up_weight, lengths, owner_request_table):
    seq_count = lax.axis_size("seq")
    tok_dev, head_dev, nope_dim = query_nope.shape[1:]
    rope_dim = query_rope.shape[2] // head_dev
    kv_rank = up_key.shape[1]
    width = kv_rank + rope_dim
    v_dim = value_up_weight.shape[2]
    req_dev = owner_request_table.shape[0] // seq_count
    groups = owner_request_table.shape[0] // lengths.shape[0]
    band_tokens = tok_dev // req_dev
    exponent_scale = math.log2(math.e) / math.sqrt(nope_dim + rope_dim)

    keys, pair, queries, prefill_out = prefill_part(
        latent[0],
        query_nope[0],
        query_rope[0],
        up_key,
        value_up_weight,
        lengths[None, :],
        seq_count,
        exponent_scale,
    )
    rows = head_dev * band_tokens
    attended = pl.pallas_call(
        functools.partial(decode_kernel, kv_rank, groups, exponent_scale),
        out_shape=jax.ShapeDtypeStruct(prefill_out.shape, jnp.bfloat16),
        grid_spec=pltpu.PrefetchScalarGridSpec(
            num_scalar_prefetch=2,
            grid=(req_dev,),
            in_specs=[
                pl.BlockSpec(memory_space=pl.ANY),
                pl.BlockSpec(memory_space=pl.ANY),
                pl.BlockSpec(memory_space=pl.ANY),
                pl.BlockSpec(memory_space=pl.ANY),
                pl.BlockSpec(memory_space=pl.ANY),
            ],
            out_specs=pl.BlockSpec(memory_space=pl.ANY),
            scratch_shapes=[
                pltpu.VMEM((rows, kv_rank), jnp.float32),
                pltpu.VMEM((rows, LANES), jnp.float32),
                pltpu.VMEM((rows, LANES), jnp.float32),
                pltpu.VMEM((4, KEY_BLOCK, width), jnp.bfloat16),
                pltpu.VMEM((head_dev, tok_dev, kv_rank), jnp.bfloat16),
                pltpu.VMEM(value_up_weight.shape, jnp.bfloat16),
                pltpu.VMEM((head_dev, tok_dev, v_dim), jnp.bfloat16),
                pltpu.VMEM(prefill_out.shape, jnp.bfloat16),
                pltpu.VMEM((2, head_dev, band_tokens, width), jnp.bfloat16),
                pltpu.VMEM((tok_dev, width), jnp.bfloat16),
                pltpu.SemaphoreType.DMA((4,)),
                pltpu.SemaphoreType.DMA((2,)),
                pltpu.SemaphoreType.DMA((3,)),
            ],
        ),
        compiler_params=pltpu.CompilerParams(vmem_limit_bytes=58 << 20),
    )(
        lengths,
        owner_request_table,
        queries,
        keys.reshape(-1, width),
        pair.reshape(-1, width),
        value_up_weight,
        prefill_out,
    )

    return attended[None]


def solution(mesh):
    in_specs = (
        P("section", "seq", "head", None),
        P("section", "seq", "head"),
        P("section", ("seq", "head"), None),
        P("head", None, None),
        P("head", None, None),
        P(),
        P(),
    )
    out_specs = P("section", "seq", "head", None)
    return jax.shard_map(shards, mesh=mesh, in_specs=in_specs, out_specs=out_specs, check_vma=False)
```

```python
import functools
import math

import jax
import jax.numpy as jnp
from jax import lax
from jax.experimental import pallas as pl
from jax.experimental.pallas import tpu as pltpu
from jax.sharding import PartitionSpec as P

SAMPLES = 8
STEPS = 4
BLOCK = 64

scale_top = 448.0
tiny_eps = 1e-06
masked_low = -1e30

KEY_BLOCK = 1024
EDGE_BLOCK = 512
FAR_HEADS = 6

CHAIN_STEPS = (0, 1, 3, 5)
ON_STEPS = (0, 2, 5, 8)
END_STEPS = (1, 3, 7, 10)
SIBLING_STEPS = (2, 5, 9, 13)
PAST_STEPS = (8, 10, 15)
LANES = 128


def prefill_kernel(
    z_count, y_count, kv_rank, exponent_scale, own_in, q_nope, q_rope, up_key, value_up, lengths,
    keys, own_out, q_out, out, block, raw, nope, up, q, far_nope, far_rope, far_q, acc, top, total,
    held, bias, ready, far_send, far_recv,
    in_sems, out_sems, held_sems, x_send, x_recv, own_sems,
    z_send, z_recv, y_send, y_recv, sib_send, sib_recv,
):
    section = lax.axis_index("section")
    seq = lax.axis_index("seq")
    core = lax.axis_index("head")
    z = seq // (2 * y_count)
    y = seq // 2 % y_count
    hi = seq % 2
    half = z_count // 2
    heads, tokens, width = q.shape
    plane_blocks = 2 * y_count
    at_block = seq % plane_blocks
    plane_keys = plane_blocks * tokens
    nt = (((1,), (1,)), ((), ()))

    def plane_at(dz):
        return lax.rem(z + dz + z_count, z_count)

    def row_at(dy):
        return lax.rem(y + dy + y_count, y_count)

    def device(dz=0, dy=0, to_hi=None, to_section=None, to_core=None):
        th = hi if to_hi is None else to_hi
        return (
            section if to_section is None else to_section,
            (plane_at(dz) * y_count + row_at(dy)) * 2 + th,
            core if to_core is None else to_core,
        )

    loads = [
        pltpu.make_async_copy(q_nope, raw, in_sems.at[0]),
        pltpu.make_async_copy(up_key, up, in_sems.at[1]),
    ]
    for load in loads:
        load.start()

    barrier = pltpu.get_barrier_semaphore()
    peers = [
        device(to_core=1 - core),
        device(to_section=1 - section),
        device(to_hi=1 - hi),
        device(to_section=1 - section, to_hi=1 - hi),
        device(dz=1),
        device(dz=-1),
        device(dy=1),
        device(dy=-1),
    ]
    for peer in peers:
        pl.semaphore_signal(barrier, inc=1, device_id=peer, device_id_type=pl.DeviceIdType.MESH)

    @pl.when(section == 0)
    def _():
        rows = own_in[...].astype(jnp.float32)
        largest = jnp.max(jnp.abs(rows))
        spread = jnp.full((8, LANES), largest, jnp.float32)
        scale = ((spread + tiny_eps) / scale_top).astype(jnp.bfloat16).astype(jnp.float32)
        factor = scale[:1, :1]
        stored = (rows / factor).astype(jnp.bfloat16)
        block[...] = (stored.astype(jnp.float32) * factor).astype(jnp.bfloat16)

    @pl.when(section == 1)
    def _():
        block[...] = own_in[...]

    pl.semaphore_wait(barrier, len(peers))

    def remote(src, dst, to, send_sem, recv_sem):
        return pltpu.make_async_remote_copy(
            src_ref=src,
            dst_ref=dst,
            send_sem=send_sem,
            recv_sem=recv_sem,
            device_id=to,
            device_id_type=pl.DeviceIdType.MESH,
        )

    def arrive(dst, recv_sem):
        remote(dst, dst, device(to_core=1 - core), recv_sem, recv_sem).wait_recv()

    def own_local():
        return pltpu.make_async_copy(block, own_out.at[core], own_sems.at[0])

    def own_away():
        to = device(to_core=1 - core)
        return remote(block, own_out.at[core], to, own_sems.at[1], own_sems.at[2])

    def x_copies():
        spot = keys.at[z, y, hi, core]
        return [
            remote(block, spot, device(to_hi=1 - hi), x_send.at[2], x_recv.at[1]),
            remote(block, spot, device(to_section=1), x_send.at[0], x_recv.at[0]),
            remote(block, spot, device(to_section=1, to_hi=1 - hi), x_send.at[1], x_recv.at[1]),
        ]

    def x_local():
        return pltpu.make_async_copy(block, keys.at[z, y, hi, core], x_send.at[3])

    @pl.when(section == 0)
    def _():
        x_local().start()
        for copy in x_copies():
            copy.start()

    own_local().start()
    own_away().start()

    for load in loads:
        load.wait()
    nope[...] = jnp.swapaxes(raw[...], 0, 1)

    near = heads - FAR_HEADS
    half_lanes = LANES // 2

    def far_copies():
        to = device(to_section=1 - section)
        rope_part = q_rope.at[:, pl.ds(near * half_lanes, FAR_HEADS * half_lanes)]
        return [
            remote(nope.at[pl.ds(near, FAR_HEADS)], far_nope, to, far_send.at[0], far_recv.at[0]),
            remote(rope_part, far_rope, to, far_send.at[1], far_recv.at[1]),
        ]

    def far_result():
        part = ready.at[pl.ds(near, FAR_HEADS)]
        return remote(part, part, device(to_section=1 - section), far_send.at[2], far_recv.at[2])

    @pl.when(section == 0)
    def _():
        for copy in far_copies():
            copy.start()

    def absorb(from_nope, from_rope, into, first, count):
        @pl.loop(0, count // 2)
        def _(pair):
            rope = from_rope[:, pl.ds(pl.multiple_of(pair * LANES, LANES), LANES)]
            for side in range(2):
                head = pair * 2 + side
                lifted = lax.dot_general(
                    from_nope[head], up[first + head], nt, preferred_element_type=jnp.float32
                )
                into[head, :, :kv_rank] = lifted.astype(jnp.bfloat16)
                into[head, :, kv_rank:] = rope[:, side * half_lanes : (side + 1) * half_lanes]

    @pl.when(section == 0)
    def _():
        absorb(nope, q_rope, q, 0, near)

    @pl.when(section == 1)
    def _():
        absorb(nope, q_rope, q, 0, heads)

    def load_value_up():
        return pltpu.make_async_copy(value_up, up, in_sems.at[1])

    @pl.when(section == 0)
    def _():
        load_value_up().start()

    @pl.when(section == 1)
    def _():
        pltpu.make_async_copy(q, q_out, out_sems.at[0]).start()

    @pl.when(section == 0)
    def _():
        x_local().wait()
        arrive(keys.at[z, y, 1 - hi, core], x_recv.at[1])

    @pl.when(section == 1)
    def _():
        arrive(keys.at[z, y, hi, core], x_recv.at[0])
        arrive(keys.at[z, y, 1 - hi, core], x_recv.at[1])

    low, high, far = row_at(-1), row_at(1), row_at(2)
    columns = [y, low, high, far]
    planes = [z]
    for s in range(1, half):
        planes += [plane_at(-s), plane_at(s)]
    planes.append(plane_at(half))
    steps = [[0]] + [[2 * s - 1, 2 * s] for s in range(1, half)] + [[z_count - 1]]

    def sender(went):
        def send(src, to, send_sem, recv_sem):
            copy = lambda: remote(src(), src(), to(), send_sem(), recv_sem())
            went.append(copy)
            copy().start()

        return send

    went = [[], [], []]

    def along_y(send, n, c, src, d, k):
        send(src, lambda: device(dy=d), lambda: y_send.at[n, k], lambda: y_recv.at[n, k])

    def spread(send, n, c):
        mine = lambda: keys.at[planes[n], y, :, c]
        along_y(send, n, c, mine, 1, 0)
        along_y(send, n, c, mine, -1, 1)

    def spread_on(send, n, c):
        arrive(keys.at[planes[n], low, :, c], y_recv.at[n, 0])
        along_y(send, n, c, lambda: keys.at[planes[n], low, 0, c], 1, 2)
        arrive(keys.at[planes[n], high, :, c], y_recv.at[n, 1])
        along_y(send, n, c, lambda: keys.at[planes[n], high, 1, c], -1, 3)

    def spread_end(n, c):
        arrive(keys.at[planes[n], far, 0, c], y_recv.at[n, 2])
        arrive(keys.at[planes[n], far, 1, c], y_recv.at[n, 3])

    def to_sibling(send, n, c):
        send(
            lambda: keys.at[planes[n], :, :, c],
            lambda: device(to_core=1 - c),
            lambda: sib_send.at[n],
            lambda: sib_recv.at[n],
        )

    def along_z(send, src, up_way, step, k):
        d, j = (1, 0) if up_way else (-1, 1)
        send(
            src,
            lambda: device(dz=d),
            lambda: z_send.at[j, step, k],
            lambda: z_recv.at[j, step, k],
        )

    ways = ((0, True), (1, False))

    def decode_a(stage):
        send = sender(went[1])

        def cell(n, k):
            return lambda: keys.at[planes[n], columns[k], :, 0]

        def column(k):
            for _, up_way in ways:
                along_z(send, cell(0, k), up_way, 0, k)

        if stage == 0:
            spread(send, 0, 0)
            column(0)
            arrive(keys.at[z, low, :, 0], y_recv.at[0, 0])
            along_y(send, 0, 0, lambda: keys.at[z, low, 0, 0], 1, 2)
            column(1)
            arrive(keys.at[z, high, :, 0], y_recv.at[0, 1])
            along_y(send, 0, 0, lambda: keys.at[z, high, 1, 0], -1, 3)
            column(2)
            spread_end(0, 0)
            column(3)
            to_sibling(send, 0, 0)
        elif stage < half:
            for k in range(y_count):
                for n, (j, up_way) in zip(steps[stage], ways):
                    arrive(cell(n, k)(), z_recv.at[j, stage - 1, k])
                    if stage < half - 1 or k // 2 == j:
                        along_z(send, cell(n, k), up_way, stage, k)
            for n in steps[stage]:
                to_sibling(send, n, 0)
        else:
            for k in range(y_count):
                arrive(cell(z_count - 1, k)(), z_recv.at[k // 2, half - 1, k])
            to_sibling(send, z_count - 1, 0)

    def decode_b(stage):
        send = sender(went[2])

        def ahead(n, s, j, up_way):
            if s < half - 1:
                part = lambda: keys.at[planes[n], y, :, 1]
            else:
                part = lambda: keys.at[planes[n], y, j, 1]
            along_z(send, part, up_way, s, 0)

        def chain(s):
            for n, (j, up_way) in zip(steps[s], ways):
                arrive(keys.at[planes[n], y, :, 1], z_recv.at[j, s - 1, 0])
                ahead(n, s, j, up_way)
                spread(send, n, 1)

        def finish(s):
            for n in steps[s]:
                spread_end(n, 1)
                to_sibling(send, n, 1)

        if stage == 0:
            for j, up_way in ways:
                ahead(0, 0, j, up_way)
            spread(send, 0, 1)
            chain(1)
            spread_on(send, 0, 1)
            return
        if stage + 1 < half:
            chain(stage + 1)
        elif stage + 1 == half:
            for j in range(2):
                arrive(keys.at[planes[-1], y, j, 1], z_recv.at[j, half - 1, 0])
            spread(send, z_count - 1, 1)
        for n in steps[stage]:
            spread_on(send, n, 1)
        finish(stage - 1)
        if stage == half:
            finish(stage)

    behind = [0] + [2 * s - 1 for s in range(1, half)] + [z_count - 1]
    past = planes[2 * (half - 1)]
    forward = sender(went[0])

    def ahead(n, s):
        along_z(forward, lambda: keys.at[planes[n], y, :, core], True, s, 0)

    def prefill_start():
        ahead(0, 0)
        spread(forward, 0, core)
        prefill_chain(1)
        spread_on(forward, 0, core)
        spread_end(0, core)
        to_sibling(forward, 0, core)
        prefill_on(1)
        from_sibling(0)

    def prefill_chain(s):
        n = behind[s]
        arrive(keys.at[planes[n], y, :, core], z_recv.at[0, s - 1, 0])
        if s < half:
            ahead(n, s)
        else:
            along_z(forward, lambda: keys.at[planes[n], y, 1, core], True, 0, 1)
        spread(forward, n, core)

    def prefill_on(s):
        spread_on(forward, behind[s], core)

    def prefill_end(s):
        spread_end(behind[s], core)
        to_sibling(forward, behind[s], core)

    def prefill_past():
        arrive(keys.at[past, y, 1, core], z_recv.at[0, 0, 1])
        n = 2 * (half - 1)
        along_y(forward, n, core, lambda: keys.at[past, y, 1, core], 1, 0)

    def prefill_past_end():
        n = 2 * (half - 1)
        spot = lambda: keys.at[past, low, 1, core]
        arrive(spot(), y_recv.at[n, 0])
        forward(
            spot,
            lambda: device(to_core=1 - core),
            lambda: sib_send.at[n],
            lambda: sib_recv.at[n],
        )

    def from_sibling(n):
        arrive(keys.at[planes[n], :, :, 1 - core], sib_recv.at[n])

    def on(at, event):
        @pl.when(at)
        def _():
            event()

    top[...] = jnp.full(top.shape, masked_low, jnp.float32)
    total[...] = jnp.zeros(total.shape, jnp.float32)
    acc[...] = jnp.zeros(acc.shape, jnp.float32)

    token = lax.broadcasted_iota(jnp.int32, (tokens, 1), 0)
    position = seq * tokens + token
    count = lengths.shape[1]
    before_it = lax.broadcasted_iota(jnp.int32, (count, count), 0) < lax.broadcasted_iota(
        jnp.int32, (count, count), 1
    )
    earlier = jnp.where(before_it, 1.0, 0.0).astype(jnp.bfloat16)
    wide = jnp.broadcast_to(lengths[...], (8, count))
    digits = [(wide // 64).astype(jnp.bfloat16), (wide % 64).astype(jnp.bfloat16)]
    upper, lower = [jnp.dot(d, earlier, preferred_element_type=jnp.float32) for d in digits]
    starts = (upper * 64.0 + lower)[:1]
    row_low = jnp.max(
        jnp.where(starts <= position.astype(jnp.float32), starts, 0.0), axis=1, keepdims=True
    ).astype(jnp.int32)

    chunk = plane_keys // 2
    tile_heads = near // 2

    def fold(asked_heads, tile, key_block):
        count = key_block.shape[0]
        tile_heads = asked_heads.shape[0]
        rows = tile_heads * tokens
        part = pl.ds(pl.multiple_of(tile * rows, rows), rows)
        asked = asked_heads[...].reshape(rows, width)
        s = lax.dot_general(asked, key_block, nt, preferred_element_type=jnp.float32)
        s = (s.reshape(tile_heads, tokens, count) + bias[:, :count][None]).reshape(rows, count)
        before = top[part, :]
        now = jnp.maximum(before, jnp.max(s, axis=1, keepdims=True))
        shrink = jnp.exp2((before - now) * exponent_scale)
        expo = jnp.exp2((s - over_lanes(now, count)) * exponent_scale)
        top[part, :] = now
        summed = total[part, :] * shrink
        for c in range(0, count, LANES):
            summed = summed + expo[:, c : c + LANES]
        total[part, :] = summed
        acc[part, :] = acc[part, :] * over_lanes(shrink, kv_rank) + jnp.dot(
            expo.astype(jnp.bfloat16),
            key_block[:, :kv_rank],
            preferred_element_type=jnp.float32,
        )

    def past_from_sibling():
        arrive(keys.at[past, low, 1, 1 - core], sib_recv.at[2 * (half - 1)])

    last_step = 4 * (half + 1)
    timetable = [
        (prefill_chain, CHAIN_STEPS),
        (prefill_on, ON_STEPS),
        (prefill_end, END_STEPS),
        (lambda s: from_sibling(behind[s]), SIBLING_STEPS),
    ]
    events = {0: [prefill_start]}
    for s in range(1, half + 1):
        for event, at_steps in timetable:
            if at_steps[s - 1] > 0:
                spot = events.setdefault(at_steps[s - 1], [])
                spot.append(functools.partial(event, s))
    for event, at_step in zip((prefill_past, prefill_past_end, past_from_sibling), PAST_STEPS):
        events.setdefault(at_step, []).append(event)

    @pl.when(section == 0)
    def _():
        mid = plane_blocks // 2
        at_first, at_mid = at_block == 0, at_block == mid
        reaches_past = at_first & (z > half)

        @pl.loop(0, last_step)
        def _(step):
            for at_step in sorted(events):
                for event in events[at_step]:
                    on(step == at_step, event)

            run = step // 2
            turn = step % 2
            rest = run == 2 * half + 1
            back = jnp.where(rest, 0, (run + 1) // 2)
            side = jnp.where(run == 0, 0, (run + 1) % 2)
            side = jnp.where(rest, 1, side)
            slot = jnp.where(rest, 1, back % 2)
            reached = z >= back

            def load(back, part, slot, into):
                plane = lax.rem(z - back + z_count, z_count)
                here = keys.at[plane, pl.ds(part * (y_count // 2), y_count // 2)]
                return pltpu.make_async_copy(here, held.at[slot, into], held_sems.at[slot, into])

            def load_first():
                return pltpu.make_async_copy(
                    keys.at[past, y_count - 1, 1], held.at[1, 0, 0, 0], held_sems.at[1, 0]
                )

            def load_mid():
                return pltpu.make_async_copy(
                    keys.at[planes[-1], y_count // 2 - 1, 1],
                    held.at[1, 1, y_count // 2 - 1, 1],
                    held_sems.at[1, 0],
                )

            @pl.when(step == 0)
            def _():
                load(0, 0, 0, 0).start()

            for s in range(1, half + 1):

                @pl.when((step == SIBLING_STEPS[s - 1]) & (z >= s))
                def _():
                    load(s, 0, s % 2, 0).start()
                    load(s, 1, s % 2, 1).start()

            @pl.when(step == last_step - 5)
            def _():
                @pl.when(reaches_past)
                def _():
                    load_first().start()

                @pl.when(at_block >= mid)
                def _():
                    rest_load = load(0, 1, 1, 1)
                    rest_load.start()
                    rest_load.wait()

                @pl.when(at_mid)
                def _():
                    load_mid().start()

            @pl.when(reached & (turn == 0) & jnp.logical_not(rest))
            def _():
                load(back, side, slot, side).wait()

            at_past = reaches_past & (run == 2 * half)

            @pl.when(at_past & (turn == 0))
            def _():
                load_first().wait()

            @pl.when((turn == 0) & rest & at_mid)
            def _():
                load_mid().wait()

            none = (rest & (at_block < mid)) | ((run == 2 * half - 1) & (at_block >= mid))
            first_spot = (z - back) * plane_keys + side * chunk

            @pl.when(reached & jnp.logical_not(none))
            def _():
                @pl.when(turn == 0)
                def _():
                    lane = lax.broadcasted_iota(jnp.int32, (1, chunk + tokens), 1)
                    spot = first_spot + lane
                    shift = (half * plane_keys) + chunk
                    spot = jnp.where(
                        rest & at_mid & (lane >= chunk - tokens), spot - shift, spot
                    )
                    spot = jnp.where(lane >= chunk, spot - plane_keys - tokens, spot)
                    seen = (spot >= row_low) & (spot <= position)
                    bias[...] = jnp.where(seen, 0.0, masked_low)

                here = held.at[slot, side]
                tile_q = q.at[pl.ds(turn * tile_heads, tile_heads)]

                @pl.when(at_past)
                def _():
                    behind_it = held[1, 0, 0, 0].reshape(tokens, width)
                    key_block = jnp.concatenate([here[...].reshape(chunk, width), behind_it])

                    fold(tile_q, turn, key_block)

                @pl.when(jnp.logical_not(at_past))
                def _():
                    fold(tile_q, turn, here[...].reshape(chunk, width))

    def far_run(run):
        rest, beyond = run == 2 * half + 1, run == 2 * half + 2
        back = jnp.where(rest, 0, jnp.where(beyond, half + 1, (run + 1) // 2))
        side = jnp.where(run == 0, 0, jnp.where(rest | beyond, 1, (run + 1) % 2))
        slot = run % 2
        middle = plane_blocks // 2
        wanted = z >= back
        wanted = wanted & jnp.logical_not(rest & (at_block < middle))
        wanted = wanted & jnp.logical_not((run == 2 * half - 1) & (at_block > middle))
        wanted = wanted & jnp.logical_not(beyond & (at_block > 0))
        plane = lax.rem(z - back + z_count, z_count)
        load = pltpu.make_async_copy(
            keys.at[plane, pl.ds(side * (y_count // 2), y_count // 2)],
            held.at[slot, 0],
            held_sems.at[slot, 0],
        )
        return wanted, load, (z - back) * plane_keys + side * chunk, slot

    def start_far(run):
        wanted, load, _, _ = far_run(run)

        @pl.when(wanted)
        def _():
            load.start()

    def far_runs(begin, end):
        start_far(jnp.int32(begin))

        @pl.loop(begin, end)
        def _(run):
            @pl.when(run + 1 < end)
            def _():
                start_far(run + 1)

            wanted, load, first_spot, slot = far_run(run)

            @pl.when(wanted)
            def _():
                load.wait()
                spot = first_spot + lax.broadcasted_iota(jnp.int32, (1, chunk), 1)
                seen = (spot >= row_low) & (spot <= position)
                bias[:, :chunk] = jnp.where(seen, 0.0, masked_low)
                fold(far_q, 0, held[slot, 0].reshape(chunk, width))

    def project(head, part):
        norm = 1.0 / jnp.sum(total[part, :], axis=1, keepdims=True)
        mixed = (acc[part, :] * norm).astype(jnp.bfloat16)
        ready[head] = jnp.dot(mixed, up[head], preferred_element_type=jnp.float32).astype(
            jnp.bfloat16
        )

    @pl.when(section == 1)
    def _():
        for stage in range(half + 1):
            on(core == 0, functools.partial(decode_a, stage))
            on(core == 1, functools.partial(decode_b, stage))
            if stage == 1:
                arrive(far_nope, far_recv.at[0])
                arrive(far_rope, far_recv.at[1])
                absorb(far_nope, far_rope, far_q, near, FAR_HEADS)
                load_value_up().start()
            if 0 < stage < half:
                for n in steps[stage - 1]:
                    from_sibling(n)
                far_runs(max(2 * stage - 3, 0), 2 * stage - 1)
        for n in steps[half - 1] + steps[half]:
            from_sibling(n)
        far_runs(2 * half - 3, 2 * half + 3)
        load_value_up().wait()

        for head in range(FAR_HEADS):
            project(near + head, pl.ds(head * tokens, tokens))

        far_result().start()

    @pl.when(section == 0)
    def _():
        load_value_up().wait()

        @pl.loop(0, 2)
        def _(part):
            for place in range(near // 2):
                head = part * (near // 2) + place
                project(head, pl.ds(pl.multiple_of(head * tokens, tokens), tokens))

        middle = heads // 2

        def leave(part):
            some = pl.ds(part * middle, middle)
            return pltpu.make_async_copy(
                raw.at[:, some, :], out.at[:, some, :], out_sems.at[part]
            )

        raw[:, :middle, :] = jnp.swapaxes(ready[:middle], 0, 1)
        leave(0).start()
        arrive(ready.at[pl.ds(near, FAR_HEADS)], far_recv.at[2])
        raw[:, middle:, :] = jnp.swapaxes(ready[middle:], 0, 1)
        leave(1).start()
        leave(0).wait()
        leave(1).wait()
        for copy in x_copies() + far_copies():
            copy.wait_send()

    @pl.when(section == 1)
    def _():
        pltpu.make_async_copy(q, q_out, out_sems.at[0]).wait()
        far_result().wait_send()

    groups = [section == 0, (section == 1) & (core == 0), (section == 1) & (core == 1)]
    for group, copies in zip(groups, went):

        @pl.when(group)
        def _():
            for copy in copies:
                copy().wait_send()

    arrive(own_out.at[1 - core], own_sems.at[2])
    own_away().wait_send()
    own_local().wait()


def prefill_part(own, q_nope, q_rope, up_key, value_up, lengths, seq_count, exponent_scale):
    rows, width = own.shape
    tokens, heads, nope_dim = q_nope.shape
    kv_rank = up_key.shape[1]
    y_count = 4
    z_count = seq_count // (2 * y_count)
    dma = pltpu.SemaphoreType.DMA
    bf16 = own.dtype
    chunk = y_count * tokens
    vmem = pl.BlockSpec(memory_space=pltpu.VMEM)
    hbm = pl.BlockSpec(memory_space=pl.ANY)
    return pl.pallas_call(
        functools.partial(prefill_kernel, z_count, y_count, kv_rank, exponent_scale),
        out_shape=[
            jax.ShapeDtypeStruct((z_count, y_count, 2, 2, rows, width), bf16),
            jax.ShapeDtypeStruct((2, rows, width), bf16),
            jax.ShapeDtypeStruct((heads, tokens, width), bf16),
            jax.ShapeDtypeStruct((tokens, heads, value_up.shape[2]), bf16),
        ],
        in_specs=[vmem, hbm, vmem, hbm, hbm, vmem],
        out_specs=[hbm] * 4,
        scratch_shapes=[
            pltpu.VMEM((rows, width), bf16),
            pltpu.VMEM(q_nope.shape, bf16),
            pltpu.VMEM((heads, tokens, nope_dim), bf16),
            pltpu.VMEM(up_key.shape, bf16),
            pltpu.VMEM((heads, tokens, width), bf16),
            pltpu.VMEM((FAR_HEADS, tokens, nope_dim), bf16),
            pltpu.VMEM((tokens, FAR_HEADS * (width - kv_rank)), bf16),
            pltpu.VMEM((FAR_HEADS, tokens, width), bf16),
            pltpu.VMEM(((heads - FAR_HEADS) * tokens, kv_rank), jnp.float32),
            pltpu.VMEM(((heads - FAR_HEADS) * tokens, LANES), jnp.float32),
            pltpu.VMEM(((heads - FAR_HEADS) * tokens, LANES), jnp.float32),
            pltpu.VMEM((2, 2, y_count // 2, 2, 2, rows, width), bf16),
            pltpu.VMEM((tokens, chunk + tokens), jnp.float32),
            pltpu.VMEM((heads, tokens, value_up.shape[2]), bf16),
            dma((3,)),
            dma((3,)),
            dma((2,)),
            dma((2,)),
            dma((2, 2)),
            dma((4,)),
            dma((2,)),
            dma((3,)),
            dma((2, z_count // 2, y_count)),
            dma((2, z_count // 2, y_count)),
            dma((z_count, 4)),
            dma((z_count, 4)),
            dma((z_count,)),
            dma((z_count,)),
        ],
        compiler_params=pltpu.CompilerParams(
            collective_id=0, has_side_effects=True, vmem_limit_bytes=56 << 20
        ),
    )(own, q_nope, q_rope, up_key, value_up, lengths)


def over_lanes(value, width):
    return jnp.concatenate([value] * (width // LANES), axis=1)


def decode_kernel(
    kv_rank,
    groups,
    exponent_scale,
    lengths,
    table,
    q_ref,
    keys,
    own_keys,
    value_up,
    prefill_out,
    out_ref,
    acc,
    top,
    total,
    held,
    lat,
    up,
    ready,
    turned,
    q_held,
    own_held,
    sems,
    q_sems,
    up_sems,
):
    band = pl.program_id(0)
    bands = pl.num_programs(0)
    _, heads, tokens, width = q_held.shape
    rows = heads * tokens
    all_keys = keys.shape[0]
    nt = (((1,), (1,)), ((), ()))

    @pl.when(lax.axis_index("section") == 0)
    def _():
        some = [pl.ds(part * (turned.shape[0] // 2), turned.shape[0] // 2) for part in range(2)]
        taken = [
            pltpu.make_async_copy(prefill_out.at[part], turned.at[part], sem)
            for part, sem in zip(some, (up_sems.at[0], up_sems.at[2]))
        ]
        handed = [
            pltpu.make_async_copy(turned.at[part], out_ref.at[part], sem)
            for part, sem in zip(some, (up_sems.at[1], q_sems.at[0]))
        ]

        @pl.when(band == 0)
        def _():
            for copy in taken:
                copy.start()
            for came, goes in zip(taken, handed):
                came.wait()
                goes.start()

        @pl.when(band == bands - 1)
        def _():
            for copy in handed:
                copy.wait()

    @pl.when(lax.axis_index("section") == 1)
    def _():
        def prompt_range(which):
            prompt = table[lax.axis_index("seq") * bands + which] // groups
            low = lax.fori_loop(0, prompt, lambda k, at: at + lengths[k], jnp.int32(0))
            return low, low + lengths[prompt]

        def chunk_at(start, i):
            return pl.multiple_of(jnp.minimum(start + i * KEY_BLOCK, all_keys - KEY_BLOCK), 16)

        def fetch_from(start, i, slot):
            return pltpu.make_async_copy(
                keys.at[pl.ds(chunk_at(start, i), KEY_BLOCK), :], held.at[slot], sems.at[slot]
            )

        def band_rows(which):
            return pl.ds(pl.multiple_of(which * tokens, tokens), tokens)

        def fetch_q(which):
            slot = lax.rem(which, 2)
            return pltpu.make_async_copy(
                q_ref.at[:, band_rows(which), :], q_held.at[slot], q_sems.at[slot]
            )

        def load_up():
            return pltpu.make_async_copy(value_up, up, up_sems.at[0])

        def load_own():
            return pltpu.make_async_copy(own_keys, own_held, up_sems.at[2])

        low, last = prompt_range(band)
        first = low // 16 * 16
        chunks = (last - first + KEY_BLOCK - 1) // KEY_BLOCK

        def fetch(i):
            slot = jnp.where(i == 0, lax.rem(band, 2), 2 + lax.rem(i, 2))
            return fetch_from(first, i, slot)

        @pl.when(band == 0)
        def _():
            load_own().start()
            fetch_q(0).start()
            fetch(0).start()
            load_up().start()
            load_own().wait()

        @pl.when(band + 1 < bands)
        def _():
            fetch_q(band + 1).start()
            next_low, _ = prompt_range(band + 1)
            fetch_from(next_low // 16 * 16, 0, lax.rem(band + 1, 2)).start()

        fetch_q(band).wait()
        q = q_held[lax.rem(band, 2)].reshape(rows, width)
        def score(key_block):
            return lax.dot_general(q, key_block, nt, preferred_element_type=jnp.float32)

        def in_range(at, count, low_spot):
            spot = at + lax.broadcasted_iota(jnp.int32, (1, count), 1)
            return jnp.where((spot >= jnp.maximum(low, low_spot)) & (spot < last), 0.0, masked_low)

        def weigh(scores, now):
            return jnp.exp2((scores - now) * exponent_scale)

        def mix(weights, key_block):
            return jnp.dot(
                weights.astype(jnp.bfloat16),
                key_block[:, :kv_rank],
                preferred_element_type=jnp.float32,
            )

        def begin(key_block, at):
            own = own_held[band_rows(band), :]
            asked = lax.broadcasted_iota(jnp.int32, (tokens, tokens), 0)
            key = lax.broadcasted_iota(jnp.int32, (tokens, tokens), 1)
            seen = (asked % SAMPLES == key % SAMPLES) & (key // SAMPLES <= asked // SAMPLES)
            bias = jnp.where(seen, 0.0, masked_low)
            bias = jnp.broadcast_to(bias[None], (heads, tokens, tokens)).reshape(rows, tokens)
            new = score(own) + bias
            count = key_block.shape[0]
            old = score(key_block) + in_range(at, count, low)
            now = jnp.maximum(
                jnp.max(new, axis=1, keepdims=True), jnp.max(old, axis=1, keepdims=True)
            )
            new = weigh(new, now)
            old = weigh(old, now)
            top[...] = jnp.broadcast_to(now, (rows, LANES))
            lane = lax.broadcasted_iota(jnp.int32, (rows, LANES), 1)
            summed = jnp.where(lane == 0, jnp.sum(new, axis=1, keepdims=True), 0.0)
            for c in range(0, count, LANES):
                summed = summed + old[:, c : c + LANES]
            total[...] = summed
            acc[...] = mix(new, own) + mix(old, key_block)

        def fold(key_block, low_spot, at):
            count = key_block.shape[0]
            s = score(key_block)
            if low_spot is not None:
                s = s + in_range(at, count, low_spot)
            before = top[...]
            now = jnp.maximum(before, jnp.max(s, axis=1, keepdims=True))
            shrink = jnp.exp2((before - now) * exponent_scale)
            expo = weigh(s, over_lanes(now, count))
            top[...] = now
            summed = total[...] * shrink
            for c in range(0, count, LANES):
                summed = summed + expo[:, c : c + LANES]
            total[...] = summed
            acc[...] = acc[...] * over_lanes(shrink, kv_rank) + mix(expo, key_block)

        @pl.loop(0, chunks)
        def _(i):
            slot = jnp.where(i == 0, lax.rem(band, 2), 2 + lax.rem(i, 2))
            fetch(i).wait()

            @pl.when(i + 1 < chunks)
            def _():
                fetch(i + 1).start()

            nominal = first + i * KEY_BLOCK
            at = chunk_at(first, i)
            whole = (i > 0) & (nominal + KEY_BLOCK <= last)
            skip = (nominal - at) // EDGE_BLOCK

            @pl.when(i == 0)
            def _():
                here = pl.multiple_of(skip * EDGE_BLOCK, EDGE_BLOCK)
                begin(held[slot, pl.ds(here, EDGE_BLOCK), :], at + here)

            @pl.when(whole)
            def _():
                fold(held[slot], None, None)

            @pl.when(jnp.logical_not(whole))
            def _():
                begun = skip + jnp.where(i == 0, 1, 0)

                @pl.loop(begun, (jnp.minimum(last - at, KEY_BLOCK) + EDGE_BLOCK - 1) // EDGE_BLOCK)
                def _(j):
                    here = pl.multiple_of(j * EDGE_BLOCK, EDGE_BLOCK)
                    fold(held[slot, pl.ds(here, EDGE_BLOCK), :], nominal, at + here)

        norm = 1.0 / jnp.sum(total[...], axis=1, keepdims=True)
        lat[:, band_rows(band), :] = (
            (acc[...] * norm).astype(jnp.bfloat16).reshape(heads, tokens, kv_rank)
        )

        @pl.when(band == bands - 1)
        def _():
            load_up().wait()

            @pl.loop(0, heads // 8)
            def _(eight):
                picked = [eight * 8 + k for k in range(8)]
                products = [
                    jnp.dot(lat[head], up[head], preferred_element_type=jnp.float32)
                    for head in picked
                ]
                for head, product in zip(picked, products):
                    ready[head] = product.astype(jnp.bfloat16)

            turned[...] = jnp.swapaxes(ready[...], 0, 1)
            done = pltpu.make_async_copy(turned, out_ref, up_sems.at[1])
            done.start()
            done.wait()


def shards(query_nope, query_rope, latent, up_key, value_up_weight, lengths, owner_request_table):
    seq_count = lax.axis_size("seq")
    tok_dev, head_dev, nope_dim = query_nope.shape[1:]
    rope_dim = query_rope.shape[2] // head_dev
    kv_rank = up_key.shape[1]
    width = kv_rank + rope_dim
    v_dim = value_up_weight.shape[2]
    req_dev = owner_request_table.shape[0] // seq_count
    groups = owner_request_table.shape[0] // lengths.shape[0]
    band_tokens = tok_dev // req_dev
    exponent_scale = math.log2(math.e) / math.sqrt(nope_dim + rope_dim)

    keys, pair, queries, prefill_out = prefill_part(
        latent[0],
        query_nope[0],
        query_rope[0],
        up_key,
        value_up_weight,
        lengths[None, :],
        seq_count,
        exponent_scale,
    )
    rows = head_dev * band_tokens
    attended = pl.pallas_call(
        functools.partial(decode_kernel, kv_rank, groups, exponent_scale),
        out_shape=jax.ShapeDtypeStruct(prefill_out.shape, jnp.bfloat16),
        grid_spec=pltpu.PrefetchScalarGridSpec(
            num_scalar_prefetch=2,
            grid=(req_dev,),
            in_specs=[
                pl.BlockSpec(memory_space=pl.ANY),
                pl.BlockSpec(memory_space=pl.ANY),
                pl.BlockSpec(memory_space=pl.ANY),
                pl.BlockSpec(memory_space=pl.ANY),
                pl.BlockSpec(memory_space=pl.ANY),
            ],
            out_specs=pl.BlockSpec(memory_space=pl.ANY),
            scratch_shapes=[
                pltpu.VMEM((rows, kv_rank), jnp.float32),
                pltpu.VMEM((rows, LANES), jnp.float32),
                pltpu.VMEM((rows, LANES), jnp.float32),
                pltpu.VMEM((4, KEY_BLOCK, width), jnp.bfloat16),
                pltpu.VMEM((head_dev, tok_dev, kv_rank), jnp.bfloat16),
                pltpu.VMEM(value_up_weight.shape, jnp.bfloat16),
                pltpu.VMEM((head_dev, tok_dev, v_dim), jnp.bfloat16),
                pltpu.VMEM(prefill_out.shape, jnp.bfloat16),
                pltpu.VMEM((2, head_dev, band_tokens, width), jnp.bfloat16),
                pltpu.VMEM((tok_dev, width), jnp.bfloat16),
                pltpu.SemaphoreType.DMA((4,)),
                pltpu.SemaphoreType.DMA((2,)),
                pltpu.SemaphoreType.DMA((3,)),
            ],
        ),
        compiler_params=pltpu.CompilerParams(vmem_limit_bytes=58 << 20),
    )(
        lengths,
        owner_request_table,
        queries,
        keys.reshape(-1, width),
        pair.reshape(-1, width),
        value_up_weight,
        prefill_out,
    )

    return attended[None]


def solution(mesh):
    in_specs = (
        P("section", "seq", "head", None),
        P("section", "seq", "head"),
        P("section", ("seq", "head"), None),
        P("head", None, None),
        P("head", None, None),
        P(),
        P(),
    )
    out_specs = P("section", "seq", "head", None)
    return jax.shard_map(shards, mesh=mesh, in_specs=in_specs, out_specs=out_specs, check_vma=False)
```
